32 devices in a mesh: dp: 8 (over z, y), tp: 4 (over x, core).
Axes of the slice: x: 2, y: 2, z: 4, core: 2. Of those that a mesh axis runs over, the one named last changes fastest.
Arguments:
- layer_input: bfloat16 [8192, 768], P('dp'), may hold values from -6 to 6
- cotangent: bfloat16 [8192, 768], P(('dp', 'tp')), may hold values from -6 to 6
- seq_lens: int32 [32], replicated, may hold values from 0 to 512, as said below
- seq_place: int32 [32], replicated, may hold values from 0 to 31, as said below
- loss_mask: int32 [8192], P(('dp', 'tp')), may hold values 0 or 1
- w_qkv: bfloat16 [768, 3, 768], P(None, None, 'tp'), may hold values from -0.21875 to 0.21875
- b_qv: bfloat16 [2, 768], P(None, 'tp'), may hold values from -3 to 3
- w_out: bfloat16 [768, 768], P('tp'), may hold values from -1.25 to 1.25
- b_out: bfloat16 [768], replicated, may hold values from -2 to 2
- ln1_gain: bfloat16 [768], replicated, may hold values from 0.5 to 1.5
- ln1_bias: bfloat16 [768], replicated, may hold values from -2 to 2
- w_in: bfloat16 [768, 3072], P(None, 'tp'), may hold values from -0.21875 to 0.21875
- b_in: bfloat16 [3072], P('tp'), may hold values from -2 to 2
- w_back: bfloat16 [3072, 768], P('tp'), may hold values from -0.15625 to 0.15625
- b_back: bfloat16 [768], replicated, may hold values from -2 to 2
- ln2_gain: bfloat16 [768], replicated, may hold values from 0.5 to 1.5
- ln2_bias: bfloat16 [768], replicated, may hold values from -2 to 2
- ad_down: bfloat16 [768, 16, 48], replicated, may hold values from -0.21875 to 0.21875
- ad_down_bias: bfloat16 [16, 48], replicated, may hold values from -3 to 3
- ad_up: bfloat16 [16, 48, 768], replicated, may hold values from -1.25 to 1.25
- ad_up_bias: bfloat16 [16, 768], replicated, may hold values from -2 to 2
- join_query: bfloat16 [768, 768], replicated, may hold values from -0.21875 to 0.21875
- join_key: bfloat16 [768, 768], replicated, may hold values from -0.4375 to 0.4375
- join_value: bfloat16 [768, 768], replicated, may hold values from -0.21875 to 0.21875
- join_gain: bfloat16 [768], replicated, may hold values from 0.5 to 1.5
- join_bias: bfloat16 [768], replicated, may hold values from -2 to 2
Outputs:
- layer_out: float32 [8192, 768], P(('dp', 'tp'))
- input_grad: float32 [8192, 768], P(('dp', 'tp'))
- grad_query: float32 [768, 768], replicated
- grad_key: float32 [768, 768], replicated
- grad_value: float32 [768, 768], replicated
- grad_gain: float32 [768], replicated
- grad_bias: float32 [768], replicated
The draws below stay inside these ranges and needn't reach their ends.
Inputs may be any that keep to these rules, and one draw needn't show every extreme that they name: `seq_lens`: lengths of the sequences; those of one data index sum to at most 1024, and some data index is filled exactly. A length may be zero. A permutation: sequence s belongs to data index seq_place[s] // 4, at place seq_place[s] % 4 among its sequences.
All inputs are finite; a program needn't handle non-finite values. No bound on the sum of `loss_mask` on one device may be relied on, other than what follows from the above.
Results may differ from the reference program's by a relative error of at most 0.03.
Values may be sent and summed in bfloat16 or wider, within the bound.
No kernel may reach another device: no remote copies, remote signals or barrier semaphores. Data moves between devices by JAX's collectives and lax.ppermute only.
A program may use at most 128 MiB of HBM per device.

```python
import jax
import jax.numpy as jnp
from jax import lax

D = 768
HEAD_DIM = 64
FF = 3072
ADAPTERS = 16
BOTTLENECK = 48
MAXLEN = 512
TOK_GRP = 1024
SEQ_GRP = 4
NSEQ = 32
TOKENS = 8192


def lay_out(key):
    groups = NSEQ // SEQ_GRP
    pair_count = SEQ_GRP // 2
    group_no = jnp.arange(groups, dtype=jnp.int32)
    capacity = MAXLEN - 2 * MAXLEN // 3 * (groups - 1 - group_no) // max(groups - 1, 1)
    cut_points = jax.random.randint(jax.random.fold_in(key, 11), (groups, pair_count), 0, MAXLEN + 1)
    first_len = cut_points * capacity[:, None] // MAXLEN
    pair_no = jnp.arange(pair_count, dtype=jnp.int32)
    forced = (group_no[:, None] == groups - 1) & (pair_no[None, :] == 0)
    first_len = jnp.where(forced, 0, first_len)
    second_len = capacity[:, None] - first_len
    by_place = jnp.stack([first_len, second_len], axis=-1).reshape(groups * SEQ_GRP).astype(jnp.int32)
    placement = jax.random.permutation(jax.random.fold_in(key, 12), groups * SEQ_GRP).astype(jnp.int32)
    return (placement, by_place)


def draw_seq_lens(key, part):
    placement, by_place = lay_out(key)
    return by_place[placement].astype(jnp.int32)


def draw_seq_place(key, part):
    placement, by_place = lay_out(key)
    return placement


def touch_ends(entries, rng, least, largest):
    longest = entries.shape.index(max(entries.shape))
    spots = []
    for shift in (0, 1):
        where = [jax.random.randint(jax.random.fold_in(rng, axis), (), 0, length) for axis, length in enumerate(entries.shape)]
        where[longest] = (where[longest] + shift) % entries.shape[longest]
        spots.append(tuple(where))
    return entries.at[spots[0]].set(least).at[spots[1]].set(largest)


def block_levels(own_key, shape, cuts, low, largest):
    gain = 1.0
    for dim, blocks in cuts:
        draws = jax.random.uniform(jax.random.fold_in(jax.random.fold_in(own_key, 6), dim), (blocks,), jnp.float32, low / len(cuts), largest / len(cuts))
        gain = gain * jnp.repeat(jnp.exp(draws), shape[dim] // blocks).reshape((-1,) + (1,) * (len(shape) - 1 - dim))
    return gain


def centred(stream_key, dims, width, most, cuts=(), kind=jnp.bfloat16):
    loudness = block_levels(stream_key, dims, cuts, -0.22, 0.18) if cuts else 1.0
    entries = jax.random.normal(stream_key, dims, jnp.float32) * width * loudness
    return jnp.minimum(jnp.maximum(entries, -most), most).astype(kind)


def setup_inputs(seed: int = 0) -> dict:
    splits = jax.random.split(jax.random.key(seed), 27)
    return {
        "layer_input": centred(splits[0], (TOKENS, D), 1.0, 6.0, ((0, 8),)),
        "cotangent": centred(splits[1], (TOKENS, D), 1.0, 6.0, ((0, 32),)),
        "seq_lens": draw_seq_lens(jax.random.fold_in(splits[26], 71), 0),
        "seq_place": draw_seq_place(jax.random.fold_in(splits[26], 71), 0),
        "loss_mask": touch_ends((jax.random.randint(splits[4], (TOKENS,), 0, 4) < 3).astype(jnp.int32), jax.random.fold_in(splits[4], 1), 0, 1),
        "w_qkv": centred(splits[5], (D, 3, D), D ** -0.5, 0.21875, ((2, 4),)),
        "b_qv": centred(splits[6], (2, D), 0.5, 3.0, ((1, 4),)),
        "w_out": centred(splits[7], (D, D), (D // 32) ** -0.5, 1.25, ((0, 4),)),
        "b_out": centred(splits[8], (D,), 0.3, 2.0),
        "ln1_gain": jnp.clip(1.0 + 0.1 * jax.random.normal(splits[9], (D,), jnp.float32), 0.5, 1.5).astype(jnp.bfloat16),
        "ln1_bias": centred(splits[10], (D,), 0.3, 2.0),
        "w_in": centred(splits[11], (D, FF), D ** -0.5, 0.21875, ((1, 4),)),
        "b_in": centred(splits[12], (FF,), 0.3, 2.0, ((0, 4),)),
        "w_back": centred(splits[13], (FF, D), (FF // 2) ** -0.5, 0.15625, ((0, 4),)),
        "b_back": centred(splits[14], (D,), 0.3, 2.0),
        "ln2_gain": jnp.clip(1.0 + 0.1 * jax.random.normal(splits[15], (D,), jnp.float32), 0.5, 1.5).astype(jnp.bfloat16),
        "ln2_bias": centred(splits[16], (D,), 0.3, 2.0),
        "ad_down": centred(splits[17], (D, ADAPTERS, BOTTLENECK), D ** -0.5, 0.21875),
        "ad_down_bias": centred(splits[18], (ADAPTERS, BOTTLENECK), 0.5, 3.0),
        "ad_up": centred(splits[19], (ADAPTERS, BOTTLENECK, D), (BOTTLENECK // 2) ** -0.5, 1.25),
        "ad_up_bias": centred(splits[20], (ADAPTERS, D), 0.3, 2.0),
        "join_query": centred(splits[21], (D, D), D ** -0.5, 0.21875),
        "join_key": centred(splits[22], (D, D), (D // 4) ** -0.5, 0.4375),
        "join_value": centred(splits[23], (D, D), D ** -0.5, 0.21875),
        "join_gain": jnp.clip(1.0 + 0.1 * jax.random.normal(splits[24], (D,), jnp.float32), 0.5, 1.5).astype(jnp.bfloat16),
        "join_bias": centred(splits[25], (D,), 0.3, 2.0),
    }


@jax.custom_vjp
def low(v):
    return lax.optimization_barrier(v.astype(jnp.bfloat16)).astype(jnp.float32)

@jax.custom_vjp
def low_back(v):
    return v

def low_keep(v):
    return (low(v), None)

def low_pass(kept, grad):
    return (grad,)

def back_keep(v):
    return (v, None)

def back_low(kept, grad):
    return (low(grad),)
low.defvjp(low_keep, low_pass)
low_back.defvjp(back_keep, back_low)
EPS = 1e-06
NEG = -1e+30
HIGH = lax.Precision.HIGHEST

def layer_norm(values, gain_vec, offset):
    center = values - lax.optimization_barrier(jnp.mean(values, axis=-1, keepdims=True))
    factor = lax.rsqrt(lax.optimization_barrier(jnp.mean(center * center, axis=-1, keepdims=True)) + EPS)
    return center * factor * gain_vec + offset

def gelu_exact(values):
    return jax.nn.gelu(values, approximate=False)

def group_layer(hidden_in, join_query, join_key, join_value, join_gain, join_bias, seg_ids, frozen):
    w_qkv, b_qv, w_out, b_out, ln1_gain, ln1_bias, w_in, b_in, w_back, b_back, ln2_gain, ln2_bias, ad_down, ad_down_bias, ad_up, ad_up_bias = frozen
    group_rows = hidden_in.shape[0]
    heads = w_qkv.shape[2] // HEAD_DIM
    projected = jnp.einsum('td,dch->cth', hidden_in, w_qkv, precision=HIGH)
    query_heads = low(low_back(projected[0] + b_qv[0])).reshape(group_rows, heads, HEAD_DIM)
    key_heads = low(low_back(projected[1])).reshape(group_rows, heads, HEAD_DIM)
    value_heads = low(low_back(projected[2] + b_qv[1])).reshape(group_rows, heads, HEAD_DIM)
    block_rows = min(512, group_rows)
    head_scale = HEAD_DIM ** (-0.5)

    def attend(pieces):
        query_rows, seg_rows = pieces
        scores = low_back(jnp.einsum('qhe,khe->hqk', query_rows, key_heads, precision=HIGH) * head_scale)
        allowed = seg_rows[:, None] == seg_ids[None, :]
        scores = jnp.where(allowed[None], scores, NEG)
        weights = low(jax.nn.softmax(scores, axis=-1))
        return jnp.einsum('hqk,khe->qhe', weights, value_heads, precision=HIGH)
    context = lax.map(jax.checkpoint(attend), (query_heads.reshape(group_rows // block_rows, block_rows, heads, HEAD_DIM), seg_ids.reshape(group_rows // block_rows, block_rows)))
    context = low(low_back(context.reshape(group_rows, heads * HEAD_DIM)))
    attn_out = low_back(jnp.dot(context, w_out, precision=HIGH))
    first = layer_norm(attn_out + b_out + hidden_in, ln1_gain, ln1_bias)
    inner_ffn = low_back(jnp.dot(low(first), w_in, precision=HIGH) + b_in)
    ffn_out = low_back(jnp.dot(low(gelu_exact(inner_ffn)), w_back, precision=HIGH))
    second = layer_norm(first + ffn_out + b_back, ln2_gain, ln2_bias)
    second_low = low(second)
    model_width = second.shape[1]
    reduced = low_back(jnp.dot(second_low, ad_down.reshape(model_width, ADAPTERS * BOTTLENECK), precision=HIGH) + ad_down_bias.reshape(ADAPTERS * BOTTLENECK))
    squeezed = low(gelu_exact(reduced)).reshape(group_rows, ADAPTERS, BOTTLENECK)
    lifted = low_back(jnp.einsum('sar,ard->asd', squeezed, ad_up, precision=HIGH))
    adapted = low(second[None] + lifted + ad_up_bias[:, None, :])
    query_f = low(low_back(jnp.dot(second_low, join_query, precision=HIGH)))
    key_f = low(low_back(jnp.einsum('asd,de->ase', adapted, join_key, precision=HIGH)))
    value_f = low(low_back(jnp.einsum('asd,de->ase', adapted, join_value, precision=HIGH)))
    logits = jnp.einsum('sd,asd->sa', query_f, key_f, precision=HIGH) * model_width ** (-0.5)
    log_probs = jax.nn.log_softmax(logits, axis=-1)
    joining_probs = jnp.exp(log_probs)
    joined_value = jnp.einsum('sa,asd->sd', joining_probs, value_f, precision=HIGH)
    layer_out = layer_norm(second + joined_value, join_gain, join_bias)
    entropy = -lax.optimization_barrier(jnp.sum(joining_probs * log_probs, axis=-1))
    return (layer_out, entropy)

def reference(layer_input, cotangent, seq_lens, seq_place, loss_mask, w_qkv, b_qv, w_out, b_out, ln1_gain, ln1_bias, w_in, b_in, w_back, b_back, ln2_gain, ln2_bias, ad_down, ad_down_bias, ad_up, ad_up_bias, join_query, join_key, join_value, join_gain, join_bias):
    groups = seq_place.shape[0] // SEQ_GRP
    wanted = jnp.arange(groups * SEQ_GRP, dtype=jnp.int32)
    matches = (seq_place[None, :] == wanted[:, None]).astype(jnp.int32)
    group_lens = lax.optimization_barrier(jnp.sum(matches * seq_lens[None, :], axis=1)).reshape(groups, SEQ_GRP)
    seq_ends = jnp.cumsum(group_lens, axis=1)
    positions = jnp.arange(TOK_GRP, dtype=jnp.int32)
    segment = lax.optimization_barrier(jnp.sum((positions[None, :, None] >= seq_ends[:, None, :]).astype(jnp.int32), axis=2))
    is_real = positions[None, :] < seq_ends[:, SEQ_GRP - 1:]
    seg_ids = jnp.where(is_real, segment, SEQ_GRP + positions[None, :]).astype(jnp.int32)
    weight_m = loss_mask.reshape(groups, TOK_GRP).astype(jnp.float32) * is_real.astype(jnp.float32)
    counted = jnp.sum(weight_m)
    ent_scale = 0.5 * TOKENS / jnp.maximum(counted, 1.0)
    frozen = tuple((tensor.astype(jnp.float32) for tensor in (w_qkv, b_qv, w_out, b_out, ln1_gain, ln1_bias, w_in, b_in, w_back, b_back, ln2_gain, ln2_bias, ad_down, ad_down_bias, ad_up, ad_up_bias)))
    trained = tuple((tensor.astype(jnp.float32) for tensor in (join_query, join_key, join_value, join_gain, join_bias)))
    inputs = layer_input.astype(jnp.float32).reshape(groups, TOK_GRP, -1)
    cot_groups = cotangent.astype(jnp.float32).reshape(groups, TOK_GRP, -1)

    def one_group(totals, pieces):
        hidden_in, cot_rows, seg_rows, weight_rows = pieces

        def forward(hidden_in, fq_arg, fk_arg, fv_arg, fg_arg, fb_arg):
            layer_out, entropy = group_layer(hidden_in, fq_arg, fk_arg, fv_arg, fg_arg, fb_arg, seg_rows, frozen)
            return (layer_out, jnp.sum(weight_rows * entropy))
        (layer_out, ent_sum), pullback = jax.vjp(forward, hidden_in, *trained)
        gradients = pullback((cot_rows, ent_scale.astype(ent_sum.dtype)))
        new_totals = tuple((running + addend for running, addend in zip(totals, gradients[1:])))
        return (new_totals, (layer_out, gradients[0]))
    zero_grads = tuple((jnp.zeros_like(tensor) for tensor in trained))
    totals, (all_outs, input_grads) = lax.scan(one_group, zero_grads, (inputs, cot_groups, seg_ids, weight_m))
    model_width = all_outs.shape[2]
    return (all_outs.reshape(TOKENS, model_width), input_grads.reshape(TOKENS, model_width), totals[0], totals[1], totals[2], totals[3], totals[4])
```

```python
import functools

import jax
import jax.numpy as jnp
from jax import lax
from jax.experimental import pallas as pl
from jax.experimental.pallas import tpu as pltpu
from jax.sharding import PartitionSpec as P

HEAD_DIM = 64
ADAPTERS = 16
BOTTLENECK = 48
SEQ_GRP = 4
LEAST_ROWS = 96
FLOPS = 1.15e9

EPS = 1e-06
NEG = -1e30
ROOT_HALF = 0.7071067811865476
INV_ROOT_TAU = 0.3989422804014327

f32 = jnp.float32
bf16 = jnp.bfloat16
i32 = jnp.int32

HEADER = 64

ORDER = (0, 2, 1, 3)


def gelu_both(values):
    phi = 0.5 * (1.0 + lax.erf(values * ROOT_HALF))
    return values * phi, phi + values * jnp.exp(-0.5 * values * values) * INV_ROOT_TAU


def row_mean(values):
    return jnp.sum(values, axis=-1, keepdims=True) * (1.0 / values.shape[-1])


def norm_parts(values):
    center = values - row_mean(values)
    factor = lax.rsqrt(row_mean(center * center) + EPS)
    return center * factor, factor


def norm_back(gradient, normed, factor, gain_vec):
    scaled = gradient * gain_vec
    return factor * (scaled - row_mean(scaled) - normed * row_mean(scaled * normed))


def mm(a, b):
    return lax.dot_general(a, b, (((1,), (0,)), ((), ())), preferred_element_type=f32)


def mm_nt(a, b):
    return lax.dot_general(a, b, (((1,), (1,)), ((), ())), preferred_element_type=f32)


def mm_tn(a, b):
    return lax.dot_general(a, b, (((0,), (0,)), ((), ())), preferred_element_type=f32)


def halves_of(a):
    high = a.astype(bf16)
    return high, (a - high.astype(f32)).astype(bf16)


def split_dot(a, b):
    high, low = halves_of(a)
    return mm(high, b) + mm(low, b)


def swap(value, axis, bit):
    size = lax.axis_size(axis)
    return lax.ppermute(value, axis, [(i, i ^ bit) for i in range(size)])


def tie(*values):
    return lax.optimization_barrier(values)


def run(kernel, scalars, inputs, outputs, streamed=(), scratch=(), vmem=12, micros=0.1):
    smem = pl.BlockSpec(memory_space=pltpu.SMEM)
    vmem_spec = pl.BlockSpec(memory_space=pltpu.VMEM)
    any_spec = pl.BlockSpec(memory_space=pl.ANY)
    outs = pl.pallas_call(
        kernel,
        in_specs=[smem] * len(scalars) + [vmem_spec] * len(inputs) + [any_spec] * len(streamed),
        out_specs=[vmem_spec if len(o) == 2 else any_spec for o in outputs],
        out_shape=[pltpu.VMEM(*o) if len(o) == 2 else jax.ShapeDtypeStruct(*o[:2]) for o in outputs],
        scratch_shapes=list(scratch),
        compiler_params=pltpu.CompilerParams(vmem_limit_bytes=vmem * 1024 * 1024),
        cost_estimate=pl.CostEstimate(flops=int(micros * FLOPS), bytes_accessed=1, transcendentals=0),
    )(
        *scalars,
        *[pltpu.with_memory_space_constraint(a, pltpu.VMEM) for a in inputs],
        *[pltpu.with_memory_space_constraint(a, pltpu.HBM) for a in streamed],
    )
    return list(outs)


def head_mask(width, head):
    lane = lax.broadcasted_iota(i32, (1, width), 1)
    return (lane >= head * HEAD_DIM) & (lane < (head + 1) * HEAD_DIM)


def group_ends(ints):
    count = (ints.shape[0] - HEADER) // 2

    def add(s, ends):
        spot = ints[HEADER + count + s] - ints[1] * SEQ_GRP
        length = jnp.where(spot >= 0, ints[HEADER + s], 0)
        return tuple(e + jnp.where(spot <= j, length, 0) for j, e in enumerate(ends))

    return lax.fori_loop(0, count, add, (jnp.int32(0),) * SEQ_GRP)


def segment_of(positions, ends):
    segment = jnp.zeros(positions.shape, i32)
    for e in ends:
        segment = segment + (positions >= e).astype(i32)
    return jnp.where(positions < ends[-1], segment, SEQ_GRP + positions)


def window(rows, start, ends, group_rows):
    low = jnp.int32(0)
    high = jnp.int32(0)
    last = start + rows - 1
    for e in ends:
        low = jnp.where(start >= e, jnp.maximum(low, e), low)
    for e in reversed(ends):
        high = jnp.where(last < e, e, high)
    padded = last >= ends[-1]
    low = jnp.where(start >= ends[-1], start, low)
    high = jnp.where(padded, start + rows, high)
    low = jnp.minimum(low // 128 * 128, group_rows - 128)
    return low, high - low


def by_window(rows, start, ends, group_rows, act):
    low, span = window(rows, start, ends, group_rows)
    widths = [w for w in (512, 768) if w < group_rows] + [group_rows]
    least = 0
    for w in widths:
        fits = (span > least) & (span <= w) if w < group_rows else span > least

        @pl.when(fits)
        def _(w=w):
            act(pl.multiple_of(jnp.minimum(low, group_rows - w), 128), w)

        least = w


def one_row(tile):
    return jnp.concatenate([tile[j : j + 1, :] for j in range(tile.shape[0])], axis=1)


def project_kernel(ids, x_hbm, w_hbm, bias_hbm, mask_hbm, *refs):
    vectors, refs = refs[:9], refs[9:]
    q_ref, k_ref, v_ref, message, weight, vecs, x_ref, w_ref, bias_ref, mask_ref, *tiles, sems = refs
    group_rows, width = q_ref.shape
    share = weight.shape[0]
    chunks = group_rows // share
    pairs = [(w_hbm, w_ref)]
    for c in range(chunks):
        rows = pl.ds(c * share, share)
        pairs.append((x_hbm.at[rows, :], x_ref.at[rows, :]))
    pairs += [(bias_hbm, bias_ref), (mask_hbm, mask_ref), *zip(vectors, tiles)]
    copies = [pltpu.make_async_copy(source, target, sems.at[j]) for j, (source, target) in enumerate(pairs)]
    for copy in copies:
        copy.start()
    bias_at = chunks + 1
    copies[0].wait()
    copies[bias_at].wait()
    bias = bias_ref[...].astype(f32)
    for c in range(chunks):
        rows = slice(c * share, (c + 1) * share)
        copies[1 + c].wait()
        x = x_ref[rows, :]
        k_ref[rows, :] = mm_nt(x, w_ref[width : 2 * width, :]).astype(bf16)
        v_ref[rows, :] = (mm_nt(x, w_ref[2 * width :, :]) + bias[1:2]).astype(bf16)
        q = (mm_nt(x, w_ref[:width, :]) + bias[0:1]).astype(bf16)
        q_ref[rows, :] = (q.astype(f32) * HEAD_DIM ** (-0.5)).astype(bf16)

    for copy in copies[bias_at + 1 :]:
        copy.wait()
    for j, tile in enumerate(tiles):
        vecs[j : j + 1, :] = one_row(tile[...].astype(f32))
    vecs[9:, :] = jnp.zeros((vecs.shape[0] - 9, vecs.shape[1]), f32)
    ends = group_ends(ids)
    lane = lax.broadcasted_iota(i32, (1, share), 1)
    row = jnp.where(ids[0] * share + lane < ends[-1], one_row(mask_ref[...].astype(f32)), 0.0)
    total = jnp.sum(row, axis=-1, keepdims=True)
    message[0:1, :] = vecs[8:9, :]
    message[1:, :] = jnp.broadcast_to(total, (message.shape[0] - 1, message.shape[1]))
    here = lax.broadcasted_iota(i32, (share, share), 0) == lax.broadcasted_iota(i32, (share, share), 1)
    weight[...] = jnp.sum(jnp.where(here, jnp.broadcast_to(row, (share, share)), 0.0), axis=-1, keepdims=True)


def project(ids, x, w_t, b_qv, mask, vectors, share):
    group_rows, model = x.shape
    width = w_t.shape[0] // 3
    streamed = [x, w_t, b_qv, mask.reshape(-1, 128), *[v.reshape(-1, 128) for v in vectors]]
    return run(
        project_kernel,
        (ids,),
        [],
        [((group_rows, width), bf16)] * 3 + [((8, model), f32), ((share, 1), f32), ((16, model), f32)],
        streamed=streamed,
        scratch=[pltpu.VMEM(a.shape, a.dtype) for a in streamed]
        + [pltpu.SemaphoreType.DMA((group_rows // share + len(streamed),))],
        micros=3.0,
    )


def attend_kernel(first, ids, q_ref, k_ref, v_ref, context_ref, e_ref, rl_ref):
    rows = context_ref.shape[0] // 2
    group_rows, width = k_ref.shape
    heads = width // HEAD_DIM
    ends = group_ends(ids)

    def one(t, carry):
        start = pl.multiple_of(ids[2 + first + t] * rows, rows)
        at = pl.multiple_of(t * rows, rows)

        def act(key0, w):
            q = q_ref[pl.ds(start, rows), :].astype(f32)
            seg_q = segment_of(start + lax.broadcasted_iota(i32, (rows, 1), 0), ends)
            seg_k = segment_of(key0 + lax.broadcasted_iota(i32, (1, w), 1), ends)
            k = k_ref[pl.ds(key0, w), :]
            v = v_ref[pl.ds(key0, w), :]
            context = jnp.zeros((rows, width), f32)
            wide = jnp.zeros((rows, width), f32)
            for h in range(heads):
                mask = head_mask(width, h)
                scores = mm_nt(jnp.where(mask, q, 0.0).astype(bf16), k)
                scores = jnp.where(seg_q == seg_k, scores, NEG)
                e = jnp.exp(scores - jnp.max(scores, axis=-1, keepdims=True))
                inverse = 1.0 / jnp.sum(e, axis=-1, keepdims=True)
                low = e.astype(bf16)
                e_ref[pl.ds(pl.multiple_of((t * heads + h) * rows, rows), rows), :w] = low
                context = jnp.where(mask, mm(low, v) * inverse, context)
                wide = jnp.where(mask, inverse, wide)
            rl_ref[pl.ds(at, rows), :] = wide
            context_ref[pl.ds(at, rows), :] = context.astype(bf16)

        by_window(rows, start, ends, group_rows, act)
        return carry

    lax.fori_loop(0, 2, one, 0)


def attend(first, ids, q, k, v, share):
    group_rows, width = k.shape
    heads = width // HEAD_DIM
    return run(
        functools.partial(attend_kernel, first),
        (ids,),
        [q, k, v],
        [
            ((2 * share, width), bf16),
            ((2 * heads * share, group_rows), bf16),
            ((2 * share, width), f32),
        ],
        vmem=20,
        micros=3.0,
    )


def attend_back_kernel(spots, first, last, ids, *refs):
    count = len(spots)
    grads, refs = refs[:count], refs[count:]
    contexts, es, rls, refs = refs[0:2], refs[2:4], refs[4:6], refs[6:]
    q_ref, k_ref, v_ref, refs = refs[0], refs[1], refs[2], refs[3:]
    if not first:
        before, refs = refs[:3], refs[3:]
    if last:
        w_ref, far_out, near_out, gq, gk, gv = refs
    else:
        gq, gk, gv = refs
    rows = grads[0].shape[0]
    group_rows, width = k_ref.shape
    heads = width // HEAD_DIM
    ends = group_ends(ids)
    if first:
        gk[...] = jnp.zeros_like(gk)
        gv[...] = jnp.zeros_like(gv)
    else:
        gq[...] = before[0][...]
        gk[...] = before[1][...]
        gv[...] = before[2][...]
    for g_ref, spot in zip(grads, spots):
        start = pl.multiple_of(ids[2 + spot] * rows, rows)
        part, t = spot // 2, spot % 2
        g = g_ref[...].astype(f32) * rls[part][t * rows : (t + 1) * rows, :]
        dots = g * contexts[part][t * rows : (t + 1) * rows, :].astype(f32)
        q = q_ref[pl.ds(start, rows), :].astype(f32)

        def act(key0, w, g=g, dots=dots, q=q, part=part, t=t, start=start):
            keys = pl.ds(key0, w)
            k = k_ref[keys, :]
            v = v_ref[keys, :]
            out = jnp.zeros((rows, width), f32)
            add_k = jnp.zeros((w, width), f32)
            add_v = jnp.zeros((w, width), f32)
            for h in range(heads):
                mask = head_mask(width, h)
                g_head = jnp.where(mask, g, 0.0).astype(bf16)
                e = es[part][(t * heads + h) * rows : (t * heads + h + 1) * rows, :w]
                delta = jnp.sum(jnp.where(mask, dots, 0.0), axis=-1, keepdims=True)
                ds = (e.astype(f32) * (mm_nt(g_head, v) - delta)).astype(bf16)
                out = jnp.where(mask, mm(ds, k), out)
                add_k = add_k + mm_tn(ds, jnp.where(mask, q, 0.0).astype(bf16))
                add_v = add_v + mm_tn(e, g_head)
            gk[keys, :] += add_k
            gv[keys, :] += add_v
            gq[pl.ds(start, rows), :] = (out * HEAD_DIM ** (-0.5)).astype(bf16)

        by_window(rows, start, ends, group_rows, act)
    if last:
        for out, pair in ((far_out, (2, 3)), (near_out, (0, 1))):
            for t, spot in enumerate(pair):
                own = pl.ds(pl.multiple_of(ids[2 + spot] * rows, rows), rows)
                part = (
                    mm(gq[own, :], w_ref[:width, :])
                    + mm(gk[own, :].astype(bf16), w_ref[width : 2 * width, :])
                    + mm(gv[own, :].astype(bf16), w_ref[2 * width :, :])
                )
                out[t * rows : (t + 1) * rows, :] = part.astype(out.dtype)


def attend_back(spots, ids, grads, contexts, es, rls, qkv, before, w_t, share):
    group_rows, width = qkv[0].shape
    last = w_t is not None
    sums = [((group_rows, width), bf16), ((group_rows, width), f32), ((group_rows, width), f32)]
    inputs = [*grads, *contexts, *es, *rls, *qkv, *before]
    if last:
        model = w_t.shape[1]
        outputs = [((2 * share, model), bf16), ((2 * share, model), f32)]
        scratch = [pltpu.VMEM(*o) for o in sums]
        inputs.append(w_t)
    else:
        outputs, scratch = sums, []
    return run(
        functools.partial(attend_back_kernel, spots, not before, last),
        (ids,),
        inputs,
        outputs,
        scratch=scratch,
        vmem=20,
        micros=4.5,
    )


def early_kernel(c0, c1, c3, o0, o1, o3, out):
    share = out.shape[0] // 2
    attn = mm(c0[...], o0[...]) + mm(c1[...], o1[...])
    for t in range(2):
        rows = slice(t * share, (t + 1) * share)
        out[rows, :] = attn[rows] + mm(c3[(1 - t) * share : (2 - t) * share, :], o3[...])


def forward_kernel(
    own, ids, early, c2, x_ref, o2, vecs, message, in0, in1, back0, back1, part_ref, slope, *rest
):
    share = part_ref.shape[0]
    t = 0 if own else 1
    attn = early[t * share : (t + 1) * share, :] + mm(c2[(1 - t) * share : (2 - t) * share, :], o2[...])
    vec = vecs[...].astype(f32)
    start = pl.multiple_of(ids[2 if own else 3] * share, share)
    normed, factor = norm_parts(attn + vec[0:1] + x_ref[pl.ds(start, share), :].astype(f32))
    first = normed * vec[1:2] + vec[2:3]
    low = first.astype(bf16)
    part = jnp.zeros(first.shape, f32)
    units = in0.shape[1]
    for j, (w_in, bias, w_back) in enumerate(((in0, vec[8:9], back0), (in1, message[0:1, :], back1))):
        act, bend = gelu_both(mm(low, w_in[...]) + bias)
        slope[:, j * units : (j + 1) * units] = bend.astype(bf16)
        part = part + mm(act.astype(bf16), w_back[...])
    part_ref[...] = part.astype(part_ref.dtype)
    if own:
        first_ref, normed_ref, factor_ref = rest
        first_ref[...] = first
        normed_ref[...] = normed
        factor_ref[...] = jnp.broadcast_to(factor, factor_ref.shape)


def forward_rows(own, ids, early, c2, x, o2, vecs, message, w_ins, w_backs, share):
    model = x.shape[1]
    units = w_ins[0].shape[1]
    outputs = [((share, model), f32 if own else bf16), ((share, 2 * units), bf16)]
    if own:
        outputs += [((share, model), f32), ((share, model), f32), ((share, 128), f32)]
    return run(
        functools.partial(forward_kernel, own),
        (ids,),
        [early, c2, x, o2, vecs, message, *w_ins, *w_backs],
        outputs,
        micros=3.0,
    )


def backward_kernel(gp, slope, back0, back1, in0, in1, part_ref):
    grad = gp[...]
    units = in0.shape[1]
    part = jnp.zeros(grad.shape, f32)
    for j, (w_back, w_in) in enumerate(((back0, in0), (back1, in1))):
        bend = slope[:, j * units : (j + 1) * units].astype(f32)
        inner = (bend * mm_nt(grad, w_back[...])).astype(bf16)
        part = part + mm_nt(inner, w_in[...])
    part_ref[...] = part.astype(part_ref.dtype)


def backward_rows(grad, slope, w_backs, w_ins, dtype):
    share, model = grad.shape
    units = w_ins[0].shape[1]
    return run(
        backward_kernel,
        (),
        [grad, slope, *w_backs, *w_ins],
        [((share, model), dtype)],
    )


def first_norm_kernel(own, got, gpre2, normed, factor, vecs, o0, o1, o2, o3, gpre1, c0, c1, c2, c3):
    grad = own[...] + got[...].astype(f32) + gpre2[...]
    grad = norm_back(grad, normed[...], factor[:, 0:1], vecs[...].astype(f32)[1:2])
    gpre1[...] = grad
    low = grad.astype(bf16)
    for c, o in ((c2, o2), (c3, o3), (c1, o1), (c0, o0)):
        c[...] = mm_nt(low, o[...]).astype(bf16)


def first_norm_back(own, got, gpre2, normed, factor, vecs, outs):
    share, model = own.shape
    width = outs[0].shape[0]
    return run(
        first_norm_kernel,
        (),
        [own, got, gpre2, normed, factor, vecs, *outs],
        [((share, model), f32)] + [((share, width), bf16)] * 4,
    )


def adapter_kernel(
    slots, ids, own, got, first_ref, cot, weight, count, vecs, down_bias, up_bias, down, up, wq, wk, wv,
    out_hbm, keep, give, sums, turn_ref, slope_ref, base_ref, normed_ref, factor_ref, layer_out, sem,
):
    flat, model = up.shape
    vec = vecs[...].astype(f32)
    lane = lax.broadcasted_iota(i32, (flat, ADAPTERS), 0) - BOTTLENECK * lax.broadcasted_iota(
        i32, (flat, ADAPTERS), 1
    )
    member = ((lane >= 0) & (lane < BOTTLENECK)).astype(f32).astype(bf16)
    lane = lax.broadcasted_iota(i32, (ADAPTERS, flat), 1) - BOTTLENECK * lax.broadcasted_iota(
        i32, (ADAPTERS, flat), 0
    )
    spread = ((lane >= 0) & (lane < BOTTLENECK)).astype(f32).astype(bf16)
    inv_root = model ** (-0.5)
    cycle = lax.broadcasted_iota(i32, (BOTTLENECK, flat), 1) - lax.broadcasted_iota(i32, (BOTTLENECK, flat), 0)
    repeat = jnp.zeros(cycle.shape, f32)
    for a in range(ADAPTERS):
        repeat = repeat + (cycle == a * BOTTLENECK).astype(f32)
    bias_wide = mm(down_bias[...], repeat.astype(bf16))
    bias_row = jnp.sum(bias_wide * spread.astype(f32), axis=0, keepdims=True)
    scale = 0.5 * slots / jnp.maximum(count[0:1, 0:1], 1.0)

    normed_two, factor_two = norm_parts(own[...] + got[...].astype(f32) + vec[3:4] + first_ref[...])
    normed_ref[...] = normed_two
    factor_ref[...] = jnp.broadcast_to(factor_two, factor_ref.shape)
    second = normed_two * vec[4:5] + vec[5:6]
    second_low = second.astype(bf16)
    reduced = mm_nt(second_low, down[...]) + bias_row
    squeezed, slope_ad = gelu_both(reduced)
    squeezed = squeezed.astype(bf16).astype(f32)
    query_f = mm(second_low, wq[...]).astype(bf16)
    query_key = mm_nt(query_f, wk[...]) * inv_root
    query_key_low = query_key.astype(bf16)
    lift_key = mm_nt(query_key_low, up[...])
    logits = (
        split_dot(squeezed * lift_key, member)
        + mm_nt(query_key_low, up_bias[...])
        + jnp.sum(query_key * second, axis=-1, keepdims=True)
    )
    shifted = logits - jnp.max(logits, axis=-1, keepdims=True)
    log_probs = shifted - jnp.log(jnp.sum(jnp.exp(shifted), axis=-1, keepdims=True))
    joining = jnp.exp(log_probs)
    entropy = -jnp.sum(joining * log_probs, axis=-1, keepdims=True)
    total = jnp.sum(joining, axis=-1, keepdims=True)
    joining_wide = split_dot(joining, spread)
    mixed = (
        total * second + mm((joining_wide * squeezed).astype(bf16), up[...]) + split_dot(joining, up_bias[...])
    )
    mixed_low = mixed.astype(bf16)
    normed_join, factor_join = norm_parts(second + mm(mixed_low, wv[...]))
    layer_out[...] = normed_join * vec[6:7] + vec[7:8]
    copy = pltpu.make_async_copy(layer_out, out_hbm, sem)
    copy.start()
    grad_out = cot[...].astype(f32)
    small = jnp.concatenate(
        [
            jnp.sum(grad_out * normed_join, axis=0, keepdims=True),
            jnp.sum(grad_out, axis=0, keepdims=True),
            jnp.zeros((sums.shape[0] - 2, model), f32),
        ],
        axis=0,
    )
    sums[...] = small
    write_small(give, small)
    grad_pref = norm_back(grad_out, normed_join, factor_join, vec[6:7])
    grad_pref_low = grad_pref.astype(bf16)
    back_value = mm_nt(grad_pref_low, wv[...])
    back_value_low = back_value.astype(bf16)
    lift_value = mm_nt(back_value_low, up[...])
    grad_probs = (
        split_dot(squeezed * lift_value, member)
        + mm_nt(back_value_low, up_bias[...])
        + jnp.sum(back_value * second, axis=-1, keepdims=True)
    )
    mean_grad = jnp.sum(joining * grad_probs, axis=-1, keepdims=True)
    grad_logits = joining * (grad_probs - mean_grad) - scale * weight[...] * joining * (log_probs + entropy)
    grad_wide = split_dot(grad_logits, spread)
    logit_sum = jnp.sum(grad_logits, axis=-1, keepdims=True)
    turned = (
        logit_sum * second + mm((grad_wide * squeezed).astype(bf16), up[...]) + split_dot(grad_logits, up_bias[...])
    ) * inv_root
    turned_low = turned.astype(bf16)
    turn_ref[...] = turned_low
    slope_ref[...] = (slope_ad * (grad_wide * lift_key + joining_wide * lift_value)).astype(bf16)
    base_ref[...] = grad_pref + logit_sum * query_key + total * back_value

    half = model // 2
    for j, (left, right) in enumerate(((second, turned_low), (mixed, grad_pref_low))):
        left_t = jnp.transpose(left).astype(bf16)
        product = mm(left_t, right).astype(bf16)
        rows = slice(j * half, (j + 1) * half)
        upper = ids[6] > 0
        keep[rows, :] = jnp.where(upper, product[half:], product[:half])
        give[rows, :] = jnp.where(upper, product[:half], product[half:])
    copy.wait()


def adapters(slots, ids, arrays):
    share, model = arrays[0].shape
    flat = arrays[10].shape[0]
    wide, low = ((share, model), f32), ((share, model), bf16)
    return run(
        functools.partial(adapter_kernel, slots),
        (ids,),
        arrays,
        [
            ((share, model), f32, None),
            ((model, model), bf16),
            ((model + 16, model), bf16),
            ((8, model), f32),
            low,
            ((share, flat), bf16),
            wide,
            wide,
            ((share, 128), f32),
        ],
        scratch=[pltpu.VMEM((share, model), f32), pltpu.SemaphoreType.DMA],
        vmem=24,
        micros=8.0,
    )


def adapter_rest_kernel(turn, slope, base, normed, factor, vecs, down, wq, wk, gpre2_ref, gpre2_low):
    grad_query_f = mm(turn[...], wk[...]).astype(bf16)
    grad_second = base[...] + mm(slope[...], down[...]) + mm_nt(grad_query_f, wq[...])
    grad_pre2 = norm_back(grad_second, normed[...], factor[:, 0:1], vecs[4:5, :])
    gpre2_ref[...] = grad_pre2
    gpre2_low[...] = grad_pre2.astype(bf16)


def write_small(message, sums):
    high, low = halves_of(sums)
    rows = message.shape[0] - 16
    message[rows:, :] = jnp.concatenate([high, low], axis=0)


def read_small(message):
    rows = message.shape[0] - 16
    both = message[rows:, :].astype(f32)
    return both[:8] + both[8:]


def fold_kernel(base, start, split, ids, *refs):
    if start:
        keep, got, sums, *outs = refs
        rows = keep.shape[0] // 2
        pieces = [(keep, got, j * rows) for j in range(2)]
    else:
        *arrays, sums = refs[:5]
        outs = refs[5:]
        rows = arrays[0].shape[0]
        pieces = [(arrays[2 * j], arrays[2 * j + 1], 0) for j in range(2)]
        got = arrays[3]
    total = sums[...] + read_small(got)
    outs[-1][...] = total
    for j, (mine, other, at) in enumerate(pieces):
        def both(where):
            return (mine[where, :].astype(f32) + other[where, :].astype(f32)).astype(bf16)

        if split:
            half = rows // 2
            bit = ids[base + j]
            outs[2 * j][...] = both(pl.ds(pl.multiple_of(at + bit * half, 16), half))
            outs[2 * j + 1][:half, :] = both(pl.ds(pl.multiple_of(at + (1 - bit) * half, 16), half))
        else:
            whole = both(pl.ds(at, rows))
            outs[2 * j][...] = whole
            outs[2 * j + 1][:rows, :] = whole
    write_small(outs[3], total)


def fold(ids, base, start, split, arrays, rows, sums):
    model = sums.shape[1]
    rows = rows // 2 if split else rows
    outputs = []
    for j in range(2):
        outputs += [((rows, model), bf16), ((rows + 16 * j, model), bf16)]
    outputs.append((sums.shape, f32))
    outs = run(functools.partial(fold_kernel, base, start, split), (ids,), [*arrays, sums], outputs)
    return outs[0:4:2], outs[1:4:2], outs[4]


def join_kernel(base, last, ids, *refs):
    outs = refs[4:]
    for j in range(2):
        mine, got = refs[2 * j : 2 * j + 2]
        rows = mine.shape[0]
        bit = ids[base + j]
        out, at = (outs[0], 2 * rows * j) if last else (outs[j], 0)
        out[pl.ds(pl.multiple_of(at + bit * rows, 16), rows), :] = mine[...]
        out[pl.ds(pl.multiple_of(at + (1 - bit) * rows, 16), rows), :] = got[...]


def join(ids, base, last, mine, gots):
    rows, model = mine[0].shape
    outputs = [((4 * rows, model), bf16)] if last else [((2 * rows, model), bf16)] * 2
    arrays = [a for pair in zip(mine, gots) for a in pair]
    return run(functools.partial(join_kernel, base, last), (ids,), arrays, outputs)


def finish_kernel(ids, mine, got, wq, wk, out_q, out_k, out_v, both, stage, sems):
    half = mine.shape[0] // 2
    outs = (out_q, out_k, out_v)
    copies = []

    def send(j, value):
        stage[j] = value
        copies.append(pltpu.make_async_copy(stage.at[j], outs[j], sems.at[j]))
        copies[-1].start()

    own = pl.ds(pl.multiple_of(ids[6] * half, half), half)
    other = pl.ds(pl.multiple_of((1 - ids[6]) * half, half), half)
    for source, rows in ((mine, own), (got, other)):
        both[0, rows, :] = source[:half, :]
        both[1, rows, :] = source[half:, :]
    send(2, both[1].astype(f32))
    send(0, mm(both[0], wk[...]))
    send(1, mm_tn(both[0], wq[...]))
    for copy in copies:
        copy.wait()


def finish(ids, mine, got, wq, wk):
    model = mine.shape[1]
    return run(
        finish_kernel,
        (ids,),
        [mine, got, wq, wk],
        [((model, model), f32, None)] * 3,
        scratch=[
            pltpu.VMEM((2, model, model), bf16),
            pltpu.VMEM((3, model, model), f32),
            pltpu.SemaphoreType.DMA((3,)),
        ],
        vmem=24,
    )


def chip_kernel(near, got, gpre1, keep, give):
    share = keep.shape[0]
    give[...] = (near[share:, :] + got[share:, :].astype(f32)).astype(bf16)
    keep[...] = near[:share, :] + got[:share, :].astype(f32) + gpre1[...]


def body(
    layer_input,
    cotangent,
    seq_lens,
    seq_place,
    loss_mask,
    w_qkv,
    b_qv,
    w_out,
    b_out,
    ln1_gain,
    ln1_bias,
    w_in,
    b_in,
    w_back,
    b_back,
    ln2_gain,
    ln2_bias,
    ad_down,
    ad_down_bias,
    ad_up,
    ad_up_bias,
    join_query,
    join_key,
    join_value,
    join_gain,
    join_bias,
):
    group_rows, model = layer_input.shape
    share = cotangent.shape[0]
    rank = lax.axis_index("tp")
    dp_rank = lax.axis_index("dp")
    total_slots = group_rows * lax.axis_size("dp")

    core, near_x = ("tp", 1), ("tp", 2)
    others = []
    bit = 1
    while bit < lax.axis_size("dp"):
        others.append(("dp", bit))
        bit *= 2
    streams = [
        [others[0], *others[1:], near_x],
        [*others[1:2], others[0], near_x, *others[2:]],
    ]

    def bit_of(axis, which):
        return (lax.axis_index(axis) // which) % 2

    ids = [rank, dp_rank] + [rank ^ j for j in ORDER] + [bit_of(*core)]
    for at in range(len(others) + 1):
        ids += [bit_of(*stream[at]) for stream in streams]
    ids = jnp.stack(ids).astype(i32)
    ids = jnp.concatenate([ids, jnp.zeros(HEADER - ids.shape[0], i32), seq_lens, seq_place])
    vectors = [b_out, ln1_gain, ln1_bias, b_back, ln2_gain, ln2_bias, join_gain, join_bias, b_in]

    outs = [w_out, swap(w_out, "tp", 1), swap(w_out, "tp", 2)]
    outs.append(None)
    w_ins = [w_in, swap(w_in, "tp", 1)]
    w_backs = [w_back, swap(w_back, "tp", 1)]

    width = w_qkv.shape[2]
    w_t = jnp.transpose(w_qkv, (1, 2, 0)).reshape(3 * width, model)
    q, k, v, message, weight_m, vecs = project(ids, layer_input, w_t, b_qv, loss_mask, vectors, share)
    message_got = swap(message, *core)
    far, e_far, rl_far = attend(2, ids, q, k, v, share)
    far, message_got, outs[1], outs[2] = tie(far, message_got, *outs[1:3])
    outs[3] = swap(outs[2], "tp", 1)
    counted = message[1:2, :128] + message_got[1:2, :128]
    got = swap(counted, *near_x)
    near, e_near, rl_near = attend(0, ids, q, k, v, share)
    near, got = tie(near, got)
    counted = counted + got
    got = swap(counted, *others[0])
    c1, c2, c3 = swap(far, "tp", 1), swap(near, "tp", 2), swap(far, "tp", 3)
    model_rows = 2 * share
    (early,) = run(early_kernel, (), [near, c1, c3, outs[0], outs[1], outs[3]], [((model_rows, model), f32)])
    early, c2 = tie(early, c2)

    give, slope_two = forward_rows(
        False, ids, early, c2, layer_input, outs[2], vecs, message_got, w_ins, w_backs, share
    )
    give, got = tie(give, got)
    ffn_got = swap(give, "tp", 2)
    counted = counted + got
    pair = [bit for _, bit in others[1:3]]
    gots = [swap(counted, "dp", bit) for bit in [*pair, *([sum(pair)] if len(pair) == 2 else [])]]
    own, slope_one, first, normed_one, factor_one = forward_rows(
        True, ids, early, c2, layer_input, outs[2], vecs, message_got, w_ins, w_backs, share
    )
    own, *gots = tie(own, *gots)
    counted = sum(gots, counted)
    for axis, which in others[3:]:
        counted = counted + swap(counted, axis, which)

    flat = ADAPTERS * BOTTLENECK
    down_t = jnp.transpose(ad_down, (1, 2, 0)).reshape(flat, model)
    up = ad_up.reshape(flat, model)
    layer_out, keep, give, sums, turn, slope_ad, base, normed_two, factor_two = adapters(
        total_slots,
        ids,
        [
            own, ffn_got, first, cotangent, weight_m, counted, vecs, ad_down_bias, ad_up_bias, down_t, up,
            join_query, join_key, join_value,
        ],
    )
    got = swap(give, *core)
    gpre2, gpre2_low = run(
        adapter_rest_kernel,
        (),
        [turn, slope_ad, base, normed_two, factor_two, vecs, down_t, join_query, join_key],
        [((share, model), f32), ((share, model), bf16)],
    )
    gpre2_got = swap(gpre2_low, "tp", 2)

    state = {"at": 0, "history": [], "rows": keep.shape[0] // 2}

    def sum_step(keeps, gots, sums):
        at = state["at"]
        start = at == 0
        split = state["rows"] // 2 >= LEAST_ROWS
        arrays = [keeps, gots] if start else [a for pair in zip(keeps, gots) for a in pair]
        keeps, gives, sums = fold(ids, 7 + 2 * at, start, split, arrays, state["rows"], sums)
        if split:
            state["rows"] //= 2
            state["history"].append(at)
        state["at"] = at + 1
        return keeps, [swap(g, *stream[at]) for g, stream in zip(gives, streams)], sums

    (back_own,) = backward_rows(gpre2_low, slope_one, w_backs, w_ins, f32)
    back_own, got = tie(back_own, got)
    keeps, gots, sums = sum_step(keep, got, sums)
    keeps[0], gpre2_got = tie(keeps[0], gpre2_got)
    (back_give,) = backward_rows(gpre2_got, slope_two, w_backs, w_ins, bf16)
    back_give, *gots = tie(back_give, *gots)
    keeps, gots, sums = sum_step(keeps, gots, sums)
    keeps[0], back_give = tie(keeps[0], back_give)
    back_got = swap(back_give, "tp", 2)
    gpre1, c0, c1, c2, c3 = first_norm_back(back_own, back_got, gpre2, normed_one, factor_one, vecs, outs)
    c0, *gots = tie(c0, *gots)
    keeps, gots, sums = sum_step(keeps, gots, sums)
    c0, keeps[0] = tie(c0, keeps[0])
    c2, c3, c1 = swap(c2, "tp", 2), swap(c3, "tp", 3), swap(c1, "tp", 1)
    shared = ((near, far), (e_near, e_far), (rl_near, rl_far), (q, k, v))
    before = list(attend_back((0, 2), ids, (c0, c1), *shared, [], None, share))
    before[0], *gots = tie(before[0], *gots)
    keeps, gots, sums = sum_step(keeps, gots, sums)
    before[0], keeps[0] = tie(before[0], keeps[0])
    far_part, near_part = attend_back((1, 3), ids, (c2, c3), *shared, before, w_t, share)
    far_part, *gots = tie(far_part, *gots)
    far_got = swap(far_part, "tp", 1)
    while state["at"] < len(others) + 1:
        keeps, gots, sums = sum_step(keeps, gots, sums)
    arrays = [a for pair in zip(keeps, gots) for a in pair]
    keeps, _, sums = fold(ids, 0, False, False, arrays, state["rows"], sums)
    keeps[0], far_got = tie(keeps[0], far_got)
    part_own, part_give = run(
        chip_kernel, (), [near_part, far_got, gpre1], [((share, model), f32), ((share, model), bf16)]
    )
    part_got = swap(part_give, "tp", 2)
    for at in reversed(state["history"]):
        gots = [swap(a, *stream[at]) for a, stream in zip(keeps, streams)]
        gots[0], part_own = tie(gots[0], part_own)
        keeps = join(ids, 7 + 2 * at, at == 0, keeps, gots)
    keeps[0], part_got = tie(keeps[0], part_got)
    got = swap(keeps[0], *core)
    input_grad = part_own + part_got.astype(f32)
    query_grad, key_grad, value_grad = finish(ids, keeps[0], got, join_query, join_key)
    return (layer_out, input_grad, query_grad, key_grad, value_grad, sums[0], sums[1])


def solution(mesh):
    placed = (
        P("dp", None),
        P(("dp", "tp"), None),
        P(),
        P(),
        P(("dp", "tp")),
        P(None, None, "tp"),
        P(None, "tp"),
        P("tp", None),
        P(),
        P(),
        P(),
        P(None, "tp"),
        P("tp"),
        P("tp", None),
        P(),
        P(),
        P(),
        P(),
        P(),
        P(),
        P(),
        P(),
        P(),
        P(),
        P(),
        P(),
    )
    return jax.shard_map(
        body,
        mesh=mesh,
        in_specs=placed,
        out_specs=(P(("dp", "tp"), None), P(("dp", "tp"), None), P(), P(), P(), P(), P()),
        check_vma=False,
    )
```

```python
import functools

import jax
import jax.numpy as jnp
from jax import lax
from jax.experimental import pallas as pl
from jax.experimental.pallas import tpu as pltpu
from jax.sharding import PartitionSpec as P

HEAD_DIM = 64
ADAPTERS = 16
BOTTLENECK = 48
SEQ_GRP = 4
LEAST_ROWS = 96
FLOPS = 1.15e9

EPS = 1e-06
NEG = -1e30
ROOT_HALF = 0.7071067811865476
INV_ROOT_TAU = 0.3989422804014327

f32 = jnp.float32
bf16 = jnp.bfloat16
i32 = jnp.int32

HEADER = 64

ORDER = (0, 2, 1, 3)


def gelu_both(values):
    phi = 0.5 * (1.0 + lax.erf(values * ROOT_HALF))
    return values * phi, phi + values * jnp.exp(-0.5 * values * values) * INV_ROOT_TAU


def row_mean(values):
    return jnp.sum(values, axis=-1, keepdims=True) * (1.0 / values.shape[-1])


def norm_parts(values):
    center = values - row_mean(values)
    factor = lax.rsqrt(row_mean(center * center) + EPS)
    return center * factor, factor


def norm_back(gradient, normed, factor, gain_vec):
    scaled = gradient * gain_vec
    return factor * (scaled - row_mean(scaled) - normed * row_mean(scaled * normed))


def mm(a, b):
    return lax.dot_general(a, b, (((1,), (0,)), ((), ())), preferred_element_type=f32)


def mm_nt(a, b):
    return lax.dot_general(a, b, (((1,), (1,)), ((), ())), preferred_element_type=f32)


def mm_tn(a, b):
    return lax.dot_general(a, b, (((0,), (0,)), ((), ())), preferred_element_type=f32)


def halves_of(a):
    high = a.astype(bf16)
    return high, (a - high.astype(f32)).astype(bf16)


def swap(value, axis, bit):
    size = lax.axis_size(axis)
    return lax.ppermute(value, axis, [(i, i ^ bit) for i in range(size)])


def tie(*values):
    return lax.optimization_barrier(values)


def run(kernel, scalars, inputs, outputs, streamed=(), scratch=(), vmem=12, micros=0.1):
    smem = pl.BlockSpec(memory_space=pltpu.SMEM)
    vmem_spec = pl.BlockSpec(memory_space=pltpu.VMEM)
    any_spec = pl.BlockSpec(memory_space=pl.ANY)
    outs = pl.pallas_call(
        kernel,
        in_specs=[smem] * len(scalars) + [vmem_spec] * len(inputs) + [any_spec] * len(streamed),
        out_specs=[vmem_spec if len(o) == 2 else any_spec for o in outputs],
        out_shape=[pltpu.VMEM(*o) if len(o) == 2 else jax.ShapeDtypeStruct(*o[:2]) for o in outputs],
        scratch_shapes=list(scratch),
        compiler_params=pltpu.CompilerParams(vmem_limit_bytes=vmem * 1024 * 1024),
        cost_estimate=pl.CostEstimate(flops=int(micros * FLOPS), bytes_accessed=1, transcendentals=0),
    )(
        *scalars,
        *[pltpu.with_memory_space_constraint(a, pltpu.VMEM) for a in inputs],
        *[pltpu.with_memory_space_constraint(a, pltpu.HBM) for a in streamed],
    )
    return list(outs)


def head_mask(width, head):
    lane = lax.broadcasted_iota(i32, (1, width), 1)
    return (lane >= head * HEAD_DIM) & (lane < (head + 1) * HEAD_DIM)


def group_ends(ints):
    count = (ints.shape[0] - HEADER) // 2

    def add(s, ends):
        spot = ints[HEADER + count + s] - ints[1] * SEQ_GRP
        length = jnp.where(spot >= 0, ints[HEADER + s], 0)
        return tuple(e + jnp.where(spot <= j, length, 0) for j, e in enumerate(ends))

    return lax.fori_loop(0, count, add, (jnp.int32(0),) * SEQ_GRP, unroll=8)


def segment_of(positions, ends):
    segment = jnp.zeros(positions.shape, i32)
    for e in ends:
        segment = segment + (positions >= e).astype(i32)
    return jnp.where(positions < ends[-1], segment, SEQ_GRP + positions)


def window(rows, start, ends, group_rows):
    low = jnp.int32(0)
    high = jnp.int32(0)
    last = start + rows - 1
    for e in ends:
        low = jnp.where(start >= e, jnp.maximum(low, e), low)
    for e in reversed(ends):
        high = jnp.where(last < e, e, high)
    padded = last >= ends[-1]
    low = jnp.where(start >= ends[-1], start, low)
    high = jnp.where(padded, start + rows, high)
    low = jnp.minimum(low // 128 * 128, group_rows - 128)
    return low, high - low


def by_window(rows, start, ends, group_rows, act):
    low, span = window(rows, start, ends, group_rows)
    widths = [w for w in (512, 768) if w < group_rows] + [group_rows]
    least = 0
    for w in widths:
        fits = (span > least) & (span <= w) if w < group_rows else span > least

        @pl.when(fits)
        def _(w=w):
            act(pl.multiple_of(jnp.minimum(low, group_rows - w), 128), w)

        least = w


def one_row(tile):
    return jnp.concatenate([tile[j : j + 1, :] for j in range(tile.shape[0])], axis=1)


def project_kernel(ids, x_hbm, w_hbm, bias_hbm, mask_hbm, *refs):
    vectors, refs = refs[:9], refs[9:]
    q_ref, k_ref, v_ref, message, weight, vecs, x_ref, w_ref, bias_ref, mask_ref, *tiles, sems = refs
    group_rows, width = q_ref.shape
    share = weight.shape[0]
    chunks = group_rows // share
    pairs = [(w_hbm, w_ref)]
    for c in range(chunks):
        rows = pl.ds(c * share, share)
        pairs.append((x_hbm.at[rows, :], x_ref.at[rows, :]))
    pairs += [(bias_hbm, bias_ref), (mask_hbm, mask_ref), *zip(vectors, tiles)]
    copies = [pltpu.make_async_copy(source, target, sems.at[j]) for j, (source, target) in enumerate(pairs)]
    for copy in copies:
        copy.start()
    bias_at = chunks + 1
    copies[0].wait()
    copies[bias_at].wait()
    bias = bias_ref[...].astype(f32)
    for c in range(chunks):
        rows = slice(c * share, (c + 1) * share)
        copies[1 + c].wait()
        x = x_ref[rows, :]
        k_ref[rows, :] = mm_nt(x, w_ref[width : 2 * width, :]).astype(bf16)
        v_ref[rows, :] = (mm_nt(x, w_ref[2 * width :, :]) + bias[1:2]).astype(bf16)
        q = (mm_nt(x, w_ref[:width, :]) + bias[0:1]).astype(bf16)
        q_ref[rows, :] = (q.astype(f32) * HEAD_DIM ** (-0.5)).astype(bf16)

    for copy in copies[bias_at + 1 :]:
        copy.wait()
    for j, tile in enumerate(tiles):
        vecs[j : j + 1, :] = one_row(tile[...].astype(f32))
    vecs[9:, :] = jnp.zeros((vecs.shape[0] - 9, vecs.shape[1]), f32)
    ends = group_ends(ids)
    lane = lax.broadcasted_iota(i32, (1, share), 1)
    row = jnp.where(ids[0] * share + lane < ends[-1], one_row(mask_ref[...].astype(f32)), 0.0)
    total = jnp.sum(row, axis=-1, keepdims=True)
    message[0:1, :] = vecs[8:9, :]
    message[1:, :] = jnp.broadcast_to(total, (message.shape[0] - 1, message.shape[1]))
    here = lax.broadcasted_iota(i32, (share, share), 0) == lax.broadcasted_iota(i32, (share, share), 1)
    weight[...] = jnp.sum(jnp.where(here, jnp.broadcast_to(row, (share, share)), 0.0), axis=-1, keepdims=True)


def project(ids, x, w_t, b_qv, mask, vectors, share):
    group_rows, model = x.shape
    width = w_t.shape[0] // 3
    streamed = [x, w_t, b_qv, mask.reshape(-1, 128), *[v.reshape(-1, 128) for v in vectors]]
    return run(
        project_kernel,
        (ids,),
        [],
        [((group_rows, width), bf16)] * 3 + [((8, model), f32), ((share, 1), f32), ((16, model), f32)],
        streamed=streamed,
        scratch=[pltpu.VMEM(a.shape, a.dtype) for a in streamed]
        + [pltpu.SemaphoreType.DMA((group_rows // share + len(streamed),))],
        micros=3.0,
    )


def attend_kernel(first, ids, q_ref, k_ref, v_ref, context_ref, e_ref, rl_ref):
    rows = context_ref.shape[0] // 2
    group_rows, width = k_ref.shape
    heads = width // HEAD_DIM
    ends = group_ends(ids)

    def one(t, carry):
        start = pl.multiple_of(ids[2 + first + t] * rows, rows)
        at = pl.multiple_of(t * rows, rows)

        def act(key0, w):
            q = q_ref[pl.ds(start, rows), :].astype(f32)
            seg_q = segment_of(start + lax.broadcasted_iota(i32, (rows, 1), 0), ends)
            seg_k = segment_of(key0 + lax.broadcasted_iota(i32, (1, w), 1), ends)
            k = k_ref[pl.ds(key0, w), :]
            v = v_ref[pl.ds(key0, w), :]
            context = jnp.zeros((rows, width), f32)
            wide = jnp.zeros((rows, width), f32)
            for h in range(heads):
                mask = head_mask(width, h)
                scores = mm_nt(jnp.where(mask, q, 0.0).astype(bf16), k)
                scores = jnp.where(seg_q == seg_k, scores, NEG)
                e = jnp.exp(scores - jnp.max(scores, axis=-1, keepdims=True))
                inverse = 1.0 / jnp.sum(e, axis=-1, keepdims=True)
                low = e.astype(bf16)
                e_ref[pl.ds(pl.multiple_of((t * heads + h) * rows, rows), rows), :w] = low
                context = jnp.where(mask, mm(low, v) * inverse, context)
                wide = jnp.where(mask, inverse, wide)
            rl_ref[pl.ds(at, rows), :] = wide
            context_ref[pl.ds(at, rows), :] = context.astype(bf16)

        by_window(rows, start, ends, group_rows, act)
        return carry

    lax.fori_loop(0, 2, one, 0)


def attend(first, ids, q, k, v, share):
    group_rows, width = k.shape
    heads = width // HEAD_DIM
    return run(
        functools.partial(attend_kernel, first),
        (ids,),
        [q, k, v],
        [
            ((2 * share, width), bf16),
            ((2 * heads * share, group_rows), bf16),
            ((2 * share, width), f32),
        ],
        vmem=20,
        micros=3.0,
    )


def attend_back_kernel(spots, first, last, ids, *refs):
    count = len(spots)
    grads, refs = refs[:count], refs[count:]
    contexts, es, rls, refs = refs[0:2], refs[2:4], refs[4:6], refs[6:]
    q_ref, k_ref, v_ref, refs = refs[0], refs[1], refs[2], refs[3:]
    if not first:
        before, refs = refs[:3], refs[3:]
    if last:
        w_ref, far_out, near_out, gq, gk, gv = refs
    else:
        gq, gk, gv = refs
    rows = grads[0].shape[0]
    group_rows, width = k_ref.shape
    heads = width // HEAD_DIM
    ends = group_ends(ids)
    if first:
        gk[...] = jnp.zeros_like(gk)
        gv[...] = jnp.zeros_like(gv)
    else:
        gq[...] = before[0][...]
        gk[...] = before[1][...]
        gv[...] = before[2][...]
    for g_ref, spot in zip(grads, spots):
        start = pl.multiple_of(ids[2 + spot] * rows, rows)
        part, t = spot // 2, spot % 2
        g = g_ref[...].astype(f32) * rls[part][t * rows : (t + 1) * rows, :]
        dots = g * contexts[part][t * rows : (t + 1) * rows, :].astype(f32)
        q = q_ref[pl.ds(start, rows), :].astype(f32)

        def act(key0, w, g=g, dots=dots, q=q, part=part, t=t, start=start):
            keys = pl.ds(key0, w)
            k = k_ref[keys, :]
            v = v_ref[keys, :]
            out = jnp.zeros((rows, width), f32)
            add_k = jnp.zeros((w, width), f32)
            add_v = jnp.zeros((w, width), f32)
            for h in range(heads):
                mask = head_mask(width, h)
                g_head = jnp.where(mask, g, 0.0).astype(bf16)
                e = es[part][(t * heads + h) * rows : (t * heads + h + 1) * rows, :w]
                delta = jnp.sum(jnp.where(mask, dots, 0.0), axis=-1, keepdims=True)
                ds = (e.astype(f32) * (mm_nt(g_head, v) - delta)).astype(bf16)
                out = jnp.where(mask, mm(ds, k), out)
                add_k = add_k + mm_tn(ds, jnp.where(mask, q, 0.0).astype(bf16))
                add_v = add_v + mm_tn(e, g_head)
            gk[keys, :] += add_k
            gv[keys, :] += add_v
            gq[pl.ds(start, rows), :] = (out * HEAD_DIM ** (-0.5)).astype(bf16)

        by_window(rows, start, ends, group_rows, act)
    if last:
        for out, pair in ((far_out, (2, 3)), (near_out, (0, 1))):
            for t, spot in enumerate(pair):
                own = pl.ds(pl.multiple_of(ids[2 + spot] * rows, rows), rows)
                part = (
                    mm(gq[own, :], w_ref[:width, :])
                    + mm(gk[own, :].astype(bf16), w_ref[width : 2 * width, :])
                    + mm(gv[own, :].astype(bf16), w_ref[2 * width :, :])
                )
                out[t * rows : (t + 1) * rows, :] = part.astype(out.dtype)


def attend_back(spots, ids, grads, contexts, es, rls, qkv, before, w_t, share):
    group_rows, width = qkv[0].shape
    last = w_t is not None
    sums = [((group_rows, width), bf16), ((group_rows, width), f32), ((group_rows, width), f32)]
    inputs = [*grads, *contexts, *es, *rls, *qkv, *before]
    if last:
        model = w_t.shape[1]
        outputs = [((2 * share, model), bf16), ((2 * share, model), f32)]
        scratch = [pltpu.VMEM(*o) for o in sums]
        inputs.append(w_t)
    else:
        outputs, scratch = sums, []
    return run(
        functools.partial(attend_back_kernel, spots, not before, last),
        (ids,),
        inputs,
        outputs,
        scratch=scratch,
        vmem=20,
        micros=5.0 if last else 0.1,
    )


def early_kernel(c0, c1, c3, o0, o1, o3, out):
    share = out.shape[0] // 2
    attn = mm(c0[...], o0[...]) + mm(c1[...], o1[...])
    for t in range(2):
        rows = slice(t * share, (t + 1) * share)
        out[rows, :] = attn[rows] + mm(c3[(1 - t) * share : (2 - t) * share, :], o3[...])


def adapter_constants(down_bias, wq, wk, query_key, member_ref, spread_ref, bias_ref):
    query_key[...] = mm_nt(wq[...], wk[...]).astype(bf16)
    flat = member_ref.shape[0]
    lane = lax.broadcasted_iota(i32, (flat, ADAPTERS), 0) - BOTTLENECK * lax.broadcasted_iota(
        i32, (flat, ADAPTERS), 1
    )
    member_ref[...] = ((lane >= 0) & (lane < BOTTLENECK)).astype(f32).astype(bf16)
    lane = lax.broadcasted_iota(i32, (ADAPTERS, flat), 1) - BOTTLENECK * lax.broadcasted_iota(
        i32, (ADAPTERS, flat), 0
    )
    spread = ((lane >= 0) & (lane < BOTTLENECK)).astype(f32)
    spread_ref[...] = spread.astype(bf16)
    cycle = lax.broadcasted_iota(i32, (BOTTLENECK, flat), 1) - lax.broadcasted_iota(i32, (BOTTLENECK, flat), 0)
    repeat = jnp.zeros(cycle.shape, f32)
    for a in range(ADAPTERS):
        repeat = repeat + (cycle == a * BOTTLENECK).astype(f32)
    bias_row = jnp.sum(mm(down_bias[...], repeat.astype(bf16)) * spread, axis=0, keepdims=True)
    bias_ref[...] = jnp.broadcast_to(bias_row, bias_ref.shape)


def forward_kernel(own, ids, early, c2, x_ref, o2, vecs, message, in0, in1, back0, back1, *rest):
    if own:
        inner_ref, down_bias, wq, wk, part_ref, slope, slope_two, first_ref, normed_ref, factor_ref, *constants = rest
    else:
        count, part_ref, inner_ref = rest
        write_small(part_ref, jnp.broadcast_to(count[0:1, 0:1], (8, x_ref.shape[1])))
    share = early.shape[0] // 2
    t = 0 if own else 1
    attn = early[t * share : (t + 1) * share, :] + mm(c2[(1 - t) * share : (2 - t) * share, :], o2[...])
    vec = vecs[...].astype(f32)
    start = pl.multiple_of(ids[2 if own else 3] * share, share)
    normed, factor = norm_parts(attn + vec[0:1] + x_ref[pl.ds(start, share), :].astype(f32))
    first = normed * vec[1:2] + vec[2:3]
    low = first.astype(bf16)
    part = jnp.zeros(first.shape, f32)
    units = in0.shape[1]
    chunk = units // 2
    for j, (w_in, bias, w_back) in enumerate(((in0, vec[8:9], back0), (in1, message[0:1, :], back1))):
        for at in range(0, units, chunk):
            here = slice(at, at + chunk)
            columns = slice(j * units + at, j * units + at + chunk)
            inner = mm(low, w_in[:, here]) + bias[:, here]
            if own:
                act, bend = gelu_both(inner)
                slope[:, columns] = bend.astype(bf16)
                slope_two[:, columns] = gelu_both(inner_ref[:, columns])[1].astype(bf16)
            else:
                act = 0.5 * inner * (1.0 + lax.erf(inner * ROOT_HALF))
                inner_ref[:, columns] = inner
            part = part + mm(act.astype(bf16), w_back[here, :])
    part_ref[:share, :] = part.astype(part_ref.dtype)
    if own:
        first_ref[...] = first
        normed_ref[...] = normed
        factor_ref[...] = jnp.broadcast_to(factor, factor_ref.shape)
        adapter_constants(down_bias, wq, wk, *constants)


def forward_rows(own, ids, early, c2, x, o2, vecs, message, w_ins, w_backs, share, *more):
    model = x.shape[1]
    units = w_ins[0].shape[1]
    slope = ((share, 2 * units), bf16)
    flat = ADAPTERS * BOTTLENECK
    if own:
        outputs = [((share, model), f32), slope, slope] + [((share, model), f32)] * 2 + [((share, 128), f32)]
        outputs += [((model, model), bf16), ((flat, ADAPTERS), bf16), ((ADAPTERS, flat), bf16), ((8, flat), f32)]
    else:
        outputs = [((share + 16, model), bf16), ((share, 2 * units), f32)]
    return run(
        functools.partial(forward_kernel, own),
        (ids,),
        [early, c2, x, o2, vecs, message, *w_ins, *w_backs, *more],
        outputs,
        vmem=16,
        micros=3.0,
    )


def backward_kernel(gp, slope, back0, back1, in0, in1, part_ref):
    grad = gp[...]
    units = in0.shape[1]
    part = jnp.zeros(grad.shape, f32)
    for j, (w_back, w_in) in enumerate(((back0, in0), (back1, in1))):
        bend = slope[:, j * units : (j + 1) * units].astype(f32)
        inner = (bend * mm_nt(grad, w_back[...])).astype(bf16)
        part = part + mm_nt(inner, w_in[...])
    part_ref[...] = part.astype(part_ref.dtype)


def backward_rows(grad, slope, w_backs, w_ins, dtype):
    share, model = grad.shape
    units = w_ins[0].shape[1]
    return run(
        backward_kernel,
        (),
        [grad, slope, *w_backs, *w_ins],
        [((share, model), dtype)],
    )


def first_norm_kernel(own, got, gpre2, normed, factor, vecs, o0, o1, o2, o3, gpre1, c0, c1, c2, c3):
    grad = own[...] + got[...].astype(f32) + gpre2[...]
    grad = norm_back(grad, normed[...], factor[:, 0:1], vecs[...].astype(f32)[1:2])
    gpre1[...] = grad
    low = grad.astype(bf16)
    for c, o in ((c2, o2), (c3, o3), (c1, o1), (c0, o0)):
        c[...] = mm_nt(low, o[...]).astype(bf16)


def first_norm_back(own, got, gpre2, normed, factor, vecs, outs):
    share, model = own.shape
    width = outs[0].shape[0]
    return run(
        first_norm_kernel,
        (),
        [own, got, gpre2, normed, factor, vecs, *outs],
        [((share, model), f32)] + [((share, width), bf16)] * 4,
    )


def adapter_kernel(
    slots, ids, own, got, first_ref, cot, weight, count, vecs, wqk, member_ref, spread_ref, bias_ref, up_bias, down, up,
    wv,
    out_hbm, keep, give, sums, turn_ref, reduced_ref, mix_ref, base_ref, normed_ref, factor_ref, layer_out, lefts, sem,
):
    flat, model = up.shape
    share = own.shape[0]
    vec = vecs[...].astype(f32)
    member = member_ref[...]
    spread = spread_ref[...]
    inv_root = model ** (-0.5)
    scale = 0.5 * slots / jnp.maximum(count[0:1, 0:1] + read_small(got)[0:1, 0:1], 1.0)

    normed_two, factor_two = norm_parts(own[...] + got[:share, :].astype(f32) + vec[3:4] + first_ref[...])
    normed_ref[...] = normed_two
    factor_ref[...] = jnp.broadcast_to(factor_two, factor_ref.shape)
    second = normed_two * vec[4:5] + vec[5:6]
    second_low = second.astype(bf16)
    query_key = mm(second_low, wqk[...]) * inv_root
    query_key_low = query_key.astype(bf16)
    lift_key = mm_nt(query_key_low, up[...])
    reduced = mm_nt(second_low, down[...]) + bias_ref[0:1, :]
    reduced_ref[...] = reduced
    squeezed = 0.5 * reduced * (1.0 + lax.erf(reduced * ROOT_HALF))
    squeezed = squeezed.astype(bf16).astype(f32)
    logits = (
        mm((squeezed * lift_key).astype(bf16), member)
        + mm_nt(query_key_low, up_bias[...])
        + jnp.sum(query_key * second, axis=-1, keepdims=True)
    )
    shifted = logits - jnp.max(logits, axis=-1, keepdims=True)
    log_probs = shifted - jnp.log(jnp.sum(jnp.exp(shifted), axis=-1, keepdims=True))
    joining = jnp.exp(log_probs)
    entropy = -jnp.sum(joining * log_probs, axis=-1, keepdims=True)
    total = jnp.sum(joining, axis=-1, keepdims=True)
    joining_low = joining.astype(bf16)
    joining_wide = mm(joining_low, spread)
    joined_low = (joining_wide * squeezed).astype(bf16)
    mixed = total * second + mm(joined_low, up[...]) + mm(joining_low, up_bias[...])
    mixed_low = mixed.astype(bf16)
    normed_join, factor_join = norm_parts(second + mm(mixed_low, wv[...]))
    grad_out = cot[...].astype(f32)
    grad_pref = norm_back(grad_out, normed_join, factor_join, vec[6:7])
    grad_pref_low = grad_pref.astype(bf16)
    back_value = mm_nt(grad_pref_low, wv[...])
    back_value_low = back_value.astype(bf16)
    lift_value = mm_nt(back_value_low, up[...])
    grad_probs = (
        mm((squeezed * lift_value).astype(bf16), member)
        + mm_nt(back_value_low, up_bias[...])
        + jnp.sum(back_value * second, axis=-1, keepdims=True)
    )
    mean_grad = jnp.sum(joining * grad_probs, axis=-1, keepdims=True)
    grad_logits = joining * (grad_probs - mean_grad) - scale * weight[...] * joining * (log_probs + entropy)
    logits_low = grad_logits.astype(bf16)
    grad_wide = mm(logits_low, spread)
    logit_sum = jnp.sum(grad_logits, axis=-1, keepdims=True)
    turned = (
        logit_sum * second + mm((grad_wide * squeezed).astype(bf16), up[...]) + mm(logits_low, up_bias[...])
    ) * inv_root
    turned_low = turned.astype(bf16)
    turn_ref[...] = turned_low

    layer_out[...] = normed_join * vec[6:7] + vec[7:8]
    copy = pltpu.make_async_copy(layer_out, out_hbm, sem)
    copy.start()
    small = jnp.concatenate(
        [
            jnp.sum(grad_out * normed_join, axis=0, keepdims=True),
            jnp.sum(grad_out, axis=0, keepdims=True),
            jnp.zeros((sums.shape[0] - 2, model), f32),
        ],
        axis=0,
    )
    sums[...] = small
    write_small(give, small)
    mix_ref[...] = grad_wide * lift_key + joining_wide * lift_value
    base_ref[...] = grad_pref + logit_sum * query_key + total * back_value

    half = model // 2
    lefts[0] = second_low
    lefts[1] = mixed_low
    for j, right in enumerate((turned_low, grad_pref_low)):
        rows = slice(j * half, (j + 1) * half)
        other = lefts[j, :, pl.ds(pl.multiple_of((1 - ids[6]) * half, 128), half)]
        give[rows, :] = mm_tn(other, right).astype(bf16)
        mine = lefts[j, :, pl.ds(pl.multiple_of(ids[6] * half, 128), half)]
        keep[rows, :] = mm_tn(mine, right).astype(bf16)
    copy.wait()


def adapters(slots, ids, arrays):
    share, model = arrays[0].shape
    flat = ADAPTERS * BOTTLENECK
    wide, flat_wide = ((share, model), f32), ((share, flat), f32)
    return run(
        functools.partial(adapter_kernel, slots),
        (ids,),
        arrays,
        [
            ((share, model), f32, None),
            ((model, model), bf16),
            ((model + 16, model), bf16),
            ((8, model), f32),
            ((share, model), bf16),
            flat_wide,
            flat_wide,
            wide,
            wide,
            ((share, 128), f32),
        ],
        scratch=[
            pltpu.VMEM((share, model), f32),
            pltpu.VMEM((2, share, model), bf16),
            pltpu.SemaphoreType.DMA,
        ],
        vmem=20,
        micros=8.0,
    )


def adapter_rest_kernel(turn, reduced, mix, base, normed, factor, vecs, down, wqk, gpre2_ref, gpre2_low):
    grad_reduced = (gelu_both(reduced[...])[1] * mix[...]).astype(bf16)
    grad_second = base[...] + mm(grad_reduced, down[...]) + mm_nt(turn[...], wqk[...])
    grad_pre2 = norm_back(grad_second, normed[...], factor[:, 0:1], vecs[4:5, :])
    gpre2_ref[...] = grad_pre2
    gpre2_low[...] = grad_pre2.astype(bf16)


def write_small(message, sums):
    high, low = halves_of(sums)
    rows = message.shape[0] - 16
    message[rows:, :] = jnp.concatenate([high, low], axis=0)


def read_small(message):
    rows = message.shape[0] - 16
    both = message[rows:, :].astype(f32)
    return both[:8] + both[8:]


def fold_kernel(base, start, split, last, ids, *refs):
    if start:
        keep, got, sums, *outs = refs
        rows = keep.shape[0] // 2
        pieces = [(keep, got, j * rows) for j in range(2)]
    else:
        *arrays, sums = refs[:5]
        outs = refs[5:]
        rows = arrays[0].shape[0]
        pieces = [(arrays[2 * j], arrays[2 * j + 1], 0) for j in range(2)]
        got = arrays[3]
    total = sums[...] + read_small(got)
    outs[-1][...] = total
    for j, (mine, other, at) in enumerate(pieces):
        def both(where):
            return (mine[where, :].astype(f32) + other[where, :].astype(f32)).astype(bf16)

        if split:
            half = rows // 2
            bit = ids[base + j]
            outs[2 * j][...] = both(pl.ds(pl.multiple_of(at + bit * half, 16), half))
            outs[2 * j + 1][:half, :] = both(pl.ds(pl.multiple_of(at + (1 - bit) * half, 16), half))
        elif last:
            outs[j][...] = both(pl.ds(at, rows))
        else:
            whole = both(pl.ds(at, rows))
            outs[2 * j][...] = whole
            outs[2 * j + 1][:rows, :] = whole
    if not last:
        write_small(outs[3], total)


def fold(ids, base, start, split, arrays, rows, sums, last=False):
    model = sums.shape[1]
    rows = rows // 2 if split else rows
    outputs = []
    for j in range(2):
        outputs += [((rows, model), bf16)] + ([] if last else [((rows + 16 * j, model), bf16)])
    outputs.append((sums.shape, f32))
    outs = run(functools.partial(fold_kernel, base, start, split, last), (ids,), [*arrays, sums], outputs)
    if last:
        return outs[:2], None, outs[2]
    return outs[0:4:2], outs[1:4:2], outs[4]


def join_kernel(base, last, ids, *refs):
    outs = refs[4:]
    for j in range(2):
        mine, got = refs[2 * j : 2 * j + 2]
        rows = mine.shape[0]
        bit = ids[base + j]
        out, at = (outs[0], 2 * rows * j) if last else (outs[j], 0)
        out[pl.ds(pl.multiple_of(at + bit * rows, 16), rows), :] = mine[...]
        out[pl.ds(pl.multiple_of(at + (1 - bit) * rows, 16), rows), :] = got[...]


def join(ids, base, last, mine, gots):
    rows, model = mine[0].shape
    outputs = [((4 * rows, model), bf16)] if last else [((2 * rows, model), bf16)] * 2
    arrays = [a for pair in zip(mine, gots) for a in pair]
    return run(functools.partial(join_kernel, base, last), (ids,), arrays, outputs)


def finish_kernel(first, ids, source, wq, wk, *refs):
    half = source.shape[0] // 2
    if first:
        out_q, out_v, key_part, stage, sems = refs
    else:
        key_before, _, _, out_q, out_v, out_k, stage, stage_k, sems = refs
    core = ids[6] if first else 1 - ids[6]
    rows = pl.ds(pl.multiple_of(core * half, half), half)
    copies = []

    def send(j, source, target):
        copies.append(pltpu.make_async_copy(source, target, sems.at[j]))
        copies[-1].start()

    mixed = source[:half, :]
    stage[1] = source[half:, :].astype(f32)
    send(1, stage.at[1], out_v.at[rows, :])
    key = mm_tn(mixed, wq[rows, :])
    if first:
        key_part[...] = key
    else:
        stage_k[...] = key_before[...] + key
        send(2, stage_k, out_k)
    stage[0] = mm(mixed, wk[...])
    send(0, stage.at[0], out_q.at[rows, :])
    for copy in copies:
        copy.wait()


def finish(ids, source, wq, wk, before):
    model = source.shape[1]
    half = source.shape[0] // 2
    first = before is None
    vmem_spec = pl.BlockSpec(memory_space=pltpu.VMEM)
    any_spec = pl.BlockSpec(memory_space=pl.ANY)
    whole = jax.ShapeDtypeStruct((model, model), f32)
    inputs = [source, wq, wk] + ([] if first else [before[2]])
    return pl.pallas_call(
        functools.partial(finish_kernel, first),
        in_specs=[pl.BlockSpec(memory_space=pltpu.SMEM)]
        + [vmem_spec] * len(inputs)
        + ([] if first else [any_spec] * 2),
        out_specs=[any_spec] * 2 + [vmem_spec if first else any_spec],
        out_shape=[whole, whole, pltpu.VMEM((model, model), f32) if first else whole],
        input_output_aliases={} if first else {5: 0, 6: 1},
        scratch_shapes=[pltpu.VMEM((2, half, model), f32)]
        + ([] if first else [pltpu.VMEM((model, model), f32)])
        + [pltpu.SemaphoreType.DMA((3,))],
        compiler_params=pltpu.CompilerParams(vmem_limit_bytes=16 * 1024 * 1024),
        cost_estimate=pl.CostEstimate(flops=int(2 * FLOPS), bytes_accessed=1, transcendentals=0),
    )(ids, *[pltpu.with_memory_space_constraint(a, pltpu.VMEM) for a in inputs], *([] if first else before[:2]))


def chip_kernel(near, got, gpre1, keep, give):
    share = keep.shape[0]
    give[...] = (near[share:, :] + got[share:, :].astype(f32)).astype(bf16)
    keep[...] = near[:share, :] + got[:share, :].astype(f32) + gpre1[...]


def body(
    layer_input,
    cotangent,
    seq_lens,
    seq_place,
    loss_mask,
    w_qkv,
    b_qv,
    w_out,
    b_out,
    ln1_gain,
    ln1_bias,
    w_in,
    b_in,
    w_back,
    b_back,
    ln2_gain,
    ln2_bias,
    ad_down,
    ad_down_bias,
    ad_up,
    ad_up_bias,
    join_query,
    join_key,
    join_value,
    join_gain,
    join_bias,
):
    group_rows, model = layer_input.shape
    share = cotangent.shape[0]
    rank = lax.axis_index("tp")
    dp_rank = lax.axis_index("dp")
    total_slots = group_rows * lax.axis_size("dp")

    core, near_x = ("tp", 1), ("tp", 2)
    others = []
    bit = 1
    while bit < lax.axis_size("dp"):
        others.append(("dp", bit))
        bit *= 2
    streams = [
        [others[0], *others[1:], near_x],
        [*others[1:2], others[0], near_x, *others[2:]],
    ]

    def bit_of(axis, which):
        return (lax.axis_index(axis) // which) % 2

    ids = [rank, dp_rank] + [rank ^ j for j in ORDER] + [bit_of(*core)]
    for at in range(len(others) + 1):
        ids += [bit_of(*stream[at]) for stream in streams]
    ids = jnp.stack(ids).astype(i32)
    ids = jnp.concatenate([ids, jnp.zeros(HEADER - ids.shape[0], i32), seq_lens, seq_place])
    vectors = [b_out, ln1_gain, ln1_bias, b_back, ln2_gain, ln2_bias, join_gain, join_bias, b_in]

    outs = [w_out, swap(w_out, "tp", 1), swap(w_out, "tp", 2)]
    outs.append(None)
    w_ins = [w_in, swap(w_in, "tp", 1)]
    w_backs = [w_back, swap(w_back, "tp", 1)]

    width = w_qkv.shape[2]
    w_t = jnp.transpose(w_qkv, (1, 2, 0)).reshape(3 * width, model)
    q, k, v, message, weight_m, vecs = project(ids, layer_input, w_t, b_qv, loss_mask, vectors, share)
    message_got = swap(message, *core)
    far, e_far, rl_far = attend(2, ids, q, k, v, share)
    far, message_got, outs[1], outs[2], w_ins[1], w_backs[1] = tie(
        far, message_got, *outs[1:3], w_ins[1], w_backs[1]
    )
    outs[3] = swap(outs[2], "tp", 1)
    c1, c3 = swap(far, "tp", 1), swap(far, "tp", 3)
    counted = message[1:2, :128] + message_got[1:2, :128]
    got = swap(counted, *others[0])
    near, e_near, rl_near = attend(0, ids, q, k, v, share)
    c2 = swap(near, "tp", 2)
    near, got, outs[3], c1 = tie(near, got, outs[3], c1)
    counted = counted + got
    pair = [bit for _, bit in others[1:3]]
    for bits in [[*pair, *([sum(pair)] if len(pair) == 2 else [])]] + [[bit] for _, bit in others[3:]]:
        counted = sum([swap(counted, "dp", bit) for bit in bits], counted)
    (early,) = run(early_kernel, (), [near, c1, c3, outs[0], outs[1], outs[3]], [((2 * share, model), f32)])
    early, counted = tie(early, counted)

    give, inner = forward_rows(
        False, ids, early, c2, layer_input, outs[2], vecs, message_got, w_ins, w_backs, share, counted
    )
    ffn_got = swap(give, *near_x)
    own, slope_one, slope_two, first, normed_one, factor_one, *constants = forward_rows(
        True, ids, early, c2, layer_input, outs[2], vecs, message_got, w_ins, w_backs, share, inner,
        ad_down_bias, join_query, join_key,
    )

    flat = ADAPTERS * BOTTLENECK
    down_t = jnp.transpose(ad_down, (1, 2, 0)).reshape(flat, model)
    up = ad_up.reshape(flat, model)
    layer_out, keep, give, sums, turn, reduced, mix, base, normed_two, factor_two = adapters(
        total_slots,
        ids,
        [
            own, ffn_got, first, cotangent, weight_m, counted, vecs, *constants, ad_up_bias, down_t, up, join_value,
        ],
    )
    got = swap(give, *core)
    gpre2, gpre2_low = run(
        adapter_rest_kernel,
        (),
        [turn, reduced, mix, base, normed_two, factor_two, vecs, down_t, constants[0]],
        [((share, model), f32), ((share, model), bf16)],
    )
    gpre2_got = swap(gpre2_low, "tp", 2)

    state = {"at": 0, "history": [], "rows": keep.shape[0] // 2}

    def sum_step(keeps, gots, sums):
        at = state["at"]
        start = at == 0
        split = state["rows"] // 2 >= LEAST_ROWS
        arrays = [keeps, gots] if start else [a for pair in zip(keeps, gots) for a in pair]
        keeps, gives, sums = fold(ids, 7 + 2 * at, start, split, arrays, state["rows"], sums)
        if split:
            state["rows"] //= 2
            state["history"].append(at)
        state["at"] = at + 1
        return keeps, [swap(g, *stream[at]) for g, stream in zip(gives, streams)], sums

    (back_own,) = backward_rows(gpre2_low, slope_one, w_backs, w_ins, f32)
    back_own, got = tie(back_own, got)
    keeps, gots, sums = sum_step(keep, got, sums)
    keeps[0], gpre2_got = tie(keeps[0], gpre2_got)
    (back_give,) = backward_rows(gpre2_got, slope_two, w_backs, w_ins, bf16)
    back_give, *gots = tie(back_give, *gots)
    keeps, gots, sums = sum_step(keeps, gots, sums)
    keeps[0], back_give = tie(keeps[0], back_give)
    back_got = swap(back_give, "tp", 2)
    keeps, gots, sums = sum_step(keeps, gots, sums)
    keeps[0], back_got = tie(keeps[0], back_got)
    gpre1, c0, c1, c2, c3 = first_norm_back(back_own, back_got, gpre2, normed_one, factor_one, vecs, outs)
    c2, c3, c1 = swap(c2, "tp", 2), swap(c3, "tp", 3), swap(c1, "tp", 1)
    shared = ((near, far), (e_near, e_far), (rl_near, rl_far), (q, k, v))
    before = list(attend_back((0,), ids, (c0,), *shared, [], None, share))
    before[0], *gots = tie(before[0], *gots)
    keeps, gots, sums = sum_step(keeps, gots, sums)
    before[0], keeps[0] = tie(before[0], keeps[0])
    far_part, near_part = attend_back((2, 1, 3), ids, (c1, c2, c3), *shared, before, w_t, share)
    far_part, *gots = tie(far_part, *gots)
    far_got = swap(far_part, "tp", 1)
    while state["at"] < len(others) + 1:
        keeps, gots, sums = sum_step(keeps, gots, sums)
    arrays = [a for pair in zip(keeps, gots) for a in pair]
    keeps, _, sums = fold(ids, 0, False, False, arrays, state["rows"], sums, last=True)
    gain_grad, bias_grad = sums[0], sums[1]
    part_own, part_give = run(
        chip_kernel, (), [near_part, far_got, gpre1], [((share, model), f32), ((share, model), bf16)]
    )
    part_got = swap(part_give, "tp", 2)
    for at in reversed(state["history"]):
        gots = [swap(a, *stream[at]) for a, stream in zip(keeps, streams)]
        gots[0], part_own, gain_grad, bias_grad = tie(gots[0], part_own, gain_grad, bias_grad)
        keeps = join(ids, 7 + 2 * at, at == 0, keeps, gots)
    keeps[0], part_got = tie(keeps[0], part_got)
    got = swap(keeps[0], *core)
    input_grad = part_own + part_got.astype(f32)
    part = finish(ids, keeps[0], join_query, join_key, None)
    query_grad, value_grad, key_grad = finish(ids, got, join_query, join_key, part)
    return (layer_out, input_grad, query_grad, key_grad, value_grad, gain_grad, bias_grad)


def solution(mesh):
    placed = (
        P("dp", None),
        P(("dp", "tp"), None),
        P(),
        P(),
        P(("dp", "tp")),
        P(None, None, "tp"),
        P(None, "tp"),
        P("tp", None),
        P(),
        P(),
        P(),
        P(None, "tp"),
        P("tp"),
        P("tp", None),
        P(),
        P(),
        P(),
        P(),
        P(),
        P(),
        P(),
        P(),
        P(),
        P(),
        P(),
        P(),
    )
    return jax.shard_map(
        body,
        mesh=mesh,
        in_specs=placed,
        out_specs=(P(("dp", "tp"), None), P(("dp", "tp"), None), P(), P(), P(), P(), P()),
        check_vma=False,
    )
```

```python
import functools

import jax
import jax.numpy as jnp
from jax import lax
from jax.experimental import pallas as pl
from jax.experimental.pallas import tpu as pltpu
from jax.sharding import PartitionSpec as P

HEAD_DIM = 64
ADAPTERS = 16
BOTTLENECK = 48
SEQ_GRP = 4
LEAST_ROWS = 96
FLOPS = 1.15e9

EPS = 1e-06
NEG = -1e30
ROOT_HALF = 0.7071067811865476
INV_ROOT_TAU = 0.3989422804014327

f32 = jnp.float32
bf16 = jnp.bfloat16
i32 = jnp.int32

HEADER = 64

ORDER = (0, 2, 1, 3)


def gelu_both(values):
    phi = 0.5 * (1.0 + lax.erf(values * ROOT_HALF))
    return values * phi, phi + values * jnp.exp(-0.5 * values * values) * INV_ROOT_TAU


def row_mean(values):
    return jnp.sum(values, axis=-1, keepdims=True) * (1.0 / values.shape[-1])


def norm_parts(values):
    center = values - row_mean(values)
    factor = lax.rsqrt(row_mean(center * center) + EPS)
    return center * factor, factor


def norm_back(gradient, normed, factor, gain_vec):
    scaled = gradient * gain_vec
    return factor * (scaled - row_mean(scaled) - normed * row_mean(scaled * normed))


def mm(a, b):
    return lax.dot_general(a, b, (((1,), (0,)), ((), ())), preferred_element_type=f32)


def mm_nt(a, b):
    return lax.dot_general(a, b, (((1,), (1,)), ((), ())), preferred_element_type=f32)


def mm_tn(a, b):
    return lax.dot_general(a, b, (((0,), (0,)), ((), ())), preferred_element_type=f32)


def halves_of(a):
    high = a.astype(bf16)
    return high, (a - high.astype(f32)).astype(bf16)


def swap(value, axis, bit):
    size = lax.axis_size(axis)
    return lax.ppermute(value, axis, [(i, i ^ bit) for i in range(size)])


def tie(*values):
    return lax.optimization_barrier(values)


def run(kernel, scalars, inputs, outputs, streamed=(), scratch=(), vmem=12, micros=0.1):
    smem = pl.BlockSpec(memory_space=pltpu.SMEM)
    vmem_spec = pl.BlockSpec(memory_space=pltpu.VMEM)
    any_spec = pl.BlockSpec(memory_space=pl.ANY)
    outs = pl.pallas_call(
        kernel,
        in_specs=[smem] * len(scalars) + [vmem_spec] * len(inputs) + [any_spec] * len(streamed),
        out_specs=[vmem_spec if len(o) == 2 else any_spec for o in outputs],
        out_shape=[pltpu.VMEM(*o) if len(o) == 2 else jax.ShapeDtypeStruct(*o[:2]) for o in outputs],
        scratch_shapes=list(scratch),
        compiler_params=pltpu.CompilerParams(vmem_limit_bytes=vmem * 1024 * 1024),
        cost_estimate=pl.CostEstimate(flops=int(micros * FLOPS), bytes_accessed=1, transcendentals=0),
    )(
        *scalars,
        *[pltpu.with_memory_space_constraint(a, pltpu.VMEM) for a in inputs],
        *[pltpu.with_memory_space_constraint(a, pltpu.HBM) for a in streamed],
    )
    return list(outs)


def head_mask(width, head):
    lane = lax.broadcasted_iota(i32, (1, width), 1)
    return (lane >= head * HEAD_DIM) & (lane < (head + 1) * HEAD_DIM)


def group_ends(ints):
    count = (ints.shape[0] - HEADER) // 2

    def add(s, ends):
        spot = ints[HEADER + count + s] - ints[1] * SEQ_GRP
        length = jnp.where(spot >= 0, ints[HEADER + s], 0)
        return tuple(e + jnp.where(spot <= j, length, 0) for j, e in enumerate(ends))

    return lax.fori_loop(0, count, add, (jnp.int32(0),) * SEQ_GRP, unroll=8)


def segment_of(positions, ends):
    segment = jnp.zeros(positions.shape, i32)
    for e in ends:
        segment = segment + (positions >= e).astype(i32)
    return jnp.where(positions < ends[-1], segment, SEQ_GRP + positions)


def window(rows, start, ends, group_rows):
    low = jnp.int32(0)
    high = jnp.int32(0)
    last = start + rows - 1
    for e in ends:
        low = jnp.where(start >= e, jnp.maximum(low, e), low)
    for e in reversed(ends):
        high = jnp.where(last < e, e, high)
    padded = last >= ends[-1]
    low = jnp.where(start >= ends[-1], start, low)
    high = jnp.where(padded, start + rows, high)
    low = jnp.minimum(low // 128 * 128, group_rows - 128)
    return low, high - low


def by_window(rows, start, ends, group_rows, act):
    low, span = window(rows, start, ends, group_rows)
    widths = [w for w in (512, 768) if w < group_rows] + [group_rows]
    least = 0
    for w in widths:
        fits = (span > least) & (span <= w) if w < group_rows else span > least

        @pl.when(fits)
        def _(w=w):
            act(pl.multiple_of(jnp.minimum(low, group_rows - w), 128), w)

        least = w


def one_row(tile):
    return jnp.concatenate([tile[j : j + 1, :] for j in range(tile.shape[0])], axis=1)


def real_row(ids, mask):
    row = one_row(mask[...].astype(f32))
    lane = lax.broadcasted_iota(i32, row.shape, 1)
    return jnp.where(ids[0] * row.shape[1] + lane < group_ends(ids)[-1], row, 0.0)


def project_kernel(
    ids, x_hbm, w_hbm, bias_hbm, mask_hbm, b_in_hbm, q_ref, k_ref, v_ref, message, x_ref, w_ref, bias_ref, mask_ref,
    b_in_ref, sems,
):
    group_rows, width = q_ref.shape
    chunks = 4
    share = group_rows // chunks
    pairs = [(w_hbm, w_ref), (bias_hbm, bias_ref)]
    for c in range(chunks):
        rows = pl.ds(c * share, share)
        pairs.append((x_hbm.at[rows, :], x_ref.at[rows, :]))
    pairs += [(mask_hbm, mask_ref), (b_in_hbm, b_in_ref)]
    copies = [pltpu.make_async_copy(source, target, sems.at[j]) for j, (source, target) in enumerate(pairs)]
    for copy in copies:
        copy.start()
    copies[0].wait()
    copies[1].wait()
    bias = bias_ref[...].astype(f32)
    for c in range(chunks):
        rows = slice(c * share, (c + 1) * share)
        copies[2 + c].wait()
        x = x_ref[rows, :]
        k_ref[rows, :] = mm_nt(x, w_ref[width : 2 * width, :]).astype(bf16)
        v_ref[rows, :] = (mm_nt(x, w_ref[2 * width :, :]) + bias[1:2]).astype(bf16)
        q = (mm_nt(x, w_ref[:width, :]) + bias[0:1]).astype(bf16)
        q_ref[rows, :] = (q.astype(f32) * HEAD_DIM ** (-0.5)).astype(bf16)
    for copy in copies[2 + chunks :]:
        copy.wait()
    message[0:1, :] = one_row(b_in_ref[...].astype(f32))
    total = jnp.sum(real_row(ids, mask_ref), axis=-1, keepdims=True)
    message[1:, :] = jnp.broadcast_to(total, (message.shape[0] - 1, message.shape[1]))


def project(ids, x, w_t, b_qv, mask, b_in):
    group_rows, model = x.shape
    width = w_t.shape[0] // 3
    streamed = [x, w_t, b_qv, mask.reshape(-1, 128), b_in.reshape(-1, 128)]
    return run(
        project_kernel,
        (ids,),
        [],
        [((group_rows, width), bf16)] * 3 + [((8, model), f32)],
        streamed=streamed,
        scratch=[pltpu.VMEM(a.shape, a.dtype) for a in streamed] + [pltpu.SemaphoreType.DMA((8,))],
        micros=3.0,
    )


def attend_kernel(first, ids, q_ref, k_ref, v_ref, *refs):
    context_ref, e_ref, rl_ref = refs
    rows = rl_ref.shape[0] // 2
    group_rows, width = k_ref.shape
    heads = width // HEAD_DIM
    ends = group_ends(ids)

    def one(t, carry):
        start = pl.multiple_of(ids[2 + first + t] * rows, rows)
        at = pl.multiple_of(t * rows, rows)

        def act(key0, w):
            q = q_ref[pl.ds(start, rows), :].astype(f32)
            seg_q = segment_of(start + lax.broadcasted_iota(i32, (rows, 1), 0), ends)
            seg_k = segment_of(key0 + lax.broadcasted_iota(i32, (1, w), 1), ends)
            k = k_ref[pl.ds(key0, w), :]
            v = v_ref[pl.ds(key0, w), :]
            context = jnp.zeros((rows, width), f32)
            wide = jnp.zeros((rows, width), f32)
            for h in range(heads):
                mask = head_mask(width, h)
                scores = mm_nt(jnp.where(mask, q, 0.0).astype(bf16), k)
                scores = jnp.where(seg_q == seg_k, scores, NEG)
                e = jnp.exp(scores - jnp.max(scores, axis=-1, keepdims=True))
                inverse = 1.0 / jnp.sum(e, axis=-1, keepdims=True)
                low = e.astype(bf16)
                e_ref[pl.ds(pl.multiple_of((t * heads + h) * rows, rows), rows), :w] = low
                context = jnp.where(mask, mm(low, v) * inverse, context)
                wide = jnp.where(mask, inverse, wide)
            rl_ref[pl.ds(at, rows), :] = wide
            context_ref[pl.ds(at, rows), :] = context.astype(bf16)

        by_window(rows, start, ends, group_rows, act)
        return carry

    lax.fori_loop(0, 2, one, 0)


def attend(first, ids, q, k, v, share):
    group_rows, width = k.shape
    heads = width // HEAD_DIM
    return run(
        functools.partial(attend_kernel, first),
        (ids,),
        [q, k, v],
        [
            ((2 * share, width), bf16),
            ((2 * heads * share, group_rows), bf16),
            ((2 * share, width), f32),
        ],
        vmem=20,
        micros=3.0,
    )


def attend_back_kernel(spots, first, last, ids, *refs):
    count = len(spots)
    grads, refs = refs[:count], refs[count:]
    contexts, es, rls, refs = refs[0:2], refs[2:4], refs[4:6], refs[6:]
    q_ref, k_ref, v_ref, refs = refs[0], refs[1], refs[2], refs[3:]
    if not first:
        before, refs = refs[:3], refs[3:]
    if last:
        w_ref, far_out, near_out, gq, gk, gv = refs
    else:
        gq, gk, gv = refs
    rows = grads[0].shape[0]
    group_rows, width = k_ref.shape
    heads = width // HEAD_DIM
    ends = group_ends(ids)
    if first:
        gk[...] = jnp.zeros_like(gk)
        gv[...] = jnp.zeros_like(gv)
    else:
        gq[...] = before[0][...]
        gk[...] = before[1][...]
        gv[...] = before[2][...]
    for g_ref, spot in zip(grads, spots):
        start = pl.multiple_of(ids[2 + spot] * rows, rows)
        part, t = spot // 2, spot % 2
        g = g_ref[...].astype(f32) * rls[part][t * rows : (t + 1) * rows, :]
        dots = g * contexts[part][t * rows : (t + 1) * rows, :].astype(f32)
        q = q_ref[pl.ds(start, rows), :].astype(f32)

        def act(key0, w, g=g, dots=dots, q=q, part=part, t=t, start=start):
            keys = pl.ds(key0, w)
            k = k_ref[keys, :]
            v = v_ref[keys, :]
            out = jnp.zeros((rows, width), f32)
            add_k = jnp.zeros((w, width), f32)
            add_v = jnp.zeros((w, width), f32)
            for h in range(heads):
                mask = head_mask(width, h)
                g_head = jnp.where(mask, g, 0.0).astype(bf16)
                e = es[part][(t * heads + h) * rows : (t * heads + h + 1) * rows, :w]
                delta = jnp.sum(jnp.where(mask, dots, 0.0), axis=-1, keepdims=True)
                ds = (e.astype(f32) * (mm_nt(g_head, v) - delta)).astype(bf16)
                out = jnp.where(mask, mm(ds, k), out)
                add_k = add_k + mm_tn(ds, jnp.where(mask, q, 0.0).astype(bf16))
                add_v = add_v + mm_tn(e, g_head)
            gk[keys, :] += add_k
            gv[keys, :] += add_v
            gq[pl.ds(start, rows), :] = (out * HEAD_DIM ** (-0.5)).astype(bf16)

        by_window(rows, start, ends, group_rows, act)
    if last:
        for out, pair in ((far_out, (2, 3)), (near_out, (0, 1))):
            for t, spot in enumerate(pair):
                own = pl.ds(pl.multiple_of(ids[2 + spot] * rows, rows), rows)
                part = (
                    mm(gq[own, :], w_ref[:width, :])
                    + mm(gk[own, :].astype(bf16), w_ref[width : 2 * width, :])
                    + mm(gv[own, :].astype(bf16), w_ref[2 * width :, :])
                )
                out[t * rows : (t + 1) * rows, :] = part.astype(out.dtype)


def attend_back(spots, ids, grads, contexts, es, rls, qkv, before, w_t, share):
    group_rows, width = qkv[0].shape
    last = w_t is not None
    sums = [((group_rows, width), bf16), ((group_rows, width), f32), ((group_rows, width), f32)]
    inputs = [*grads, *contexts, *es, *rls, *qkv, *before]
    if last:
        model = w_t.shape[1]
        outputs = [((2 * share, model), bf16), ((2 * share, model), f32)]
        scratch = [pltpu.VMEM(*o) for o in sums]
        inputs.append(w_t)
    else:
        outputs, scratch = sums, []
    return run(
        functools.partial(attend_back_kernel, spots, not before, last),
        (ids,),
        inputs,
        outputs,
        scratch=scratch,
        vmem=20,
        micros=5.0 if last else 0.1,
    )


def early_kernel(ids, c0, c1, c3, o0, o1, o3, *refs):
    mask_hbm, *vectors = refs[:10]
    out, vecs, weight, mask_ref, *tiles, sems = refs[10:]
    pairs = [(mask_hbm, mask_ref), *zip(vectors, tiles)]
    copies = [pltpu.make_async_copy(source, target, sems.at[j]) for j, (source, target) in enumerate(pairs)]
    for copy in copies:
        copy.start()
    share = out.shape[0] // 2
    attn = mm(c0[...], o0[...]) + mm(c1[...], o1[...])
    for t in range(2):
        rows = slice(t * share, (t + 1) * share)
        out[rows, :] = attn[rows] + mm(c3[(1 - t) * share : (2 - t) * share, :], o3[...])
    for copy in copies:
        copy.wait()
    for j, tile in enumerate(tiles):
        vecs[j : j + 1, :] = one_row(tile[...].astype(f32))
    vecs[9:, :] = jnp.zeros((vecs.shape[0] - 9, vecs.shape[1]), f32)
    row = real_row(ids, mask_ref)
    here = lax.broadcasted_iota(i32, (share, share), 0) == lax.broadcasted_iota(i32, (share, share), 1)
    weight[...] = jnp.sum(jnp.where(here, jnp.broadcast_to(row, (share, share)), 0.0), axis=-1, keepdims=True)


def early_part(ids, arrays, mask, vectors, share):
    model = arrays[3].shape[1]
    streamed = [mask.reshape(-1, 128), *[v.reshape(-1, 128) for v in vectors]]
    return run(
        early_kernel,
        (ids,),
        arrays,
        [((2 * share, model), f32), ((16, model), f32), ((share, 1), f32)],
        streamed=streamed,
        scratch=[pltpu.VMEM(a.shape, a.dtype) for a in streamed] + [pltpu.SemaphoreType.DMA((len(streamed),))],
    )


def adapter_constants(down_bias, wq, wk, query_key, member_ref, spread_ref, bias_ref):
    query_key[...] = mm_nt(wq[...], wk[...]).astype(bf16)
    flat = member_ref.shape[0]
    lane = lax.broadcasted_iota(i32, (flat, ADAPTERS), 0) - BOTTLENECK * lax.broadcasted_iota(
        i32, (flat, ADAPTERS), 1
    )
    member_ref[...] = ((lane >= 0) & (lane < BOTTLENECK)).astype(f32).astype(bf16)
    lane = lax.broadcasted_iota(i32, (ADAPTERS, flat), 1) - BOTTLENECK * lax.broadcasted_iota(
        i32, (ADAPTERS, flat), 0
    )
    spread = ((lane >= 0) & (lane < BOTTLENECK)).astype(f32)
    spread_ref[...] = spread.astype(bf16)
    cycle = lax.broadcasted_iota(i32, (BOTTLENECK, flat), 1) - lax.broadcasted_iota(i32, (BOTTLENECK, flat), 0)
    repeat = jnp.zeros(cycle.shape, f32)
    for a in range(ADAPTERS):
        repeat = repeat + (cycle == a * BOTTLENECK).astype(f32)
    bias_row = jnp.sum(mm(down_bias[...], repeat.astype(bf16)) * spread, axis=0, keepdims=True)
    bias_ref[...] = jnp.broadcast_to(bias_row, bias_ref.shape)


def forward_kernel(own, ids, early, c2, x_ref, o2, vecs, message, in0, in1, back0, back1, *rest):
    if own:
        inner_ref, down_bias, wq, wk, part_ref, slope, slope_two, first_ref, normed_ref, factor_ref, *constants = rest
    else:
        count, part_ref, inner_ref = rest
        write_small(part_ref, jnp.broadcast_to(count[0:1, 0:1], (8, x_ref.shape[1])))
    share = early.shape[0] // 2
    t = 0 if own else 1
    attn = early[t * share : (t + 1) * share, :] + mm(c2[(1 - t) * share : (2 - t) * share, :], o2[...])
    vec = vecs[...].astype(f32)
    start = pl.multiple_of(ids[2 if own else 3] * share, share)
    normed, factor = norm_parts(attn + vec[0:1] + x_ref[pl.ds(start, share), :].astype(f32))
    first = normed * vec[1:2] + vec[2:3]
    low = first.astype(bf16)
    part = jnp.zeros(first.shape, f32)
    units = in0.shape[1]
    chunk = units
    for j, (w_in, bias, w_back) in enumerate(((in0, vec[8:9], back0), (in1, message[0:1, :], back1))):
        for at in range(0, units, chunk):
            here = slice(at, at + chunk)
            columns = slice(j * units + at, j * units + at + chunk)
            inner = mm(low, w_in[:, here]) + bias[:, here]
            if own:
                act, bend = gelu_both(inner)
                slope[:, columns] = bend.astype(bf16)
                slope_two[:, columns] = gelu_both(inner_ref[:, columns])[1].astype(bf16)
            else:
                act = 0.5 * inner * (1.0 + lax.erf(inner * ROOT_HALF))
                inner_ref[:, columns] = inner
            part = part + mm(act.astype(bf16), w_back[here, :])
    part_ref[:share, :] = part.astype(part_ref.dtype)
    if own:
        first_ref[...] = first
        normed_ref[...] = normed
        factor_ref[...] = jnp.broadcast_to(factor, factor_ref.shape)
        adapter_constants(down_bias, wq, wk, *constants)


def forward_rows(own, ids, early, c2, x, o2, vecs, message, w_ins, w_backs, share, *more):
    model = x.shape[1]
    units = w_ins[0].shape[1]
    slope = ((share, 2 * units), bf16)
    flat = ADAPTERS * BOTTLENECK
    if own:
        outputs = [((share, model), f32), slope, slope] + [((share, model), f32)] * 2 + [((share, 128), f32)]
        outputs += [((model, model), bf16), ((flat, ADAPTERS), bf16), ((ADAPTERS, flat), bf16), ((8, flat), f32)]
    else:
        outputs = [((share + 16, model), bf16), ((share, 2 * units), f32)]
    return run(
        functools.partial(forward_kernel, own),
        (ids,),
        [early, c2, x, o2, vecs, message, *w_ins, *w_backs, *more],
        outputs,
        vmem=16,
        micros=3.0,
    )


def backward_kernel(gp, slope, back0, back1, in0, in1, part_ref):
    grad = gp[...]
    units = in0.shape[1]
    part = jnp.zeros(grad.shape, f32)
    for j, (w_back, w_in) in enumerate(((back0, in0), (back1, in1))):
        bend = slope[:, j * units : (j + 1) * units].astype(f32)
        inner = (bend * mm_nt(grad, w_back[...])).astype(bf16)
        part = part + mm_nt(inner, w_in[...])
    part_ref[...] = part.astype(part_ref.dtype)


def backward_rows(grad, slope, w_backs, w_ins, dtype):
    share, model = grad.shape
    units = w_ins[0].shape[1]
    return run(
        backward_kernel,
        (),
        [grad, slope, *w_backs, *w_ins],
        [((share, model), dtype)],
    )


def first_norm_kernel(own, got, gpre2, normed, factor, vecs, o0, o1, o2, o3, gpre1, c0, c1, c2, c3):
    grad = own[...] + got[...].astype(f32) + gpre2[...]
    grad = norm_back(grad, normed[...], factor[:, 0:1], vecs[...].astype(f32)[1:2])
    gpre1[...] = grad
    low = grad.astype(bf16)
    for c, o in ((c2, o2), (c3, o3), (c1, o1), (c0, o0)):
        c[...] = mm_nt(low, o[...]).astype(bf16)


def first_norm_back(own, got, gpre2, normed, factor, vecs, outs):
    share, model = own.shape
    width = outs[0].shape[0]
    return run(
        first_norm_kernel,
        (),
        [own, got, gpre2, normed, factor, vecs, *outs],
        [((share, model), f32)] + [((share, width), bf16)] * 4,
    )


def adapter_kernel(
    slots, ids, own, got, first_ref, cot, weight, count, vecs, member_ref, spread_ref, bias_ref, up_bias, down, up,
    wq, wk, wv,
    out_hbm, keep, give, sums, turn_ref, reduced_ref, mix_ref, base_ref, normed_ref, factor_ref, layer_out, lefts, sem,
):
    flat, model = up.shape
    vec = vecs[...].astype(f32)
    member = member_ref[...]
    spread = spread_ref[...]
    inv_root = model ** (-0.5)
    scale = 0.5 * slots / jnp.maximum(count[0:1, 0:1] + read_small(got)[0:1, 0:1], 1.0)

    normed_two, factor_two = norm_parts(own[...] + got[: own.shape[0], :].astype(f32) + vec[3:4] + first_ref[...])
    normed_ref[...] = normed_two
    factor_ref[...] = jnp.broadcast_to(factor_two, factor_ref.shape)
    second = normed_two * vec[4:5] + vec[5:6]
    second_low = second.astype(bf16)
    query_key = mm_nt(mm(second_low, wq[...]).astype(bf16), wk[...]) * inv_root
    query_key_low = query_key.astype(bf16)
    lift_key = mm_nt(query_key_low, up[...])
    reduced = mm_nt(second_low, down[...]) + bias_ref[0:1, :]
    reduced_ref[...] = reduced
    squeezed = 0.5 * reduced * (1.0 + lax.erf(reduced * ROOT_HALF))
    squeezed = squeezed.astype(bf16).astype(f32)
    logits = (
        mm((squeezed * lift_key).astype(bf16), member)
        + mm_nt(query_key_low, up_bias[...])
        + jnp.sum(query_key * second, axis=-1, keepdims=True)
    )
    shifted = logits - jnp.max(logits, axis=-1, keepdims=True)
    log_probs = shifted - jnp.log(jnp.sum(jnp.exp(shifted), axis=-1, keepdims=True))
    joining = jnp.exp(log_probs)
    entropy = -jnp.sum(joining * log_probs, axis=-1, keepdims=True)
    total = jnp.sum(joining, axis=-1, keepdims=True)
    joining_low = joining.astype(bf16)
    joining_wide = mm(joining_low, spread)
    joined_low = (joining_wide * squeezed).astype(bf16)
    mixed = total * second + mm(joined_low, up[...]) + mm(joining_low, up_bias[...])
    mixed_low = mixed.astype(bf16)
    normed_join, factor_join = norm_parts(second + mm(mixed_low, wv[...]))
    grad_out = cot[...].astype(f32)
    grad_pref = norm_back(grad_out, normed_join, factor_join, vec[6:7])
    grad_pref_low = grad_pref.astype(bf16)
    back_value = mm_nt(grad_pref_low, wv[...])
    back_value_low = back_value.astype(bf16)
    lift_value = mm_nt(back_value_low, up[...])
    grad_probs = (
        mm((squeezed * lift_value).astype(bf16), member)
        + mm_nt(back_value_low, up_bias[...])
        + jnp.sum(back_value * second, axis=-1, keepdims=True)
    )
    mean_grad = jnp.sum(joining * grad_probs, axis=-1, keepdims=True)
    grad_logits = joining * (grad_probs - mean_grad) - scale * weight[...] * joining * (log_probs + entropy)
    logits_low = grad_logits.astype(bf16)
    grad_wide = mm(logits_low, spread)
    logit_sum = jnp.sum(grad_logits, axis=-1, keepdims=True)
    turned = (
        logit_sum * second + mm((grad_wide * squeezed).astype(bf16), up[...]) + mm(logits_low, up_bias[...])
    ) * inv_root
    turned_low = turned.astype(bf16)
    turn_ref[...] = turned_low

    layer_out[...] = normed_join * vec[6:7] + vec[7:8]
    copy = pltpu.make_async_copy(layer_out, out_hbm, sem)
    copy.start()
    small = jnp.concatenate(
        [
            jnp.sum(grad_out * normed_join, axis=0, keepdims=True),
            jnp.sum(grad_out, axis=0, keepdims=True),
            jnp.zeros((sums.shape[0] - 2, model), f32),
        ],
        axis=0,
    )
    sums[...] = small
    write_small(give, small)
    mix_ref[...] = grad_wide * lift_key + joining_wide * lift_value
    base_ref[...] = grad_pref + logit_sum * query_key + total * back_value

    half = model // 2
    lefts[0] = second_low
    lefts[1] = mixed_low
    for j, right in enumerate((turned_low, grad_pref_low)):
        rows = slice(j * half, (j + 1) * half)
        other = lefts[j, :, pl.ds(pl.multiple_of((1 - ids[6]) * half, 128), half)]
        give[rows, :] = mm_tn(other, right).astype(bf16)
        mine = lefts[j, :, pl.ds(pl.multiple_of(ids[6] * half, 128), half)]
        keep[rows, :] = mm_tn(mine, right).astype(bf16)
    copy.wait()


def adapters(slots, ids, arrays):
    share, model = arrays[0].shape
    flat = ADAPTERS * BOTTLENECK
    wide, flat_wide = ((share, model), f32), ((share, flat), f32)
    return run(
        functools.partial(adapter_kernel, slots),
        (ids,),
        arrays,
        [
            ((share, model), f32, None),
            ((model, model), bf16),
            ((model + 16, model), bf16),
            ((8, model), f32),
            ((share, model), bf16),
            flat_wide,
            flat_wide,
            wide,
            wide,
            ((share, 128), f32),
        ],
        scratch=[
            pltpu.VMEM((share, model), f32),
            pltpu.VMEM((2, share, model), bf16),
            pltpu.SemaphoreType.DMA,
        ],
        vmem=20,
        micros=8.0,
    )


def adapter_rest_kernel(turn, reduced, mix, base, normed, factor, vecs, down, wqk, gpre2_ref, gpre2_low):
    grad_reduced = (gelu_both(reduced[...])[1] * mix[...]).astype(bf16)
    grad_second = base[...] + mm(grad_reduced, down[...]) + mm_nt(turn[...], wqk[...])
    grad_pre2 = norm_back(grad_second, normed[...], factor[:, 0:1], vecs[4:5, :])
    gpre2_ref[...] = grad_pre2
    gpre2_low[...] = grad_pre2.astype(bf16)


def write_small(message, sums):
    high, low = halves_of(sums)
    rows = message.shape[0] - 16
    message[rows:, :] = jnp.concatenate([high, low], axis=0)


def read_small(message):
    rows = message.shape[0] - 16
    both = message[rows:, :].astype(f32)
    return both[:8] + both[8:]


def fold_kernel(base, start, split, last, ids, *refs):
    if start:
        keep, got, sums, *outs = refs
        rows = keep.shape[0] // 2
        pieces = [(keep, got, j * rows) for j in range(2)]
    else:
        *arrays, sums = refs[:5]
        outs = refs[5:]
        rows = arrays[0].shape[0]
        pieces = [(arrays[2 * j], arrays[2 * j + 1], 0) for j in range(2)]
        got = arrays[3]
    total = sums[...] + read_small(got)
    outs[-1][...] = total
    for j, (mine, other, at) in enumerate(pieces):
        def both(where):
            return (mine[where, :].astype(f32) + other[where, :].astype(f32)).astype(bf16)

        if split:
            half = rows // 2
            bit = ids[base + j]
            outs[2 * j][...] = both(pl.ds(pl.multiple_of(at + bit * half, 16), half))
            outs[2 * j + 1][:half, :] = both(pl.ds(pl.multiple_of(at + (1 - bit) * half, 16), half))
        elif last:
            outs[j][...] = both(pl.ds(at, rows))
        else:
            whole = both(pl.ds(at, rows))
            outs[2 * j][...] = whole
            outs[2 * j + 1][:rows, :] = whole
    if not last:
        write_small(outs[3], total)


def fold(ids, base, start, split, arrays, rows, sums, last=False):
    model = sums.shape[1]
    rows = rows // 2 if split else rows
    outputs = []
    for j in range(2):
        outputs += [((rows, model), bf16)] + ([] if last else [((rows + 16 * j, model), bf16)])
    outputs.append((sums.shape, f32))
    outs = run(functools.partial(fold_kernel, base, start, split, last), (ids,), [*arrays, sums], outputs)
    if last:
        return outs[:2], None, outs[2]
    return outs[0:4:2], outs[1:4:2], outs[4]


def join_kernel(base, ids, *refs):
    outs = refs[4:]
    for j in range(2):
        mine, got = refs[2 * j : 2 * j + 2]
        rows = mine.shape[0]
        bit = ids[base + j]
        outs[j][pl.ds(pl.multiple_of(bit * rows, 16), rows), :] = mine[...]
        outs[j][pl.ds(pl.multiple_of((1 - bit) * rows, 16), rows), :] = got[...]


def join(ids, base, mine, gots):
    rows, model = mine[0].shape
    arrays = [a for pair in zip(mine, gots) for a in pair]
    return run(functools.partial(join_kernel, base), (ids,), arrays, [((2 * rows, model), bf16)] * 2)


def finish_kernel(other, far, at, first, last, ids, mixed_ref, value_ref, wq, wk, *refs):
    rows = mixed_ref.shape[0]
    if first:
        out_q, out_v, key_ref, stage, sems = refs
    elif last:
        key_before, _, _, out_q, out_v, out_k, stage, key_ref, sems = refs
    else:
        key_before, _, _, out_q, out_v, key_ref, stage, sems = refs
    core = 1 - ids[6] if other else ids[6]
    spots = []
    for j in range(2):
        bit = 1 - ids[at + j] if far else ids[at + j]
        spots.append(pl.ds(pl.multiple_of((2 * core + bit) * rows, rows), rows))
    copies = []

    def send(j, source, target):
        copies.append(pltpu.make_async_copy(source, target, sems.at[j]))
        copies[-1].start()

    mixed = mixed_ref[...]
    key = mm_tn(mixed, wq[spots[0], :])
    key_ref[...] = key if first else key_before[...] + key
    if last:
        send(2, key_ref, out_k)
    stage[0] = mm(mixed, wk[...])
    send(0, stage.at[0], out_q.at[spots[0], :])
    stage[1] = value_ref[...].astype(f32)
    send(1, stage.at[1], out_v.at[spots[1], :])
    for copy in copies:
        copy.wait()


def finish(ids, at, other, far, pair, wq, wk, before, last=False):
    rows, model = pair[0].shape
    first = before is None
    vmem_spec = pl.BlockSpec(memory_space=pltpu.VMEM)
    any_spec = pl.BlockSpec(memory_space=pl.ANY)
    whole = jax.ShapeDtypeStruct((model, model), f32)
    key = whole if last else pltpu.VMEM((model, model), f32)
    inputs = [*pair, wq, wk] + ([] if first else [before[2]])
    call = pl.pallas_call(
        functools.partial(finish_kernel, other, far, at, first, last),
        in_specs=[pl.BlockSpec(memory_space=pltpu.SMEM)]
        + [vmem_spec] * len(inputs)
        + ([] if first else [any_spec] * 2),
        out_specs=[any_spec] * 2 + [any_spec if last else vmem_spec],
        out_shape=[whole, whole, key],
        input_output_aliases={} if first else {6: 0, 7: 1},
        scratch_shapes=[pltpu.VMEM((2, rows, model), f32)]
        + ([pltpu.VMEM((model, model), f32)] if last else [])
        + [pltpu.SemaphoreType.DMA((3,))],
        compiler_params=pltpu.CompilerParams(vmem_limit_bytes=16 * 1024 * 1024),
        cost_estimate=pl.CostEstimate(flops=int(0.1 * FLOPS), bytes_accessed=1, transcendentals=0),
    )
    return list(
        call(ids, *[pltpu.with_memory_space_constraint(a, pltpu.VMEM) for a in inputs], *([] if first else before[:2]))
    )


def chip_kernel(near, got, gpre1, keep, give):
    share = keep.shape[0]
    give[...] = (near[share:, :] + got[share:, :].astype(f32)).astype(bf16)
    keep[...] = near[:share, :] + got[:share, :].astype(f32) + gpre1[...]


def body(
    layer_input,
    cotangent,
    seq_lens,
    seq_place,
    loss_mask,
    w_qkv,
    b_qv,
    w_out,
    b_out,
    ln1_gain,
    ln1_bias,
    w_in,
    b_in,
    w_back,
    b_back,
    ln2_gain,
    ln2_bias,
    ad_down,
    ad_down_bias,
    ad_up,
    ad_up_bias,
    join_query,
    join_key,
    join_value,
    join_gain,
    join_bias,
):
    group_rows, model = layer_input.shape
    share = cotangent.shape[0]
    rank = lax.axis_index("tp")
    dp_rank = lax.axis_index("dp")
    total_slots = group_rows * lax.axis_size("dp")

    core, near_x = ("tp", 1), ("tp", 2)
    others = []
    bit = 1
    while bit < lax.axis_size("dp"):
        others.append(("dp", bit))
        bit *= 2
    streams = [
        [others[0], *others[1:], near_x],
        [*others[1:2], others[0], near_x, *others[2:]],
    ]

    def bit_of(axis, which):
        return (lax.axis_index(axis) // which) % 2

    ids = [rank, dp_rank] + [rank ^ j for j in ORDER] + [bit_of(*core)]
    for at in range(len(others) + 1):
        ids += [bit_of(*stream[at]) for stream in streams]
    ids = jnp.stack(ids).astype(i32)
    ids = jnp.concatenate([ids, jnp.zeros(HEADER - ids.shape[0], i32), seq_lens, seq_place])
    vectors = [b_out, ln1_gain, ln1_bias, b_back, ln2_gain, ln2_bias, join_gain, join_bias, b_in]

    outs = [w_out, swap(w_out, "tp", 1), swap(w_out, "tp", 2)]
    outs.append(None)
    w_ins = [w_in, swap(w_in, "tp", 1)]
    w_backs = [w_back, swap(w_back, "tp", 1)]

    width = w_qkv.shape[2]
    w_t = jnp.transpose(w_qkv, (1, 2, 0)).reshape(3 * width, model)
    q, k, v, message = project(ids, layer_input, w_t, b_qv, loss_mask, b_in)
    message_got = swap(message, *core)
    far, e_far, rl_far = attend(2, ids, q, k, v, share)
    far, message_got, outs[1], outs[2], w_ins[1], w_backs[1] = tie(
        far, message_got, *outs[1:3], w_ins[1], w_backs[1]
    )
    outs[3] = swap(outs[2], "tp", 1)
    c1, c3 = swap(far, "tp", 1), swap(far, "tp", 3)
    counted = message[1:2, :128] + message_got[1:2, :128]
    count_got = swap(counted, *others[0])
    near, e_near, rl_near = attend(0, ids, q, k, v, share)
    c2 = swap(near, *near_x)
    near, count_got, outs[3], c1 = tie(near, count_got, outs[3], c1)
    counted = counted + count_got
    pair = [bit for _, bit in others[1:3]]
    count_gots = [swap(counted, "dp", bit) for bit in [*pair, *([sum(pair)] if len(pair) == 2 else [])]]
    early, vecs, weight_m = early_part(
        ids, [near, c1, c3, outs[0], outs[1], outs[3]], loss_mask, vectors, share
    )
    counted = sum(count_gots, counted)
    for axis, which in others[3:]:
        counted = counted + swap(counted, axis, which)
    early, counted = tie(early, counted)

    give, inner = forward_rows(
        False, ids, early, c2, layer_input, outs[2], vecs, message_got, w_ins, w_backs, share, counted
    )
    ffn_got = swap(give, *near_x)
    own, slope_one, slope_two, first, normed_one, factor_one, *constants = forward_rows(
        True, ids, early, c2, layer_input, outs[2], vecs, message_got, w_ins, w_backs, share, inner,
        ad_down_bias, join_query, join_key,
    )

    flat = ADAPTERS * BOTTLENECK
    down_t = jnp.transpose(ad_down, (1, 2, 0)).reshape(flat, model)
    up = ad_up.reshape(flat, model)
    layer_out, keep, give, sums, turn, reduced, mix, base, normed_two, factor_two = adapters(
        total_slots,
        ids,
        [
            own, ffn_got, first, cotangent, weight_m, counted, vecs, *constants[1:], ad_up_bias, down_t, up,
            join_query, join_key, join_value,
        ],
    )
    got = swap(give, *core)
    gpre2, gpre2_low = run(
        adapter_rest_kernel,
        (),
        [turn, reduced, mix, base, normed_two, factor_two, vecs, down_t, constants[0]],
        [((share, model), f32), ((share, model), bf16)],
    )
    gpre2_got = swap(gpre2_low, "tp", 2)

    state = {"at": 0, "history": [], "rows": keep.shape[0] // 2}

    def sum_step(keeps, gots, sums):
        at = state["at"]
        start = at == 0
        split = state["rows"] // 2 >= LEAST_ROWS
        arrays = [keeps, gots] if start else [a for pair in zip(keeps, gots) for a in pair]
        keeps, gives, sums = fold(ids, 7 + 2 * at, start, split, arrays, state["rows"], sums)
        if split:
            state["rows"] //= 2
            state["history"].append(at)
        state["at"] = at + 1
        return keeps, [swap(g, *stream[at]) for g, stream in zip(gives, streams)], sums

    (back_own,) = backward_rows(gpre2_low, slope_one, w_backs, w_ins, f32)
    back_own, got = tie(back_own, got)
    keeps, gots, sums = sum_step(keep, got, sums)
    keeps[0], gpre2_got = tie(keeps[0], gpre2_got)
    (back_give,) = backward_rows(gpre2_got, slope_two, w_backs, w_ins, bf16)
    back_give, *gots = tie(back_give, *gots)
    keeps, gots, sums = sum_step(keeps, gots, sums)
    keeps[0], back_give = tie(keeps[0], back_give)
    back_got = swap(back_give, "tp", 2)
    keeps, gots, sums = sum_step(keeps, gots, sums)
    keeps[0], back_got = tie(keeps[0], back_got)
    gpre1, c0, c1, c2, c3 = first_norm_back(back_own, back_got, gpre2, normed_one, factor_one, vecs, outs)
    c2, c3, c1 = swap(c2, "tp", 2), swap(c3, "tp", 3), swap(c1, "tp", 1)
    shared = ((near, far), (e_near, e_far), (rl_near, rl_far), (q, k, v))
    before = list(attend_back((0,), ids, (c0,), *shared, [], None, share))
    before[0], *gots = tie(before[0], *gots)
    keeps, gots, sums = sum_step(keeps, gots, sums)
    before[0], keeps[0] = tie(before[0], keeps[0])
    far_part, near_part = attend_back((2, 1, 3), ids, (c1, c2, c3), *shared, before, w_t, share)
    far_part, *gots = tie(far_part, *gots)
    far_got = swap(far_part, "tp", 1)
    while state["at"] < len(others) + 1:
        keeps, gots, sums = sum_step(keeps, gots, sums)
    arrays = [a for pair in zip(keeps, gots) for a in pair]
    keeps, _, sums = fold(ids, 0, False, False, arrays, state["rows"], sums, last=True)
    gain_grad, bias_grad = sums[0], sums[1]
    part_own, part_give = run(
        chip_kernel, (), [near_part, far_got, gpre1], [((share, model), f32), ((share, model), bf16)]
    )
    part_got = swap(part_give, "tp", 2)
    for at in reversed(state["history"][1:]):
        gots = [swap(a, *stream[at]) for a, stream in zip(keeps, streams)]
        gots[0], part_own, gain_grad, bias_grad = tie(gots[0], part_own, gain_grad, bias_grad)
        keeps = join(ids, 7 + 2 * at, keeps, gots)
    gots = [swap(a, *stream[0]) for a, stream in zip(keeps, streams)]
    over = [swap(a, *core) for a in keeps]
    part = finish(ids, 7, False, False, keeps, join_query, join_key, None)
    part = finish(ids, 7, True, False, over, join_query, join_key, part)
    part[2], *gots = tie(part[2], *gots)
    over = [swap(a, *core) for a in gots]
    input_grad = part_own + part_got.astype(f32)
    part = finish(ids, 7, False, True, gots, join_query, join_key, part)
    query_grad, value_grad, key_grad = finish(ids, 7, True, True, over, join_query, join_key, part, last=True)
    return (layer_out, input_grad, query_grad, key_grad, value_grad, gain_grad, bias_grad)


def solution(mesh):
    placed = (
        P("dp", None),
        P(("dp", "tp"), None),
        P(),
        P(),
        P(("dp", "tp")),
        P(None, None, "tp"),
        P(None, "tp"),
        P("tp", None),
        P(),
        P(),
        P(),
        P(None, "tp"),
        P("tp"),
        P("tp", None),
        P(),
        P(),
        P(),
        P(),
        P(),
        P(),
        P(),
        P(),
        P(),
        P(),
        P(),
        P(),
    )
    return jax.shard_map(
        body,
        mesh=mesh,
        in_specs=placed,
        out_specs=(P(("dp", "tp"), None), P(("dp", "tp"), None), P(), P(), P(), P(), P()),
        check_vma=False,
    )
```

```python
import functools

import jax
import jax.numpy as jnp
from jax import lax
from jax.experimental import pallas as pl
from jax.experimental.pallas import tpu as pltpu
from jax.sharding import PartitionSpec as P

HEAD_DIM = 64
ADAPTERS = 16
BOTTLENECK = 48
SEQ_GRP = 4
LEAST_ROWS = 96
FLOPS = 1.15e9

EPS = 1e-06
NEG = -1e30
ROOT_HALF = 0.7071067811865476
INV_ROOT_TAU = 0.3989422804014327

f32 = jnp.float32
bf16 = jnp.bfloat16
i32 = jnp.int32

HEADER = 64

ORDER = (0, 2, 1, 3)


def gelu_both(values):
    phi = 0.5 * (1.0 + lax.erf(values * ROOT_HALF))
    return values * phi, phi + values * jnp.exp(-0.5 * values * values) * INV_ROOT_TAU


def row_mean(values):
    return jnp.sum(values, axis=-1, keepdims=True) * (1.0 / values.shape[-1])


def norm_parts(values):
    center = values - row_mean(values)
    factor = lax.rsqrt(row_mean(center * center) + EPS)
    return center * factor, factor


def norm_back(gradient, normed, factor, gain_vec):
    scaled = gradient * gain_vec
    return factor * (scaled - row_mean(scaled) - normed * row_mean(scaled * normed))


def mm(a, b):
    return lax.dot_general(a, b, (((1,), (0,)), ((), ())), preferred_element_type=f32)


def mm_nt(a, b):
    return lax.dot_general(a, b, (((1,), (1,)), ((), ())), preferred_element_type=f32)


def mm_tn(a, b):
    return lax.dot_general(a, b, (((0,), (0,)), ((), ())), preferred_element_type=f32)


def halves_of(a):
    high = a.astype(bf16)
    return high, (a - high.astype(f32)).astype(bf16)


def swap(value, axis, bit):
    size = lax.axis_size(axis)
    return lax.ppermute(value, axis, [(i, i ^ bit) for i in range(size)])


def tie(*values):
    return lax.optimization_barrier(values)


def run(kernel, scalars, inputs, outputs, streamed=(), scratch=(), vmem=12, micros=0.1):
    smem = pl.BlockSpec(memory_space=pltpu.SMEM)
    vmem_spec = pl.BlockSpec(memory_space=pltpu.VMEM)
    any_spec = pl.BlockSpec(memory_space=pl.ANY)
    outs = pl.pallas_call(
        kernel,
        in_specs=[smem] * len(scalars) + [vmem_spec] * len(inputs) + [any_spec] * len(streamed),
        out_specs=[vmem_spec if len(o) == 2 else any_spec for o in outputs],
        out_shape=[pltpu.VMEM(*o) if len(o) == 2 else jax.ShapeDtypeStruct(*o[:2]) for o in outputs],
        scratch_shapes=list(scratch),
        compiler_params=pltpu.CompilerParams(vmem_limit_bytes=vmem * 1024 * 1024),
        cost_estimate=pl.CostEstimate(flops=int(micros * FLOPS), bytes_accessed=1, transcendentals=0),
    )(
        *scalars,
        *[pltpu.with_memory_space_constraint(a, pltpu.VMEM) for a in inputs],
        *[pltpu.with_memory_space_constraint(a, pltpu.HBM) for a in streamed],
    )
    return list(outs)


def head_mask(width, head):
    lane = lax.broadcasted_iota(i32, (1, width), 1)
    return (lane >= head * HEAD_DIM) & (lane < (head + 1) * HEAD_DIM)


def group_ends(ints):
    count = (ints.shape[0] - HEADER) // 2

    def add(s, ends):
        spot = ints[HEADER + count + s] - ints[1] * SEQ_GRP
        length = jnp.where(spot >= 0, ints[HEADER + s], 0)
        return tuple(e + jnp.where(spot <= j, length, 0) for j, e in enumerate(ends))

    return lax.fori_loop(0, count, add, (jnp.int32(0),) * SEQ_GRP, unroll=8)


def segment_of(positions, ends):
    segment = jnp.zeros(positions.shape, i32)
    for e in ends:
        segment = segment + (positions >= e).astype(i32)
    return jnp.where(positions < ends[-1], segment, SEQ_GRP + positions)


def window(rows, start, ends, group_rows):
    low = jnp.int32(0)
    high = jnp.int32(0)
    last = start + rows - 1
    for e in ends:
        low = jnp.where(start >= e, jnp.maximum(low, e), low)
    for e in reversed(ends):
        high = jnp.where(last < e, e, high)
    padded = last >= ends[-1]
    low = jnp.where(start >= ends[-1], start, low)
    high = jnp.where(padded, start + rows, high)
    low = jnp.minimum(low // 128 * 128, group_rows - 128)
    return low, high - low


def by_window(rows, start, ends, group_rows, act):
    low, span = window(rows, start, ends, group_rows)
    widths = [w for w in (512, 768) if w < group_rows] + [group_rows]
    least = 0
    for w in widths:
        fits = (span > least) & (span <= w) if w < group_rows else span > least

        @pl.when(fits)
        def _(w=w):
            act(pl.multiple_of(jnp.minimum(low, group_rows - w), 128), w)

        least = w


def one_row(tile):
    return jnp.concatenate([tile[j : j + 1, :] for j in range(tile.shape[0])], axis=1)


def real_row(ids, mask):
    row = one_row(mask[...].astype(f32))
    lane = lax.broadcasted_iota(i32, row.shape, 1)
    return jnp.where(ids[0] * row.shape[1] + lane < group_ends(ids)[-1], row, 0.0)


def project_kernel(
    ids, x_hbm, w_hbm, bias_hbm, mask_hbm, b_in_hbm, q_ref, k_ref, v_ref, message, x_ref, w_ref, bias_ref, mask_ref,
    b_in_ref, sems,
):
    group_rows, width = q_ref.shape
    chunks = 4
    share = group_rows // chunks
    pairs = [(w_hbm, w_ref), (bias_hbm, bias_ref)]
    for c in range(chunks):
        rows = pl.ds(c * share, share)
        pairs.append((x_hbm.at[rows, :], x_ref.at[rows, :]))
    pairs += [(mask_hbm, mask_ref), (b_in_hbm, b_in_ref)]
    copies = [pltpu.make_async_copy(source, target, sems.at[j]) for j, (source, target) in enumerate(pairs)]
    for copy in copies:
        copy.start()
    copies[0].wait()
    copies[1].wait()
    bias = bias_ref[...].astype(f32)
    for c in range(chunks):
        rows = slice(c * share, (c + 1) * share)
        copies[2 + c].wait()
        x = x_ref[rows, :]
        k_ref[rows, :] = mm_nt(x, w_ref[width : 2 * width, :]).astype(bf16)
        v_ref[rows, :] = (mm_nt(x, w_ref[2 * width :, :]) + bias[1:2]).astype(bf16)
        q = (mm_nt(x, w_ref[:width, :]) + bias[0:1]).astype(bf16)
        q_ref[rows, :] = (q.astype(f32) * HEAD_DIM ** (-0.5)).astype(bf16)
    for copy in copies[2 + chunks :]:
        copy.wait()
    message[0:1, :] = one_row(b_in_ref[...].astype(f32))
    total = jnp.sum(real_row(ids, mask_ref), axis=-1, keepdims=True)
    message[1:, :] = jnp.broadcast_to(total, (message.shape[0] - 1, message.shape[1]))


def project(ids, x, w_t, b_qv, mask, b_in):
    group_rows, model = x.shape
    width = w_t.shape[0] // 3
    streamed = [x, w_t, b_qv, mask.reshape(-1, 128), b_in.reshape(-1, 128)]
    return run(
        project_kernel,
        (ids,),
        [],
        [((group_rows, width), bf16)] * 3 + [((8, model), f32)],
        streamed=streamed,
        scratch=[pltpu.VMEM(a.shape, a.dtype) for a in streamed] + [pltpu.SemaphoreType.DMA((8,))],
        micros=3.0,
    )


def attend_kernel(first, ids, q_ref, k_ref, v_ref, *refs):
    context_ref, e_ref, rl_ref = refs
    rows = rl_ref.shape[0] // 2
    group_rows, width = k_ref.shape
    heads = width // HEAD_DIM
    ends = group_ends(ids)

    def one(t, carry):
        start = pl.multiple_of(ids[2 + first + t] * rows, rows)
        at = pl.multiple_of(t * rows, rows)

        def act(key0, w):
            q = q_ref[pl.ds(start, rows), :].astype(f32)
            seg_q = segment_of(start + lax.broadcasted_iota(i32, (rows, 1), 0), ends)
            seg_k = segment_of(key0 + lax.broadcasted_iota(i32, (1, w), 1), ends)
            k = k_ref[pl.ds(key0, w), :]
            v = v_ref[pl.ds(key0, w), :]
            context = jnp.zeros((rows, width), f32)
            wide = jnp.zeros((rows, width), f32)
            for h in range(heads):
                mask = head_mask(width, h)
                scores = mm_nt(jnp.where(mask, q, 0.0).astype(bf16), k)
                scores = jnp.where(seg_q == seg_k, scores, NEG)
                e = jnp.exp(scores - jnp.max(scores, axis=-1, keepdims=True))
                inverse = 1.0 / jnp.sum(e, axis=-1, keepdims=True)
                low = e.astype(bf16)
                e_ref[pl.ds(pl.multiple_of((t * heads + h) * rows, rows), rows), :w] = low
                context = jnp.where(mask, mm(low, v) * inverse, context)
                wide = jnp.where(mask, inverse, wide)
            rl_ref[pl.ds(at, rows), :] = wide
            context_ref[pl.ds(at, rows), :] = context.astype(bf16)

        by_window(rows, start, ends, group_rows, act)
        return carry

    lax.fori_loop(0, 2, one, 0)


def attend(first, ids, q, k, v, share):
    group_rows, width = k.shape
    heads = width // HEAD_DIM
    return run(
        functools.partial(attend_kernel, first),
        (ids,),
        [q, k, v],
        [
            ((2 * share, width), bf16),
            ((2 * heads * share, group_rows), bf16),
            ((2 * share, width), f32),
        ],
        vmem=20,
        micros=3.0,
    )


def attend_back_kernel(spots, first, last, ids, *refs):
    count = len(spots)
    grads, refs = refs[:count], refs[count:]
    contexts, es, rls, refs = refs[0:2], refs[2:4], refs[4:6], refs[6:]
    q_ref, k_ref, v_ref, refs = refs[0], refs[1], refs[2], refs[3:]
    if not first:
        before, refs = refs[:3], refs[3:]
    if last:
        w_ref, far_out, near_out, gq, gk, gv = refs
    else:
        gq, gk, gv = refs
    rows = grads[0].shape[0]
    group_rows, width = k_ref.shape
    heads = width // HEAD_DIM
    ends = group_ends(ids)
    if first:
        gk[...] = jnp.zeros_like(gk)
        gv[...] = jnp.zeros_like(gv)
    else:
        gq[...] = before[0][...]
        gk[...] = before[1][...]
        gv[...] = before[2][...]
    for g_ref, spot in zip(grads, spots):
        start = pl.multiple_of(ids[2 + spot] * rows, rows)
        part, t = spot // 2, spot % 2
        g = g_ref[...].astype(f32) * rls[part][t * rows : (t + 1) * rows, :]
        dots = g * contexts[part][t * rows : (t + 1) * rows, :].astype(f32)
        q = q_ref[pl.ds(start, rows), :].astype(f32)

        def act(key0, w, g=g, dots=dots, q=q, part=part, t=t, start=start):
            keys = pl.ds(key0, w)
            k = k_ref[keys, :]
            v = v_ref[keys, :]
            out = jnp.zeros((rows, width), f32)
            add_k = jnp.zeros((w, width), f32)
            add_v = jnp.zeros((w, width), f32)
            for h in range(heads):
                mask = head_mask(width, h)
                g_head = jnp.where(mask, g, 0.0).astype(bf16)
                e = es[part][(t * heads + h) * rows : (t * heads + h + 1) * rows, :w]
                delta = jnp.sum(jnp.where(mask, dots, 0.0), axis=-1, keepdims=True)
                ds = (e.astype(f32) * (mm_nt(g_head, v) - delta)).astype(bf16)
                out = jnp.where(mask, mm(ds, k), out)
                add_k = add_k + mm_tn(ds, jnp.where(mask, q, 0.0).astype(bf16))
                add_v = add_v + mm_tn(e, g_head)
            gk[keys, :] += add_k
            gv[keys, :] += add_v
            gq[pl.ds(start, rows), :] = (out * HEAD_DIM ** (-0.5)).astype(bf16)

        by_window(rows, start, ends, group_rows, act)
    if last:
        for out, pair in ((far_out, (2, 3)), (near_out, (0, 1))):
            for t, spot in enumerate(pair):
                own = pl.ds(pl.multiple_of(ids[2 + spot] * rows, rows), rows)
                part = (
                    mm(gq[own, :], w_ref[:width, :])
                    + mm(gk[own, :].astype(bf16), w_ref[width : 2 * width, :])
                    + mm(gv[own, :].astype(bf16), w_ref[2 * width :, :])
                )
                out[t * rows : (t + 1) * rows, :] = part.astype(out.dtype)


def attend_back(spots, ids, grads, contexts, es, rls, qkv, before, w_t, share):
    group_rows, width = qkv[0].shape
    last = w_t is not None
    sums = [((group_rows, width), bf16), ((group_rows, width), f32), ((group_rows, width), f32)]
    inputs = [*grads, *contexts, *es, *rls, *qkv, *before]
    if last:
        model = w_t.shape[1]
        outputs = [((2 * share, model), bf16), ((2 * share, model), f32)]
        scratch = [pltpu.VMEM(*o) for o in sums]
        inputs.append(w_t)
    else:
        outputs, scratch = sums, []
    return run(
        functools.partial(attend_back_kernel, spots, not before, last),
        (ids,),
        inputs,
        outputs,
        scratch=scratch,
        vmem=20,
        micros=5.0 if last else 0.1,
    )


def early_kernel(ids, c0, c1, c3, o0, o1, o3, *refs):
    mask_hbm, *vectors = refs[:10]
    out, vecs, weight, mask_ref, *tiles, sems = refs[10:]
    pairs = [(mask_hbm, mask_ref), *zip(vectors, tiles)]
    copies = [pltpu.make_async_copy(source, target, sems.at[j]) for j, (source, target) in enumerate(pairs)]
    for copy in copies:
        copy.start()
    share = out.shape[0] // 2
    attn = mm(c0[...], o0[...]) + mm(c1[...], o1[...])
    for t in range(2):
        rows = slice(t * share, (t + 1) * share)
        out[rows, :] = attn[rows] + mm(c3[(1 - t) * share : (2 - t) * share, :], o3[...])
    for copy in copies:
        copy.wait()
    for j, tile in enumerate(tiles):
        vecs[j : j + 1, :] = one_row(tile[...].astype(f32))
    vecs[9:, :] = jnp.zeros((vecs.shape[0] - 9, vecs.shape[1]), f32)
    row = real_row(ids, mask_ref)
    here = lax.broadcasted_iota(i32, (share, share), 0) == lax.broadcasted_iota(i32, (share, share), 1)
    weight[...] = jnp.sum(jnp.where(here, jnp.broadcast_to(row, (share, share)), 0.0), axis=-1, keepdims=True)


def early_part(ids, arrays, mask, vectors, share):
    model = arrays[3].shape[1]
    streamed = [mask.reshape(-1, 128), *[v.reshape(-1, 128) for v in vectors]]
    return run(
        early_kernel,
        (ids,),
        arrays,
        [((2 * share, model), f32), ((16, model), f32), ((share, 1), f32)],
        streamed=streamed,
        scratch=[pltpu.VMEM(a.shape, a.dtype) for a in streamed] + [pltpu.SemaphoreType.DMA((len(streamed),))],
    )


def adapter_constants(down_bias, member_ref, spread_ref, bias_ref):
    flat = member_ref.shape[0]
    lane = lax.broadcasted_iota(i32, (flat, ADAPTERS), 0) - BOTTLENECK * lax.broadcasted_iota(
        i32, (flat, ADAPTERS), 1
    )
    member_ref[...] = ((lane >= 0) & (lane < BOTTLENECK)).astype(f32).astype(bf16)
    lane = lax.broadcasted_iota(i32, (ADAPTERS, flat), 1) - BOTTLENECK * lax.broadcasted_iota(
        i32, (ADAPTERS, flat), 0
    )
    spread = ((lane >= 0) & (lane < BOTTLENECK)).astype(f32)
    spread_ref[...] = spread.astype(bf16)
    cycle = lax.broadcasted_iota(i32, (BOTTLENECK, flat), 1) - lax.broadcasted_iota(i32, (BOTTLENECK, flat), 0)
    repeat = jnp.zeros(cycle.shape, f32)
    for a in range(ADAPTERS):
        repeat = repeat + (cycle == a * BOTTLENECK).astype(f32)
    bias_row = jnp.sum(mm(down_bias[...], repeat.astype(bf16)) * spread, axis=0, keepdims=True)
    bias_ref[...] = jnp.broadcast_to(bias_row, bias_ref.shape)


def forward_kernel(own, ids, early, c2, x_ref, o2, vecs, message, in0, in1, back0, back1, *rest):
    if own:
        inner_ref, down_bias, part_ref, slope, slope_two, first_ref, normed_ref, factor_ref, *constants = rest
    else:
        count, part_ref, inner_ref = rest
        write_small(part_ref, jnp.broadcast_to(count[0:1, 0:1], (8, x_ref.shape[1])))
    share = early.shape[0] // 2
    t = 0 if own else 1
    attn = early[t * share : (t + 1) * share, :] + mm(c2[(1 - t) * share : (2 - t) * share, :], o2[...])
    vec = vecs[...].astype(f32)
    start = pl.multiple_of(ids[2 if own else 3] * share, share)
    normed, factor = norm_parts(attn + vec[0:1] + x_ref[pl.ds(start, share), :].astype(f32))
    first = normed * vec[1:2] + vec[2:3]
    low = first.astype(bf16)
    part = jnp.zeros(first.shape, f32)
    units = in0.shape[1]
    chunk = units
    for j, (w_in, bias, w_back) in enumerate(((in0, vec[8:9], back0), (in1, message[0:1, :], back1))):
        for at in range(0, units, chunk):
            here = slice(at, at + chunk)
            columns = slice(j * units + at, j * units + at + chunk)
            inner = mm(low, w_in[:, here]) + bias[:, here]
            if own:
                act, bend = gelu_both(inner)
                slope[:, columns] = bend.astype(bf16)
                slope_two[:, columns] = gelu_both(inner_ref[:, columns])[1].astype(bf16)
            else:
                act = 0.5 * inner * (1.0 + lax.erf(inner * ROOT_HALF))
                inner_ref[:, columns] = inner
            part = part + mm(act.astype(bf16), w_back[here, :])
    part_ref[:share, :] = part.astype(part_ref.dtype)
    if own:
        first_ref[...] = first
        normed_ref[...] = normed
        factor_ref[...] = jnp.broadcast_to(factor, factor_ref.shape)
        adapter_constants(down_bias, *constants)


def forward_rows(own, ids, early, c2, x, o2, vecs, message, w_ins, w_backs, share, *more):
    model = x.shape[1]
    units = w_ins[0].shape[1]
    slope = ((share, 2 * units), bf16)
    flat = ADAPTERS * BOTTLENECK
    if own:
        outputs = [((share, model), f32), slope, slope] + [((share, model), f32)] * 2 + [((share, 128), f32)]
        outputs += [((flat, ADAPTERS), bf16), ((ADAPTERS, flat), bf16), ((8, flat), f32)]
    else:
        outputs = [((share + 16, model), bf16), ((share, 2 * units), f32)]
    return run(
        functools.partial(forward_kernel, own),
        (ids,),
        [early, c2, x, o2, vecs, message, *w_ins, *w_backs, *more],
        outputs,
        vmem=16,
        micros=3.0,
    )


def backward_kernel(gp, slope, back0, back1, in0, in1, part_ref):
    grad = gp[...]
    units = in0.shape[1]
    part = jnp.zeros(grad.shape, f32)
    for j, (w_back, w_in) in enumerate(((back0, in0), (back1, in1))):
        bend = slope[:, j * units : (j + 1) * units].astype(f32)
        inner = (bend * mm_nt(grad, w_back[...])).astype(bf16)
        part = part + mm_nt(inner, w_in[...])
    part_ref[...] = part.astype(part_ref.dtype)


def backward_rows(grad, slope, w_backs, w_ins, dtype):
    share, model = grad.shape
    units = w_ins[0].shape[1]
    return run(
        backward_kernel,
        (),
        [grad, slope, *w_backs, *w_ins],
        [((share, model), dtype)],
    )


def first_norm_kernel(own, got, gpre2, normed, factor, vecs, o0, o1, o2, o3, gpre1, c0, c1, c2, c3):
    grad = own[...] + got[...].astype(f32) + gpre2[...]
    grad = norm_back(grad, normed[...], factor[:, 0:1], vecs[...].astype(f32)[1:2])
    gpre1[...] = grad
    low = grad.astype(bf16)
    for c, o in ((c2, o2), (c3, o3), (c1, o1), (c0, o0)):
        c[...] = mm_nt(low, o[...]).astype(bf16)


def first_norm_back(own, got, gpre2, normed, factor, vecs, outs):
    share, model = own.shape
    width = outs[0].shape[0]
    return run(
        first_norm_kernel,
        (),
        [own, got, gpre2, normed, factor, vecs, *outs],
        [((share, model), f32)] + [((share, width), bf16)] * 4,
    )


def adapter_kernel(
    slots, ids, own, got, first_ref, cot, weight, count, vecs, member_ref, spread_ref, bias_ref, up_bias, down, up,
    wq, wk, wv,
    out_hbm, keep, give, sums, turn_ref, reduced_ref, mix_ref, base_ref, normed_ref, factor_ref, layer_out, lefts, sem,
):
    flat, model = up.shape
    vec = vecs[...].astype(f32)
    member = member_ref[...]
    spread = spread_ref[...]
    inv_root = model ** (-0.5)
    scale = 0.5 * slots / jnp.maximum(count[0:1, 0:1] + read_small(got)[0:1, 0:1], 1.0)

    normed_two, factor_two = norm_parts(own[...] + got[: own.shape[0], :].astype(f32) + vec[3:4] + first_ref[...])
    normed_ref[...] = normed_two
    factor_ref[...] = jnp.broadcast_to(factor_two, factor_ref.shape)
    second = normed_two * vec[4:5] + vec[5:6]
    second_low = second.astype(bf16)
    query_key = mm_nt(mm(second_low, wq[...]).astype(bf16), wk[...]) * inv_root
    query_key_low = query_key.astype(bf16)
    lift_key = mm_nt(query_key_low, up[...])
    reduced = mm_nt(second_low, down[...]) + bias_ref[0:1, :]
    reduced_ref[...] = reduced
    squeezed = 0.5 * reduced * (1.0 + lax.erf(reduced * ROOT_HALF))
    squeezed = squeezed.astype(bf16).astype(f32)
    logits = (
        mm((squeezed * lift_key).astype(bf16), member)
        + mm_nt(query_key_low, up_bias[...])
        + jnp.sum(query_key * second, axis=-1, keepdims=True)
    )
    shifted = logits - jnp.max(logits, axis=-1, keepdims=True)
    log_probs = shifted - jnp.log(jnp.sum(jnp.exp(shifted), axis=-1, keepdims=True))
    joining = jnp.exp(log_probs)
    entropy = -jnp.sum(joining * log_probs, axis=-1, keepdims=True)
    total = jnp.sum(joining, axis=-1, keepdims=True)
    joining_low = joining.astype(bf16)
    joining_wide = mm(joining_low, spread)
    joined_low = (joining_wide * squeezed).astype(bf16)
    mixed = total * second + mm(joined_low, up[...]) + mm(joining_low, up_bias[...])
    mixed_low = mixed.astype(bf16)
    normed_join, factor_join = norm_parts(second + mm(mixed_low, wv[...]))
    grad_out = cot[...].astype(f32)
    grad_pref = norm_back(grad_out, normed_join, factor_join, vec[6:7])
    grad_pref_low = grad_pref.astype(bf16)
    back_value = mm_nt(grad_pref_low, wv[...])
    back_value_low = back_value.astype(bf16)
    lift_value = mm_nt(back_value_low, up[...])
    grad_probs = (
        mm((squeezed * lift_value).astype(bf16), member)
        + mm_nt(back_value_low, up_bias[...])
        + jnp.sum(back_value * second, axis=-1, keepdims=True)
    )
    mean_grad = jnp.sum(joining * grad_probs, axis=-1, keepdims=True)
    grad_logits = joining * (grad_probs - mean_grad) - scale * weight[...] * joining * (log_probs + entropy)
    logits_low = grad_logits.astype(bf16)
    grad_wide = mm(logits_low, spread)
    logit_sum = jnp.sum(grad_logits, axis=-1, keepdims=True)
    turned = (
        logit_sum * second + mm((grad_wide * squeezed).astype(bf16), up[...]) + mm(logits_low, up_bias[...])
    ) * inv_root
    turned_low = turned.astype(bf16)
    turn_ref[...] = turned_low

    layer_out[...] = normed_join * vec[6:7] + vec[7:8]
    copy = pltpu.make_async_copy(layer_out, out_hbm, sem)
    copy.start()
    small = jnp.concatenate(
        [
            jnp.sum(grad_out * normed_join, axis=0, keepdims=True),
            jnp.sum(grad_out, axis=0, keepdims=True),
            jnp.zeros((sums.shape[0] - 2, model), f32),
        ],
        axis=0,
    )
    sums[...] = small
    write_small(give, small)
    mix_ref[...] = grad_wide * lift_key + joining_wide * lift_value
    base_ref[...] = grad_pref + logit_sum * query_key + total * back_value

    half = model // 2
    lefts[0] = second_low
    lefts[1] = mixed_low
    for j, right in enumerate((turned_low, grad_pref_low)):
        rows = slice(j * half, (j + 1) * half)
        other = lefts[j, :, pl.ds(pl.multiple_of((1 - ids[6]) * half, 128), half)]
        give[rows, :] = mm_tn(other, right).astype(bf16)
        mine = lefts[j, :, pl.ds(pl.multiple_of(ids[6] * half, 128), half)]
        keep[rows, :] = mm_tn(mine, right).astype(bf16)
    copy.wait()


def adapters(slots, ids, arrays):
    share, model = arrays[0].shape
    flat = ADAPTERS * BOTTLENECK
    wide, flat_wide = ((share, model), f32), ((share, flat), f32)
    return run(
        functools.partial(adapter_kernel, slots),
        (ids,),
        arrays,
        [
            ((share, model), f32, None),
            ((model, model), bf16),
            ((model + 16, model), bf16),
            ((8, model), f32),
            ((share, model), bf16),
            flat_wide,
            flat_wide,
            wide,
            wide,
            ((share, 128), f32),
        ],
        scratch=[
            pltpu.VMEM((share, model), f32),
            pltpu.VMEM((2, share, model), bf16),
            pltpu.SemaphoreType.DMA,
        ],
        vmem=20,
        micros=8.0,
    )


def adapter_rest_kernel(turn, reduced, mix, base, normed, factor, vecs, down, wq, wk, gpre2_ref, gpre2_low):
    grad_query_f = mm(turn[...], wk[...]).astype(bf16)
    grad_reduced = (gelu_both(reduced[...])[1] * mix[...]).astype(bf16)
    grad_second = base[...] + mm(grad_reduced, down[...]) + mm_nt(grad_query_f, wq[...])
    grad_pre2 = norm_back(grad_second, normed[...], factor[:, 0:1], vecs[4:5, :])
    gpre2_ref[...] = grad_pre2
    gpre2_low[...] = grad_pre2.astype(bf16)


def write_small(message, sums):
    high, low = halves_of(sums)
    rows = message.shape[0] - 16
    message[rows:, :] = jnp.concatenate([high, low], axis=0)


def read_small(message):
    rows = message.shape[0] - 16
    both = message[rows:, :].astype(f32)
    return both[:8] + both[8:]


def fold_kernel(base, start, split, last, ids, *refs):
    if start:
        keep, got, sums, *outs = refs
        rows = keep.shape[0] // 2
        pieces = [(keep, got, j * rows) for j in range(2)]
    else:
        *arrays, sums = refs[:5]
        outs = refs[5:]
        rows = arrays[0].shape[0]
        pieces = [(arrays[2 * j], arrays[2 * j + 1], 0) for j in range(2)]
        got = arrays[3]
    total = sums[...] + read_small(got)
    outs[-1][...] = total
    for j, (mine, other, at) in enumerate(pieces):
        def both(where):
            return (mine[where, :].astype(f32) + other[where, :].astype(f32)).astype(bf16)

        if split:
            half = rows // 2
            bit = ids[base + j]
            outs[2 * j][...] = both(pl.ds(pl.multiple_of(at + bit * half, 16), half))
            outs[2 * j + 1][:half, :] = both(pl.ds(pl.multiple_of(at + (1 - bit) * half, 16), half))
        elif last:
            outs[j][...] = both(pl.ds(at, rows))
        else:
            whole = both(pl.ds(at, rows))
            outs[2 * j][...] = whole
            outs[2 * j + 1][:rows, :] = whole
    if not last:
        write_small(outs[3], total)


def fold(ids, base, start, split, arrays, rows, sums, last=False):
    model = sums.shape[1]
    rows = rows // 2 if split else rows
    outputs = []
    for j in range(2):
        outputs += [((rows, model), bf16)] + ([] if last else [((rows + 16 * j, model), bf16)])
    outputs.append((sums.shape, f32))
    outs = run(functools.partial(fold_kernel, base, start, split, last), (ids,), [*arrays, sums], outputs)
    if last:
        return outs[:2], None, outs[2]
    return outs[0:4:2], outs[1:4:2], outs[4]


def join_kernel(base, last, ids, *refs):
    outs = refs[4:]
    for j in range(2):
        mine, got = refs[2 * j : 2 * j + 2]
        rows = mine.shape[0]
        bit = ids[base + j]
        out, at = (outs[0], 2 * rows * j) if last else (outs[j], 0)
        out[pl.ds(pl.multiple_of(at + bit * rows, 16), rows), :] = mine[...]
        out[pl.ds(pl.multiple_of(at + (1 - bit) * rows, 16), rows), :] = got[...]


def join(ids, base, last, mine, gots):
    rows, model = mine[0].shape
    outputs = [((4 * rows, model), bf16)] if last else [((2 * rows, model), bf16)] * 2
    arrays = [a for pair in zip(mine, gots) for a in pair]
    return run(functools.partial(join_kernel, base, last), (ids,), arrays, outputs)


def finish_kernel(first, ids, source, wq, wk, *refs):
    half = source.shape[0] // 2
    if first:
        out_q, out_v, key_part, stage, sems = refs
    else:
        key_before, _, _, out_q, out_v, out_k, stage, stage_k, sems = refs
    core = ids[6] if first else 1 - ids[6]
    rows = pl.ds(pl.multiple_of(core * half, half), half)
    copies = []

    def send(j, source, target):
        copies.append(pltpu.make_async_copy(source, target, sems.at[j]))
        copies[-1].start()

    mixed = source[:half, :]
    key = mm_tn(mixed, wq[rows, :])
    if first:
        key_part[...] = key
    else:
        stage_k[...] = key_before[...] + key
        send(2, stage_k, out_k)
    stage[1] = source[half:, :].astype(f32)
    send(1, stage.at[1], out_v.at[rows, :])
    stage[0] = mm(mixed, wk[...])
    send(0, stage.at[0], out_q.at[rows, :])
    for copy in copies:
        copy.wait()


def finish(ids, source, wq, wk, before):
    model = source.shape[1]
    half = source.shape[0] // 2
    first = before is None
    vmem_spec = pl.BlockSpec(memory_space=pltpu.VMEM)
    any_spec = pl.BlockSpec(memory_space=pl.ANY)
    whole = jax.ShapeDtypeStruct((model, model), f32)
    inputs = [source, wq, wk] + ([] if first else [before[2]])
    return pl.pallas_call(
        functools.partial(finish_kernel, first),
        in_specs=[pl.BlockSpec(memory_space=pltpu.SMEM)]
        + [vmem_spec] * len(inputs)
        + ([] if first else [any_spec] * 2),
        out_specs=[any_spec] * 2 + [vmem_spec if first else any_spec],
        out_shape=[whole, whole, pltpu.VMEM((model, model), f32) if first else whole],
        input_output_aliases={} if first else {5: 0, 6: 1},
        scratch_shapes=[pltpu.VMEM((2, half, model), f32)]
        + ([] if first else [pltpu.VMEM((model, model), f32)])
        + [pltpu.SemaphoreType.DMA((3,))],
        compiler_params=pltpu.CompilerParams(vmem_limit_bytes=16 * 1024 * 1024),
        cost_estimate=pl.CostEstimate(flops=int(2 * FLOPS), bytes_accessed=1, transcendentals=0),
    )(ids, *[pltpu.with_memory_space_constraint(a, pltpu.VMEM) for a in inputs], *([] if first else before[:2]))


def chip_kernel(near, got, gpre1, keep, give):
    share = keep.shape[0]
    give[...] = (near[share:, :] + got[share:, :].astype(f32)).astype(bf16)
    keep[...] = near[:share, :] + got[:share, :].astype(f32) + gpre1[...]


def body(
    layer_input,
    cotangent,
    seq_lens,
    seq_place,
    loss_mask,
    w_qkv,
    b_qv,
    w_out,
    b_out,
    ln1_gain,
    ln1_bias,
    w_in,
    b_in,
    w_back,
    b_back,
    ln2_gain,
    ln2_bias,
    ad_down,
    ad_down_bias,
    ad_up,
    ad_up_bias,
    join_query,
    join_key,
    join_value,
    join_gain,
    join_bias,
):
    group_rows, model = layer_input.shape
    share = cotangent.shape[0]
    rank = lax.axis_index("tp")
    dp_rank = lax.axis_index("dp")
    total_slots = group_rows * lax.axis_size("dp")

    core, near_x = ("tp", 1), ("tp", 2)
    others = []
    bit = 1
    while bit < lax.axis_size("dp"):
        others.append(("dp", bit))
        bit *= 2
    streams = [
        [others[0], *others[1:], near_x],
        [*others[1:2], others[0], near_x, *others[2:]],
    ]

    def bit_of(axis, which):
        return (lax.axis_index(axis) // which) % 2

    ids = [rank, dp_rank] + [rank ^ j for j in ORDER] + [bit_of(*core)]
    for at in range(len(others) + 1):
        ids += [bit_of(*stream[at]) for stream in streams]
    ids = jnp.stack(ids).astype(i32)
    ids = jnp.concatenate([ids, jnp.zeros(HEADER - ids.shape[0], i32), seq_lens, seq_place])
    vectors = [b_out, ln1_gain, ln1_bias, b_back, ln2_gain, ln2_bias, join_gain, join_bias, b_in]

    outs = [w_out, swap(w_out, "tp", 1), swap(w_out, "tp", 2)]
    outs.append(None)
    w_ins = [w_in, swap(w_in, "tp", 1)]
    w_backs = [w_back, swap(w_back, "tp", 1)]

    width = w_qkv.shape[2]
    w_t = jnp.transpose(w_qkv, (1, 2, 0)).reshape(3 * width, model)
    q, k, v, message = project(ids, layer_input, w_t, b_qv, loss_mask, b_in)
    message_got = swap(message, *core)
    far, e_far, rl_far = attend(2, ids, q, k, v, share)
    far, message_got, outs[1], outs[2], w_ins[1], w_backs[1] = tie(
        far, message_got, *outs[1:3], w_ins[1], w_backs[1]
    )
    outs[3] = swap(outs[2], "tp", 1)
    c1, c3 = swap(far, "tp", 1), swap(far, "tp", 3)
    counted = message[1:2, :128] + message_got[1:2, :128]
    count_got = swap(counted, *others[0])
    near, e_near, rl_near = attend(0, ids, q, k, v, share)
    c2 = swap(near, *near_x)
    near, count_got, outs[3], c1 = tie(near, count_got, outs[3], c1)
    counted = counted + count_got
    pair = [bit for _, bit in others[1:3]]
    count_gots = [swap(counted, "dp", bit) for bit in [*pair, *([sum(pair)] if len(pair) == 2 else [])]]
    early, vecs, weight_m = early_part(
        ids, [near, c1, c3, outs[0], outs[1], outs[3]], loss_mask, vectors, share
    )
    counted = sum(count_gots, counted)
    for axis, which in others[3:]:
        counted = counted + swap(counted, axis, which)
    early, counted = tie(early, counted)

    give, inner = forward_rows(
        False, ids, early, c2, layer_input, outs[2], vecs, message_got, w_ins, w_backs, share, counted
    )
    ffn_got = swap(give, *near_x)
    own, slope_one, slope_two, first, normed_one, factor_one, *constants = forward_rows(
        True, ids, early, c2, layer_input, outs[2], vecs, message_got, w_ins, w_backs, share, inner,
        ad_down_bias,
    )

    flat = ADAPTERS * BOTTLENECK
    down_t = jnp.transpose(ad_down, (1, 2, 0)).reshape(flat, model)
    up = ad_up.reshape(flat, model)
    layer_out, keep, give, sums, turn, reduced, mix, base, normed_two, factor_two = adapters(
        total_slots,
        ids,
        [
            own, ffn_got, first, cotangent, weight_m, counted, vecs, *constants, ad_up_bias, down_t, up,
            join_query, join_key, join_value,
        ],
    )
    got = swap(give, *core)
    gpre2, gpre2_low = run(
        adapter_rest_kernel,
        (),
        [turn, reduced, mix, base, normed_two, factor_two, vecs, down_t, join_query, join_key],
        [((share, model), f32), ((share, model), bf16)],
    )
    gpre2_got = swap(gpre2_low, "tp", 2)

    state = {"at": 0, "history": [], "rows": keep.shape[0] // 2}

    def sum_step(keeps, gots, sums):
        at = state["at"]
        start = at == 0
        split = state["rows"] // 2 >= LEAST_ROWS
        arrays = [keeps, gots] if start else [a for pair in zip(keeps, gots) for a in pair]
        keeps, gives, sums = fold(ids, 7 + 2 * at, start, split, arrays, state["rows"], sums)
        if split:
            state["rows"] //= 2
            state["history"].append(at)
        state["at"] = at + 1
        return keeps, [swap(g, *stream[at]) for g, stream in zip(gives, streams)], sums

    (back_own,) = backward_rows(gpre2_low, slope_one, w_backs, w_ins, f32)
    back_own, got = tie(back_own, got)
    keeps, gots, sums = sum_step(keep, got, sums)
    keeps[0], gpre2_got = tie(keeps[0], gpre2_got)
    (back_give,) = backward_rows(gpre2_got, slope_two, w_backs, w_ins, bf16)
    back_give, *gots = tie(back_give, *gots)
    keeps, gots, sums = sum_step(keeps, gots, sums)
    keeps[0], back_give = tie(keeps[0], back_give)
    back_got = swap(back_give, "tp", 2)
    keeps, gots, sums = sum_step(keeps, gots, sums)
    keeps[0], back_got = tie(keeps[0], back_got)
    gpre1, c0, c1, c2, c3 = first_norm_back(back_own, back_got, gpre2, normed_one, factor_one, vecs, outs)
    c2, c3, c1 = swap(c2, "tp", 2), swap(c3, "tp", 3), swap(c1, "tp", 1)
    shared = ((near, far), (e_near, e_far), (rl_near, rl_far), (q, k, v))
    before = list(attend_back((0,), ids, (c0,), *shared, [], None, share))
    before[0], *gots = tie(before[0], *gots)
    keeps, gots, sums = sum_step(keeps, gots, sums)
    before[0], keeps[0] = tie(before[0], keeps[0])
    far_part, near_part = attend_back((2, 1, 3), ids, (c1, c2, c3), *shared, before, w_t, share)
    far_part, *gots = tie(far_part, *gots)
    far_got = swap(far_part, "tp", 1)
    while state["at"] < len(others) + 1:
        keeps, gots, sums = sum_step(keeps, gots, sums)
    arrays = [a for pair in zip(keeps, gots) for a in pair]
    keeps, _, sums = fold(ids, 0, False, False, arrays, state["rows"], sums, last=True)
    gain_grad, bias_grad = sums[0], sums[1]
    part_own, part_give = run(
        chip_kernel, (), [near_part, far_got, gpre1], [((share, model), f32), ((share, model), bf16)]
    )
    part_got = swap(part_give, "tp", 2)
    for at in reversed(state["history"]):
        gots = [swap(a, *stream[at]) for a, stream in zip(keeps, streams)]
        if at == 0:
            input_grad = part_own + part_got.astype(f32)
            gots[0], input_grad = tie(gots[0], input_grad)
        else:
            gots[0], part_own, gain_grad, bias_grad = tie(gots[0], part_own, gain_grad, bias_grad)
        keeps = join(ids, 7 + 2 * at, at == 0, keeps, gots)
    got = swap(keeps[0], *core)
    part = finish(ids, keeps[0], join_query, join_key, None)
    query_grad, value_grad, key_grad = finish(ids, got, join_query, join_key, part)
    return (layer_out, input_grad, query_grad, key_grad, value_grad, gain_grad, bias_grad)


def solution(mesh):
    placed = (
        P("dp", None),
        P(("dp", "tp"), None),
        P(),
        P(),
        P(("dp", "tp")),
        P(None, None, "tp"),
        P(None, "tp"),
        P("tp", None),
        P(),
        P(),
        P(),
        P(None, "tp"),
        P("tp"),
        P("tp", None),
        P(),
        P(),
        P(),
        P(),
        P(),
        P(),
        P(),
        P(),
        P(),
        P(),
        P(),
        P(),
    )
    return jax.shard_map(
        body,
        mesh=mesh,
        in_specs=placed,
        out_specs=(P(("dp", "tp"), None), P(("dp", "tp"), None), P(), P(), P(), P(), P()),
        check_vma=False,
    )
```

```python
import functools

import jax
import jax.numpy as jnp
from jax import lax
from jax.experimental import pallas as pl
from jax.experimental.pallas import tpu as pltpu
from jax.sharding import PartitionSpec as P

HEAD_DIM = 64
ADAPTERS = 16
BOTTLENECK = 48
SEQ_GRP = 4
LEAST_ROWS = 96
FLOPS = 1.15e9

EPS = 1e-06
NEG = -1e30
ROOT_HALF = 0.7071067811865476
INV_ROOT_TAU = 0.3989422804014327

f32 = jnp.float32
bf16 = jnp.bfloat16
i32 = jnp.int32

HEADER = 64

ORDER = (0, 2, 1, 3)


def gelu_both(values):
    phi = 0.5 * (1.0 + lax.erf(values * ROOT_HALF))
    return values * phi, phi + values * jnp.exp(-0.5 * values * values) * INV_ROOT_TAU


def row_mean(values):
    return jnp.sum(values, axis=-1, keepdims=True) * (1.0 / values.shape[-1])


def norm_parts(values):
    center = values - row_mean(values)
    factor = lax.rsqrt(row_mean(center * center) + EPS)
    return center * factor, factor


def norm_back(gradient, normed, factor, gain_vec):
    scaled = gradient * gain_vec
    return factor * (scaled - row_mean(scaled) - normed * row_mean(scaled * normed))


def mm(a, b):
    return lax.dot_general(a, b, (((1,), (0,)), ((), ())), preferred_element_type=f32)


def mm_nt(a, b):
    return lax.dot_general(a, b, (((1,), (1,)), ((), ())), preferred_element_type=f32)


def mm_tn(a, b):
    return lax.dot_general(a, b, (((0,), (0,)), ((), ())), preferred_element_type=f32)


def halves_of(a):
    high = a.astype(bf16)
    return high, (a - high.astype(f32)).astype(bf16)


def swap(value, axis, bit):
    size = lax.axis_size(axis)
    return lax.ppermute(value, axis, [(i, i ^ bit) for i in range(size)])


def tie(*values):
    return lax.optimization_barrier(values)


def run(kernel, scalars, inputs, outputs, streamed=(), scratch=(), vmem=12, micros=0.1):
    smem = pl.BlockSpec(memory_space=pltpu.SMEM)
    vmem_spec = pl.BlockSpec(memory_space=pltpu.VMEM)
    any_spec = pl.BlockSpec(memory_space=pl.ANY)
    outs = pl.pallas_call(
        kernel,
        in_specs=[smem] * len(scalars) + [vmem_spec] * len(inputs) + [any_spec] * len(streamed),
        out_specs=[vmem_spec if len(o) == 2 else any_spec for o in outputs],
        out_shape=[pltpu.VMEM(*o) if len(o) == 2 else jax.ShapeDtypeStruct(*o[:2]) for o in outputs],
        scratch_shapes=list(scratch),
        compiler_params=pltpu.CompilerParams(vmem_limit_bytes=vmem * 1024 * 1024),
        cost_estimate=pl.CostEstimate(flops=int(micros * FLOPS), bytes_accessed=1, transcendentals=0),
    )(
        *scalars,
        *[pltpu.with_memory_space_constraint(a, pltpu.VMEM) for a in inputs],
        *[pltpu.with_memory_space_constraint(a, pltpu.HBM) for a in streamed],
    )
    return list(outs)


def head_mask(width, head):
    lane = lax.broadcasted_iota(i32, (1, width), 1)
    return (lane >= head * HEAD_DIM) & (lane < (head + 1) * HEAD_DIM)


def group_ends(ints):
    count = (ints.shape[0] - HEADER) // 2

    def add(s, ends):
        spot = ints[HEADER + count + s] - ints[1] * SEQ_GRP
        length = jnp.where(spot >= 0, ints[HEADER + s], 0)
        return tuple(e + jnp.where(spot <= j, length, 0) for j, e in enumerate(ends))

    return lax.fori_loop(0, count, add, (jnp.int32(0),) * SEQ_GRP, unroll=8)


def segment_of(positions, ends):
    segment = jnp.zeros(positions.shape, i32)
    for e in ends:
        segment = segment + (positions >= e).astype(i32)
    return jnp.where(positions < ends[-1], segment, SEQ_GRP + positions)


def window(rows, start, ends, group_rows):
    low = jnp.int32(0)
    high = jnp.int32(0)
    last = start + rows - 1
    for e in ends:
        low = jnp.where(start >= e, jnp.maximum(low, e), low)
    for e in reversed(ends):
        high = jnp.where(last < e, e, high)
    padded = last >= ends[-1]
    low = jnp.where(start >= ends[-1], start, low)
    high = jnp.where(padded, start + rows, high)
    low = jnp.minimum(low // 128 * 128, group_rows - 128)
    return low, high - low


def by_window(rows, start, ends, group_rows, act):
    low, span = window(rows, start, ends, group_rows)
    widths = [w for w in (512, 768) if w < group_rows] + [group_rows]
    least = 0
    for w in widths:
        fits = (span > least) & (span <= w) if w < group_rows else span > least

        @pl.when(fits)
        def _(w=w):
            act(pl.multiple_of(jnp.minimum(low, group_rows - w), 128), w)

        least = w


def one_row(tile):
    return jnp.concatenate([tile[j : j + 1, :] for j in range(tile.shape[0])], axis=1)


def real_row(ids, mask):
    row = one_row(mask[...].astype(f32))
    lane = lax.broadcasted_iota(i32, row.shape, 1)
    return jnp.where(ids[0] * row.shape[1] + lane < group_ends(ids)[-1], row, 0.0)


def project_kernel(
    ids, x_hbm, w_hbm, bias_hbm, mask_hbm, b_in_hbm, q_ref, k_ref, v_ref, message, x_ref, w_ref, bias_ref, mask_ref,
    b_in_ref, sems,
):
    group_rows, width = q_ref.shape
    chunks = 4
    share = group_rows // chunks
    pairs = [(w_hbm, w_ref), (bias_hbm, bias_ref)]
    for c in range(chunks):
        rows = pl.ds(c * share, share)
        pairs.append((x_hbm.at[rows, :], x_ref.at[rows, :]))
    pairs += [(mask_hbm, mask_ref), (b_in_hbm, b_in_ref)]
    copies = [pltpu.make_async_copy(source, target, sems.at[j]) for j, (source, target) in enumerate(pairs)]
    for copy in copies:
        copy.start()
    copies[0].wait()
    copies[1].wait()
    bias = bias_ref[...].astype(f32)
    for c in range(chunks):
        rows = slice(c * share, (c + 1) * share)
        copies[2 + c].wait()
        x = x_ref[rows, :]
        k_ref[rows, :] = mm_nt(x, w_ref[width : 2 * width, :]).astype(bf16)
        v_ref[rows, :] = (mm_nt(x, w_ref[2 * width :, :]) + bias[1:2]).astype(bf16)
        q = (mm_nt(x, w_ref[:width, :]) + bias[0:1]).astype(bf16)
        q_ref[rows, :] = (q.astype(f32) * HEAD_DIM ** (-0.5)).astype(bf16)
    for copy in copies[2 + chunks :]:
        copy.wait()
    message[0:1, :] = one_row(b_in_ref[...].astype(f32))
    total = jnp.sum(real_row(ids, mask_ref), axis=-1, keepdims=True)
    message[1:, :] = jnp.broadcast_to(total, (message.shape[0] - 1, message.shape[1]))


def project(ids, x, w_t, b_qv, mask, b_in):
    group_rows, model = x.shape
    width = w_t.shape[0] // 3
    streamed = [x, w_t, b_qv, mask.reshape(-1, 128), b_in.reshape(-1, 128)]
    return run(
        project_kernel,
        (ids,),
        [],
        [((group_rows, width), bf16)] * 3 + [((8, model), f32)],
        streamed=streamed,
        scratch=[pltpu.VMEM(a.shape, a.dtype) for a in streamed] + [pltpu.SemaphoreType.DMA((8,))],
        micros=3.0,
    )


def attend_kernel(first, ids, q_ref, k_ref, v_ref, *refs):
    context_ref, e_ref, rl_ref = refs
    rows = rl_ref.shape[0] // 2
    group_rows, width = k_ref.shape
    heads = width // HEAD_DIM
    ends = group_ends(ids)

    def one(t, carry):
        start = pl.multiple_of(ids[2 + first + t] * rows, rows)
        at = pl.multiple_of(t * rows, rows)

        def act(key0, w):
            q = q_ref[pl.ds(start, rows), :].astype(f32)
            seg_q = segment_of(start + lax.broadcasted_iota(i32, (rows, 1), 0), ends)
            seg_k = segment_of(key0 + lax.broadcasted_iota(i32, (1, w), 1), ends)
            k = k_ref[pl.ds(key0, w), :]
            v = v_ref[pl.ds(key0, w), :]
            context = jnp.zeros((rows, width), f32)
            wide = jnp.zeros((rows, width), f32)
            for h in range(heads):
                mask = head_mask(width, h)
                scores = mm_nt(jnp.where(mask, q, 0.0).astype(bf16), k)
                scores = jnp.where(seg_q == seg_k, scores, NEG)
                e = jnp.exp(scores - jnp.max(scores, axis=-1, keepdims=True))
                inverse = 1.0 / jnp.sum(e, axis=-1, keepdims=True)
                low = e.astype(bf16)
                e_ref[pl.ds(pl.multiple_of((t * heads + h) * rows, rows), rows), :w] = low
                context = jnp.where(mask, mm(low, v) * inverse, context)
                wide = jnp.where(mask, inverse, wide)
            rl_ref[pl.ds(at, rows), :] = wide
            context_ref[pl.ds(at, rows), :] = context.astype(bf16)

        by_window(rows, start, ends, group_rows, act)
        return carry

    lax.fori_loop(0, 2, one, 0)


def attend(first, ids, q, k, v, share):
    group_rows, width = k.shape
    heads = width // HEAD_DIM
    return run(
        functools.partial(attend_kernel, first),
        (ids,),
        [q, k, v],
        [
            ((2 * share, width), bf16),
            ((2 * heads * share, group_rows), bf16),
            ((2 * share, width), f32),
        ],
        vmem=20,
        micros=3.0,
    )


def attend_back_kernel(spots, first, last, ids, *refs):
    count = len(spots)
    grads, refs = refs[:count], refs[count:]
    contexts, es, rls, refs = refs[0:2], refs[2:4], refs[4:6], refs[6:]
    q_ref, k_ref, v_ref, refs = refs[0], refs[1], refs[2], refs[3:]
    if not first:
        before, refs = refs[:3], refs[3:]
    if last:
        w_ref, far_out, near_out, gq, gk, gv = refs
    else:
        gq, gk, gv = refs
    rows = grads[0].shape[0]
    group_rows, width = k_ref.shape
    heads = width // HEAD_DIM
    ends = group_ends(ids)
    if first:
        gk[...] = jnp.zeros_like(gk)
        gv[...] = jnp.zeros_like(gv)
    else:
        gq[...] = before[0][...]
        gk[...] = before[1][...]
        gv[...] = before[2][...]
    for g_ref, spot in zip(grads, spots):
        start = pl.multiple_of(ids[2 + spot] * rows, rows)
        part, t = spot // 2, spot % 2
        g = g_ref[...].astype(f32) * rls[part][t * rows : (t + 1) * rows, :]
        dots = g * contexts[part][t * rows : (t + 1) * rows, :].astype(f32)
        q = q_ref[pl.ds(start, rows), :].astype(f32)

        def act(key0, w, g=g, dots=dots, q=q, part=part, t=t, start=start):
            keys = pl.ds(key0, w)
            k = k_ref[keys, :]
            v = v_ref[keys, :]
            out = jnp.zeros((rows, width), f32)
            add_k = jnp.zeros((w, width), f32)
            add_v = jnp.zeros((w, width), f32)
            for h in range(heads):
                mask = head_mask(width, h)
                g_head = jnp.where(mask, g, 0.0).astype(bf16)
                e = es[part][(t * heads + h) * rows : (t * heads + h + 1) * rows, :w]
                delta = jnp.sum(jnp.where(mask, dots, 0.0), axis=-1, keepdims=True)
                ds = (e.astype(f32) * (mm_nt(g_head, v) - delta)).astype(bf16)
                out = jnp.where(mask, mm(ds, k), out)
                add_k = add_k + mm_tn(ds, jnp.where(mask, q, 0.0).astype(bf16))
                add_v = add_v + mm_tn(e, g_head)
            gk[keys, :] += add_k
            gv[keys, :] += add_v
            gq[pl.ds(start, rows), :] = (out * HEAD_DIM ** (-0.5)).astype(bf16)

        by_window(rows, start, ends, group_rows, act)
    if last:
        for out, pair in ((far_out, (2, 3)), (near_out, (0, 1))):
            for t, spot in enumerate(pair):
                own = pl.ds(pl.multiple_of(ids[2 + spot] * rows, rows), rows)
                part = (
                    mm(gq[own, :], w_ref[:width, :])
                    + mm(gk[own, :].astype(bf16), w_ref[width : 2 * width, :])
                    + mm(gv[own, :].astype(bf16), w_ref[2 * width :, :])
                )
                out[t * rows : (t + 1) * rows, :] = part.astype(out.dtype)


def attend_back(spots, ids, grads, contexts, es, rls, qkv, before, w_t, share):
    group_rows, width = qkv[0].shape
    last = w_t is not None
    sums = [((group_rows, width), bf16), ((group_rows, width), f32), ((group_rows, width), f32)]
    inputs = [*grads, *contexts, *es, *rls, *qkv, *before]
    if last:
        model = w_t.shape[1]
        outputs = [((2 * share, model), bf16), ((2 * share, model), f32)]
        scratch = [pltpu.VMEM(*o) for o in sums]
        inputs.append(w_t)
    else:
        outputs, scratch = sums, []
    return run(
        functools.partial(attend_back_kernel, spots, not before, last),
        (ids,),
        inputs,
        outputs,
        scratch=scratch,
        vmem=20,
        micros=5.0 if last else 0.1,
    )


def early_kernel(ids, c0, c1, c3, o0, o1, o3, *refs):
    mask_hbm, *vectors = refs[:10]
    out, vecs, weight, mask_ref, *tiles, sems = refs[10:]
    pairs = [(mask_hbm, mask_ref), *zip(vectors, tiles)]
    copies = [pltpu.make_async_copy(source, target, sems.at[j]) for j, (source, target) in enumerate(pairs)]
    for copy in copies:
        copy.start()
    share = out.shape[0] // 2
    attn = mm(c0[...], o0[...]) + mm(c1[...], o1[...])
    for t in range(2):
        rows = slice(t * share, (t + 1) * share)
        out[rows, :] = attn[rows] + mm(c3[(1 - t) * share : (2 - t) * share, :], o3[...])
    for copy in copies:
        copy.wait()
    for j, tile in enumerate(tiles):
        vecs[j : j + 1, :] = one_row(tile[...].astype(f32))
    vecs[9:, :] = jnp.zeros((vecs.shape[0] - 9, vecs.shape[1]), f32)
    row = real_row(ids, mask_ref)
    here = lax.broadcasted_iota(i32, (share, share), 0) == lax.broadcasted_iota(i32, (share, share), 1)
    weight[...] = jnp.sum(jnp.where(here, jnp.broadcast_to(row, (share, share)), 0.0), axis=-1, keepdims=True)


def early_part(ids, arrays, mask, vectors, share):
    model = arrays[3].shape[1]
    streamed = [mask.reshape(-1, 128), *[v.reshape(-1, 128) for v in vectors]]
    return run(
        early_kernel,
        (ids,),
        arrays,
        [((2 * share, model), f32), ((16, model), f32), ((share, 1), f32)],
        streamed=streamed,
        scratch=[pltpu.VMEM(a.shape, a.dtype) for a in streamed] + [pltpu.SemaphoreType.DMA((len(streamed),))],
    )


def adapter_constants(down_bias, member_ref, spread_ref, bias_ref):
    flat = member_ref.shape[0]
    lane = lax.broadcasted_iota(i32, (flat, ADAPTERS), 0) - BOTTLENECK * lax.broadcasted_iota(
        i32, (flat, ADAPTERS), 1
    )
    member_ref[...] = ((lane >= 0) & (lane < BOTTLENECK)).astype(f32).astype(bf16)
    lane = lax.broadcasted_iota(i32, (ADAPTERS, flat), 1) - BOTTLENECK * lax.broadcasted_iota(
        i32, (ADAPTERS, flat), 0
    )
    spread = ((lane >= 0) & (lane < BOTTLENECK)).astype(f32)
    spread_ref[...] = spread.astype(bf16)
    cycle = lax.broadcasted_iota(i32, (BOTTLENECK, flat), 1) - lax.broadcasted_iota(i32, (BOTTLENECK, flat), 0)
    repeat = jnp.zeros(cycle.shape, f32)
    for a in range(ADAPTERS):
        repeat = repeat + (cycle == a * BOTTLENECK).astype(f32)
    bias_row = jnp.sum(mm(down_bias[...], repeat.astype(bf16)) * spread, axis=0, keepdims=True)
    bias_ref[...] = jnp.broadcast_to(bias_row, bias_ref.shape)


def forward_kernel(own, ids, early, c2, x_ref, o2, vecs, message, in0, in1, back0, back1, *rest):
    if own:
        inner_ref, down_bias, part_ref, slope, slope_two, first_ref, normed_ref, factor_ref, *constants = rest
    else:
        count, part_ref, inner_ref = rest
        write_small(part_ref, jnp.broadcast_to(count[0:1, 0:1], (8, x_ref.shape[1])))
    share = early.shape[0] // 2
    t = 0 if own else 1
    attn = early[t * share : (t + 1) * share, :] + mm(c2[(1 - t) * share : (2 - t) * share, :], o2[...])
    vec = vecs[...].astype(f32)
    start = pl.multiple_of(ids[2 if own else 3] * share, share)
    normed, factor = norm_parts(attn + vec[0:1] + x_ref[pl.ds(start, share), :].astype(f32))
    first = normed * vec[1:2] + vec[2:3]
    low = first.astype(bf16)
    part = jnp.zeros(first.shape, f32)
    units = in0.shape[1]
    chunk = units
    for j, (w_in, bias, w_back) in enumerate(((in0, vec[8:9], back0), (in1, message[0:1, :], back1))):
        for at in range(0, units, chunk):
            here = slice(at, at + chunk)
            columns = slice(j * units + at, j * units + at + chunk)
            inner = mm(low, w_in[:, here]) + bias[:, here]
            if own:
                act, bend = gelu_both(inner)
                slope[:, columns] = bend.astype(bf16)
                slope_two[:, columns] = gelu_both(inner_ref[:, columns])[1].astype(bf16)
            else:
                act = 0.5 * inner * (1.0 + lax.erf(inner * ROOT_HALF))
                inner_ref[:, columns] = inner
            part = part + mm(act.astype(bf16), w_back[here, :])
    part_ref[:share, :] = part.astype(part_ref.dtype)
    if own:
        first_ref[...] = first
        normed_ref[...] = normed
        factor_ref[...] = jnp.broadcast_to(factor, factor_ref.shape)
        adapter_constants(down_bias, *constants)


def forward_rows(own, ids, early, c2, x, o2, vecs, message, w_ins, w_backs, share, *more):
    model = x.shape[1]
    units = w_ins[0].shape[1]
    slope = ((share, 2 * units), bf16)
    flat = ADAPTERS * BOTTLENECK
    if own:
        outputs = [((share, model), f32), slope, slope] + [((share, model), f32)] * 2 + [((share, 128), f32)]
        outputs += [((flat, ADAPTERS), bf16), ((ADAPTERS, flat), bf16), ((8, flat), f32)]
    else:
        outputs = [((share + 16, model), bf16), ((share, 2 * units), f32)]
    return run(
        functools.partial(forward_kernel, own),
        (ids,),
        [early, c2, x, o2, vecs, message, *w_ins, *w_backs, *more],
        outputs,
        vmem=16,
        micros=3.0,
    )


def backward_kernel(gp, slope, back0, back1, in0, in1, part_ref):
    grad = gp[...]
    units = in0.shape[1]
    part = jnp.zeros(grad.shape, f32)
    for j, (w_back, w_in) in enumerate(((back0, in0), (back1, in1))):
        bend = slope[:, j * units : (j + 1) * units].astype(f32)
        inner = (bend * mm_nt(grad, w_back[...])).astype(bf16)
        part = part + mm_nt(inner, w_in[...])
    part_ref[...] = part.astype(part_ref.dtype)


def backward_rows(grad, slope, w_backs, w_ins, dtype):
    share, model = grad.shape
    units = w_ins[0].shape[1]
    return run(
        backward_kernel,
        (),
        [grad, slope, *w_backs, *w_ins],
        [((share, model), dtype)],
    )


def first_norm_kernel(own, got, gpre2, normed, factor, vecs, o0, o1, o2, o3, gpre1, c0, c1, c2, c3):
    grad = own[...] + got[...].astype(f32) + gpre2[...]
    grad = norm_back(grad, normed[...], factor[:, 0:1], vecs[...].astype(f32)[1:2])
    gpre1[...] = grad
    low = grad.astype(bf16)
    for c, o in ((c2, o2), (c3, o3), (c1, o1), (c0, o0)):
        c[...] = mm_nt(low, o[...]).astype(bf16)


def first_norm_back(own, got, gpre2, normed, factor, vecs, outs):
    share, model = own.shape
    width = outs[0].shape[0]
    return run(
        first_norm_kernel,
        (),
        [own, got, gpre2, normed, factor, vecs, *outs],
        [((share, model), f32)] + [((share, width), bf16)] * 4,
    )


def adapter_kernel(
    slots, ids, own, got, first_ref, cot, weight, count, vecs, member_ref, spread_ref, bias_ref, up_bias, down, up,
    wq, wk, wv,
    out_hbm, keep, give, sums, turn_ref, reduced_ref, mix_ref, base_ref, normed_ref, factor_ref, layer_out, lefts, sem,
):
    flat, model = up.shape
    vec = vecs[...].astype(f32)
    member = member_ref[...]
    spread = spread_ref[...]
    inv_root = model ** (-0.5)
    scale = 0.5 * slots / jnp.maximum(count[0:1, 0:1] + read_small(got)[0:1, 0:1], 1.0)

    normed_two, factor_two = norm_parts(own[...] + got[: own.shape[0], :].astype(f32) + vec[3:4] + first_ref[...])
    normed_ref[...] = normed_two
    factor_ref[...] = jnp.broadcast_to(factor_two, factor_ref.shape)
    second = normed_two * vec[4:5] + vec[5:6]
    second_low = second.astype(bf16)
    query_key = mm_nt(mm(second_low, wq[...]).astype(bf16), wk[...]) * inv_root
    query_key_low = query_key.astype(bf16)
    lift_key = mm_nt(query_key_low, up[...])
    reduced = mm_nt(second_low, down[...]) + bias_ref[0:1, :]
    reduced_ref[...] = reduced
    squeezed = 0.5 * reduced * (1.0 + lax.erf(reduced * ROOT_HALF))
    squeezed = squeezed.astype(bf16).astype(f32)
    logits = (
        mm((squeezed * lift_key).astype(bf16), member)
        + mm_nt(query_key_low, up_bias[...])
        + jnp.sum(query_key * second, axis=-1, keepdims=True)
    )
    shifted = logits - jnp.max(logits, axis=-1, keepdims=True)
    log_probs = shifted - jnp.log(jnp.sum(jnp.exp(shifted), axis=-1, keepdims=True))
    joining = jnp.exp(log_probs)
    entropy = -jnp.sum(joining * log_probs, axis=-1, keepdims=True)
    total = jnp.sum(joining, axis=-1, keepdims=True)
    joining_low = joining.astype(bf16)
    joining_wide = mm(joining_low, spread)
    joined_low = (joining_wide * squeezed).astype(bf16)
    mixed = total * second + mm(joined_low, up[...]) + mm(joining_low, up_bias[...])
    mixed_low = mixed.astype(bf16)
    normed_join, factor_join = norm_parts(second + mm(mixed_low, wv[...]))
    grad_out = cot[...].astype(f32)
    grad_pref = norm_back(grad_out, normed_join, factor_join, vec[6:7])
    grad_pref_low = grad_pref.astype(bf16)
    back_value = mm_nt(grad_pref_low, wv[...])
    back_value_low = back_value.astype(bf16)
    lift_value = mm_nt(back_value_low, up[...])
    grad_probs = (
        mm((squeezed * lift_value).astype(bf16), member)
        + mm_nt(back_value_low, up_bias[...])
        + jnp.sum(back_value * second, axis=-1, keepdims=True)
    )
    mean_grad = jnp.sum(joining * grad_probs, axis=-1, keepdims=True)
    grad_logits = joining * (grad_probs - mean_grad) - scale * weight[...] * joining * (log_probs + entropy)
    logits_low = grad_logits.astype(bf16)
    grad_wide = mm(logits_low, spread)
    logit_sum = jnp.sum(grad_logits, axis=-1, keepdims=True)
    turned = (
        logit_sum * second + mm((grad_wide * squeezed).astype(bf16), up[...]) + mm(logits_low, up_bias[...])
    ) * inv_root
    turned_low = turned.astype(bf16)
    turn_ref[...] = turned_low

    layer_out[...] = normed_join * vec[6:7] + vec[7:8]
    copy = pltpu.make_async_copy(layer_out, out_hbm, sem)
    copy.start()
    small = jnp.concatenate(
        [
            jnp.sum(grad_out * normed_join, axis=0, keepdims=True),
            jnp.sum(grad_out, axis=0, keepdims=True),
            jnp.zeros((sums.shape[0] - 2, model), f32),
        ],
        axis=0,
    )
    sums[...] = small
    write_small(give, small)
    mix_ref[...] = grad_wide * lift_key + joining_wide * lift_value
    base_ref[...] = grad_pref + logit_sum * query_key + total * back_value

    half = model // 2
    lefts[0] = second_low
    lefts[1] = mixed_low
    for j, right in enumerate((turned_low, grad_pref_low)):
        rows = slice(j * half, (j + 1) * half)
        other = lefts[j, :, pl.ds(pl.multiple_of((1 - ids[6]) * half, 128), half)]
        give[rows, :] = mm_tn(other, right).astype(bf16)
        mine = lefts[j, :, pl.ds(pl.multiple_of(ids[6] * half, 128), half)]
        keep[rows, :] = mm_tn(mine, right).astype(bf16)
    copy.wait()


def adapters(slots, ids, arrays):
    share, model = arrays[0].shape
    flat = ADAPTERS * BOTTLENECK
    wide, flat_wide = ((share, model), f32), ((share, flat), f32)
    return run(
        functools.partial(adapter_kernel, slots),
        (ids,),
        arrays,
        [
            ((share, model), f32, None),
            ((model, model), bf16),
            ((model + 16, model), bf16),
            ((8, model), f32),
            ((share, model), bf16),
            flat_wide,
            flat_wide,
            wide,
            wide,
            ((share, 128), f32),
        ],
        scratch=[
            pltpu.VMEM((share, model), f32),
            pltpu.VMEM((2, share, model), bf16),
            pltpu.SemaphoreType.DMA,
        ],
        vmem=20,
        micros=8.0,
    )


def adapter_rest_kernel(turn, reduced, mix, base, normed, factor, vecs, down, wq, wk, gpre2_ref, gpre2_low):
    grad_query_f = mm(turn[...], wk[...]).astype(bf16)
    grad_reduced = (gelu_both(reduced[...])[1] * mix[...]).astype(bf16)
    grad_second = base[...] + mm(grad_reduced, down[...]) + mm_nt(grad_query_f, wq[...])
    grad_pre2 = norm_back(grad_second, normed[...], factor[:, 0:1], vecs[4:5, :])
    gpre2_ref[...] = grad_pre2
    gpre2_low[...] = grad_pre2.astype(bf16)


def write_small(message, sums):
    high, low = halves_of(sums)
    rows = message.shape[0] - 16
    message[rows:, :] = jnp.concatenate([high, low], axis=0)


def read_small(message):
    rows = message.shape[0] - 16
    both = message[rows:, :].astype(f32)
    return both[:8] + both[8:]


def fold_kernel(base, start, split, last, ids, *refs):
    if start:
        keep, got, sums, *outs = refs
        rows = keep.shape[0] // 2
        pieces = [(keep, got, j * rows) for j in range(2)]
    else:
        *arrays, sums = refs[:5]
        outs = refs[5:]
        rows = arrays[0].shape[0]
        pieces = [(arrays[2 * j], arrays[2 * j + 1], 0) for j in range(2)]
        got = arrays[3]
    total = sums[...] + read_small(got)
    outs[-1][...] = total
    for j, (mine, other, at) in enumerate(pieces):
        def both(where):
            return (mine[where, :].astype(f32) + other[where, :].astype(f32)).astype(bf16)

        if split:
            half = rows // 2
            bit = ids[base + j]
            outs[2 * j][...] = both(pl.ds(pl.multiple_of(at + bit * half, 16), half))
            outs[2 * j + 1][:half, :] = both(pl.ds(pl.multiple_of(at + (1 - bit) * half, 16), half))
        elif last:
            outs[j][...] = both(pl.ds(at, rows))
        else:
            whole = both(pl.ds(at, rows))
            outs[2 * j][...] = whole
            outs[2 * j + 1][:rows, :] = whole
    if not last:
        write_small(outs[3], total)


def fold(ids, base, start, split, arrays, rows, sums, last=False):
    model = sums.shape[1]
    rows = rows // 2 if split else rows
    outputs = []
    for j in range(2):
        outputs += [((rows, model), bf16)] + ([] if last else [((rows + 16 * j, model), bf16)])
    outputs.append((sums.shape, f32))
    outs = run(functools.partial(fold_kernel, base, start, split, last), (ids,), [*arrays, sums], outputs)
    if last:
        return outs[:2], None, outs[2]
    return outs[0:4:2], outs[1:4:2], outs[4]


def join_kernel(base, last, ids, *refs):
    outs = refs[4:]
    for j in range(2):
        mine, got = refs[2 * j : 2 * j + 2]
        rows = mine.shape[0]
        bit = ids[base + j]
        out, at = (outs[0], 2 * rows * j) if last else (outs[j], 0)
        out[pl.ds(pl.multiple_of(at + bit * rows, 16), rows), :] = mine[...]
        out[pl.ds(pl.multiple_of(at + (1 - bit) * rows, 16), rows), :] = got[...]


def join(ids, base, last, mine, gots):
    rows, model = mine[0].shape
    outputs = [((4 * rows, model), bf16)] if last else [((2 * rows, model), bf16)] * 2
    arrays = [a for pair in zip(mine, gots) for a in pair]
    return run(functools.partial(join_kernel, base, last), (ids,), arrays, outputs)


def finish_kernel(first, ids, source, wq, wk, *refs):
    half = source.shape[0] // 2
    if first:
        out_q, out_v, key_part, stage, sems = refs
    else:
        key_before, _, _, out_q, out_v, out_k, stage, stage_k, sems = refs
    core = ids[6] if first else 1 - ids[6]
    rows = pl.ds(pl.multiple_of(core * half, half), half)
    copies = []

    def send(j, source, target):
        copies.append(pltpu.make_async_copy(source, target, sems.at[j]))
        copies[-1].start()

    mixed = source[:half, :]
    key = mm_tn(mixed, wq[rows, :])
    if first:
        key_part[...] = key
    else:
        stage_k[...] = key_before[...] + key
        send(2, stage_k, out_k)
    stage[1] = source[half:, :].astype(f32)
    send(1, stage.at[1], out_v.at[rows, :])
    stage[0] = mm(mixed, wk[...])
    send(0, stage.at[0], out_q.at[rows, :])
    for copy in copies:
        copy.wait()


def finish(ids, source, wq, wk, before):
    model = source.shape[1]
    half = source.shape[0] // 2
    first = before is None
    vmem_spec = pl.BlockSpec(memory_space=pltpu.VMEM)
    any_spec = pl.BlockSpec(memory_space=pl.ANY)
    whole = jax.ShapeDtypeStruct((model, model), f32)
    inputs = [source, wq, wk] + ([] if first else [before[2]])
    return pl.pallas_call(
        functools.partial(finish_kernel, first),
        in_specs=[pl.BlockSpec(memory_space=pltpu.SMEM)]
        + [vmem_spec] * len(inputs)
        + ([] if first else [any_spec] * 2),
        out_specs=[any_spec] * 2 + [vmem_spec if first else any_spec],
        out_shape=[whole, whole, pltpu.VMEM((model, model), f32) if first else whole],
        input_output_aliases={} if first else {5: 0, 6: 1},
        scratch_shapes=[pltpu.VMEM((2, half, model), f32)]
        + ([] if first else [pltpu.VMEM((model, model), f32)])
        + [pltpu.SemaphoreType.DMA((3,))],
        compiler_params=pltpu.CompilerParams(vmem_limit_bytes=16 * 1024 * 1024),
        cost_estimate=pl.CostEstimate(flops=int(2 * FLOPS), bytes_accessed=1, transcendentals=0),
    )(ids, *[pltpu.with_memory_space_constraint(a, pltpu.VMEM) for a in inputs], *([] if first else before[:2]))


def chip_kernel(near, got, gpre1, keep, give):
    share = keep.shape[0]
    give[...] = (near[share:, :] + got[share:, :].astype(f32)).astype(bf16)
    keep[...] = near[:share, :] + got[:share, :].astype(f32) + gpre1[...]


def body(
    layer_input,
    cotangent,
    seq_lens,
    seq_place,
    loss_mask,
    w_qkv,
    b_qv,
    w_out,
    b_out,
    ln1_gain,
    ln1_bias,
    w_in,
    b_in,
    w_back,
    b_back,
    ln2_gain,
    ln2_bias,
    ad_down,
    ad_down_bias,
    ad_up,
    ad_up_bias,
    join_query,
    join_key,
    join_value,
    join_gain,
    join_bias,
):
    group_rows, model = layer_input.shape
    share = cotangent.shape[0]
    rank = lax.axis_index("tp")
    dp_rank = lax.axis_index("dp")
    total_slots = group_rows * lax.axis_size("dp")

    core, near_x = ("tp", 1), ("tp", 2)
    others = []
    bit = 1
    while bit < lax.axis_size("dp"):
        others.append(("dp", bit))
        bit *= 2
    streams = [
        [others[0], *others[1:], near_x],
        [*others[1:2], others[0], near_x, *others[2:]],
    ]

    def bit_of(axis, which):
        return (lax.axis_index(axis) // which) % 2

    ids = [rank, dp_rank] + [rank ^ j for j in ORDER] + [bit_of(*core)]
    for at in range(len(others) + 1):
        ids += [bit_of(*stream[at]) for stream in streams]
    ids = jnp.stack(ids).astype(i32)
    ids = jnp.concatenate([ids, jnp.zeros(HEADER - ids.shape[0], i32), seq_lens, seq_place])
    vectors = [b_out, ln1_gain, ln1_bias, b_back, ln2_gain, ln2_bias, join_gain, join_bias, b_in]

    outs = [w_out, swap(w_out, "tp", 1), swap(w_out, "tp", 2)]
    outs.append(None)
    w_ins = [w_in, swap(w_in, "tp", 1)]
    w_backs = [w_back, swap(w_back, "tp", 1)]

    width = w_qkv.shape[2]
    w_t = jnp.transpose(w_qkv, (1, 2, 0)).reshape(3 * width, model)
    q, k, v, message = project(ids, layer_input, w_t, b_qv, loss_mask, b_in)
    message_got = swap(message, *core)
    far, e_far, rl_far = attend(2, ids, q, k, v, share)
    far, message_got, outs[1], outs[2], w_ins[1], w_backs[1] = tie(
        far, message_got, *outs[1:3], w_ins[1], w_backs[1]
    )
    outs[3] = swap(outs[2], "tp", 1)
    c1, c3 = swap(far, "tp", 1), swap(far, "tp", 3)
    counted = message[1:2, :128] + message_got[1:2, :128]
    count_got = swap(counted, *others[0])
    near, e_near, rl_near = attend(0, ids, q, k, v, share)
    c2 = swap(near, *near_x)
    near, count_got, outs[3], c1 = tie(near, count_got, outs[3], c1)
    counted = counted + count_got
    pair = [bit for _, bit in others[1:3]]
    count_gots = [swap(counted, "dp", bit) for bit in [*pair, *([sum(pair)] if len(pair) == 2 else [])]]
    early, vecs, weight_m = early_part(
        ids, [near, c1, c3, outs[0], outs[1], outs[3]], loss_mask, vectors, share
    )
    counted = sum(count_gots, counted)
    for axis, which in others[3:]:
        counted = counted + swap(counted, axis, which)
    early, counted = tie(early, counted)

    give, inner = forward_rows(
        False, ids, early, c2, layer_input, outs[2], vecs, message_got, w_ins, w_backs, share, counted
    )
    ffn_got = swap(give, *near_x)
    own, slope_one, slope_two, first, normed_one, factor_one, *constants = forward_rows(
        True, ids, early, c2, layer_input, outs[2], vecs, message_got, w_ins, w_backs, share, inner,
        ad_down_bias,
    )

    flat = ADAPTERS * BOTTLENECK
    down_t = jnp.transpose(ad_down, (1, 2, 0)).reshape(flat, model)
    up = ad_up.reshape(flat, model)
    layer_out, keep, give, sums, turn, reduced, mix, base, normed_two, factor_two = adapters(
        total_slots,
        ids,
        [
            own, ffn_got, first, cotangent, weight_m, counted, vecs, *constants, ad_up_bias, down_t, up,
            join_query, join_key, join_value,
        ],
    )
    got = swap(give, *core)
    gpre2, gpre2_low = run(
        adapter_rest_kernel,
        (),
        [turn, reduced, mix, base, normed_two, factor_two, vecs, down_t, join_query, join_key],
        [((share, model), f32), ((share, model), bf16)],
    )
    gpre2_got = swap(gpre2_low, "tp", 2)

    state = {"at": 0, "history": [], "rows": keep.shape[0] // 2}

    def sum_step(keeps, gots, sums):
        at = state["at"]
        start = at == 0
        split = state["rows"] // 2 >= LEAST_ROWS
        arrays = [keeps, gots] if start else [a for pair in zip(keeps, gots) for a in pair]
        keeps, gives, sums = fold(ids, 7 + 2 * at, start, split, arrays, state["rows"], sums)
        if split:
            state["rows"] //= 2
            state["history"].append(at)
        state["at"] = at + 1
        return keeps, [swap(g, *stream[at]) for g, stream in zip(gives, streams)], sums

    (back_own,) = backward_rows(gpre2_low, slope_one, w_backs, w_ins, f32)
    back_own, got = tie(back_own, got)
    keeps, gots, sums = sum_step(keep, got, sums)
    keeps[0], gpre2_got = tie(keeps[0], gpre2_got)
    (back_give,) = backward_rows(gpre2_got, slope_two, w_backs, w_ins, bf16)
    back_give, *gots = tie(back_give, *gots)
    keeps, gots, sums = sum_step(keeps, gots, sums)
    keeps[0], back_give = tie(keeps[0], back_give)
    back_got = swap(back_give, "tp", 2)
    keeps, gots, sums = sum_step(keeps, gots, sums)
    keeps[0], back_got = tie(keeps[0], back_got)
    gpre1, c0, c1, c2, c3 = first_norm_back(back_own, back_got, gpre2, normed_one, factor_one, vecs, outs)
    c2, c3, c1 = swap(c2, "tp", 2), swap(c3, "tp", 3), swap(c1, "tp", 1)
    shared = ((near, far), (e_near, e_far), (rl_near, rl_far), (q, k, v))
    before = list(attend_back((0,), ids, (c0,), *shared, [], None, share))
    before[0], *gots = tie(before[0], *gots)
    keeps, gots, sums = sum_step(keeps, gots, sums)
    before[0], keeps[0] = tie(before[0], keeps[0])
    far_part, near_part = attend_back((2, 1, 3), ids, (c1, c2, c3), *shared, before, w_t, share)
    far_part, *gots = tie(far_part, *gots)
    far_got = swap(far_part, "tp", 1)
    while state["at"] < len(others) + 1:
        keeps, gots, sums = sum_step(keeps, gots, sums)
    arrays = [a for pair in zip(keeps, gots) for a in pair]
    keeps, _, sums = fold(ids, 0, False, False, arrays, state["rows"], sums, last=True)
    gain_grad, bias_grad = sums[0], sums[1]
    part_own, part_give = run(
        chip_kernel, (), [near_part, far_got, gpre1], [((share, model), f32), ((share, model), bf16)]
    )
    part_got = swap(part_give, "tp", 2)
    for at in reversed(state["history"]):
        gots = [swap(a, *stream[at]) for a, stream in zip(keeps, streams)]
        gots[0], part_own, gain_grad, bias_grad = tie(gots[0], part_own, gain_grad, bias_grad)
        keeps = join(ids, 7 + 2 * at, at == 0, keeps, gots)
    keeps[0], part_got = tie(keeps[0], part_got)
    got = swap(keeps[0], *core)
    input_grad = part_own + part_got.astype(f32)
    part = finish(ids, keeps[0], join_query, join_key, None)
    query_grad, value_grad, key_grad = finish(ids, got, join_query, join_key, part)
    return (layer_out, input_grad, query_grad, key_grad, value_grad, gain_grad, bias_grad)


def solution(mesh):
    placed = (
        P("dp", None),
        P(("dp", "tp"), None),
        P(),
        P(),
        P(("dp", "tp")),
        P(None, None, "tp"),
        P(None, "tp"),
        P("tp", None),
        P(),
        P(),
        P(),
        P(None, "tp"),
        P("tp"),
        P("tp", None),
        P(),
        P(),
        P(),
        P(),
        P(),
        P(),
        P(),
        P(),
        P(),
        P(),
        P(),
        P(),
    )
    return jax.shard_map(
        body,
        mesh=mesh,
        in_specs=placed,
        out_specs=(P(("dp", "tp"), None), P(("dp", "tp"), None), P(), P(), P(), P(), P()),
        check_vma=False,
    )
```

```python
import functools

import jax
import jax.numpy as jnp
from jax import lax
from jax.experimental import pallas as pl
from jax.experimental.pallas import tpu as pltpu
from jax.sharding import PartitionSpec as P

HEAD_DIM = 64
ADAPTERS = 16
BOTTLENECK = 48
SEQ_GRP = 4
LEAST_ROWS = 96
FLOPS = 1.15e9

EPS = 1e-06
NEG = -1e30
ROOT_HALF = 0.7071067811865476
INV_ROOT_TAU = 0.3989422804014327

f32 = jnp.float32
bf16 = jnp.bfloat16
i32 = jnp.int32

HEADER = 64

ORDER = (0, 2, 1, 3)


def gelu_both(values):
    phi = 0.5 * (1.0 + lax.erf(values * ROOT_HALF))
    return values * phi, phi + values * jnp.exp(-0.5 * values * values) * INV_ROOT_TAU


def row_mean(values):
    return jnp.sum(values, axis=-1, keepdims=True) * (1.0 / values.shape[-1])


def norm_parts(values):
    center = values - row_mean(values)
    factor = lax.rsqrt(row_mean(center * center) + EPS)
    return center * factor, factor


def norm_back(gradient, normed, factor, gain_vec):
    scaled = gradient * gain_vec
    return factor * (scaled - row_mean(scaled) - normed * row_mean(scaled * normed))


def mm(a, b):
    return lax.dot_general(a, b, (((1,), (0,)), ((), ())), preferred_element_type=f32)


def mm_nt(a, b):
    return lax.dot_general(a, b, (((1,), (1,)), ((), ())), preferred_element_type=f32)


def mm_tn(a, b):
    return lax.dot_general(a, b, (((0,), (0,)), ((), ())), preferred_element_type=f32)


def halves_of(a):
    high = a.astype(bf16)
    return high, (a - high.astype(f32)).astype(bf16)


def swap(value, axis, bit):
    size = lax.axis_size(axis)
    return lax.ppermute(value, axis, [(i, i ^ bit) for i in range(size)])


def tie(*values):
    return lax.optimization_barrier(values)


def run(kernel, scalars, inputs, outputs, streamed=(), scratch=(), vmem=12, micros=0.1):
    smem = pl.BlockSpec(memory_space=pltpu.SMEM)
    vmem_spec = pl.BlockSpec(memory_space=pltpu.VMEM)
    any_spec = pl.BlockSpec(memory_space=pl.ANY)
    outs = pl.pallas_call(
        kernel,
        in_specs=[smem] * len(scalars) + [vmem_spec] * len(inputs) + [any_spec] * len(streamed),
        out_specs=[vmem_spec if len(o) == 2 else any_spec for o in outputs],
        out_shape=[pltpu.VMEM(*o) if len(o) == 2 else jax.ShapeDtypeStruct(*o[:2]) for o in outputs],
        scratch_shapes=list(scratch),
        compiler_params=pltpu.CompilerParams(vmem_limit_bytes=vmem * 1024 * 1024),
        cost_estimate=pl.CostEstimate(flops=int(micros * FLOPS), bytes_accessed=1, transcendentals=0),
    )(
        *scalars,
        *[pltpu.with_memory_space_constraint(a, pltpu.VMEM) for a in inputs],
        *[pltpu.with_memory_space_constraint(a, pltpu.HBM) for a in streamed],
    )
    return list(outs)


def head_mask(width, head):
    lane = lax.broadcasted_iota(i32, (1, width), 1)
    return (lane >= head * HEAD_DIM) & (lane < (head + 1) * HEAD_DIM)


def group_ends(ints):
    count = (ints.shape[0] - HEADER) // 2

    def add(s, ends):
        spot = ints[HEADER + count + s] - ints[1] * SEQ_GRP
        length = jnp.where(spot >= 0, ints[HEADER + s], 0)
        return tuple(e + jnp.where(spot <= j, length, 0) for j, e in enumerate(ends))

    return lax.fori_loop(0, count, add, (jnp.int32(0),) * SEQ_GRP, unroll=8)


def segment_of(positions, ends):
    segment = jnp.zeros(positions.shape, i32)
    for e in ends:
        segment = segment + (positions >= e).astype(i32)
    return jnp.where(positions < ends[-1], segment, SEQ_GRP + positions)


def window(rows, start, ends, group_rows):
    low = jnp.int32(0)
    high = jnp.int32(0)
    last = start + rows - 1
    for e in ends:
        low = jnp.where(start >= e, jnp.maximum(low, e), low)
    for e in reversed(ends):
        high = jnp.where(last < e, e, high)
    padded = last >= ends[-1]
    low = jnp.where(start >= ends[-1], start, low)
    high = jnp.where(padded, start + rows, high)
    low = jnp.minimum(low // 128 * 128, group_rows - 128)
    return low, high - low


def by_window(rows, start, ends, group_rows, act):
    low, span = window(rows, start, ends, group_rows)
    widths = [w for w in (512,) if w < group_rows] + [group_rows]
    least = 0
    for w in widths:
        fits = (span > least) & (span <= w) if w < group_rows else span > least

        @pl.when(fits)
        def _(w=w):
            act(pl.multiple_of(jnp.minimum(low, group_rows - w), 128), w)

        least = w


def one_row(tile):
    return jnp.concatenate([tile[j : j + 1, :] for j in range(tile.shape[0])], axis=1)


def real_row(ids, mask):
    row = one_row(mask[...].astype(f32))
    lane = lax.broadcasted_iota(i32, row.shape, 1)
    return jnp.where(ids[0] * row.shape[1] + lane < group_ends(ids)[-1], row, 0.0)


def project_kernel(
    ids, x_hbm, w_hbm, bias_hbm, mask_hbm, b_in_hbm, q_ref, k_ref, v_ref, message, x_ref, w_ref, bias_ref, mask_ref,
    b_in_ref, sems,
):
    group_rows, width = q_ref.shape
    chunks = 4
    share = group_rows // chunks
    pairs = [(w_hbm, w_ref), (bias_hbm, bias_ref)]
    for c in range(chunks):
        rows = pl.ds(c * share, share)
        pairs.append((x_hbm.at[rows, :], x_ref.at[rows, :]))
    pairs += [(mask_hbm, mask_ref), (b_in_hbm, b_in_ref)]
    copies = [pltpu.make_async_copy(source, target, sems.at[j]) for j, (source, target) in enumerate(pairs)]
    for copy in copies:
        copy.start()
    copies[0].wait()
    copies[1].wait()
    bias = bias_ref[...].astype(f32)
    for c in range(chunks):
        rows = slice(c * share, (c + 1) * share)
        copies[2 + c].wait()
        x = x_ref[rows, :]
        k_ref[rows, :] = mm_nt(x, w_ref[width : 2 * width, :]).astype(bf16)
        v_ref[rows, :] = (mm_nt(x, w_ref[2 * width :, :]) + bias[1:2]).astype(bf16)
        q = (mm_nt(x, w_ref[:width, :]) + bias[0:1]).astype(bf16)
        q_ref[rows, :] = (q.astype(f32) * HEAD_DIM ** (-0.5)).astype(bf16)
    for copy in copies[2 + chunks :]:
        copy.wait()
    message[0:1, :] = one_row(b_in_ref[...].astype(f32))
    total = jnp.sum(real_row(ids, mask_ref), axis=-1, keepdims=True)
    message[1:, :] = jnp.broadcast_to(total, (message.shape[0] - 1, message.shape[1]))


def project(ids, x, w_t, b_qv, mask, b_in):
    group_rows, model = x.shape
    width = w_t.shape[0] // 3
    streamed = [x, w_t, b_qv, mask.reshape(-1, 128), b_in.reshape(-1, 128)]
    return run(
        project_kernel,
        (ids,),
        [],
        [((group_rows, width), bf16)] * 3 + [((8, model), f32)],
        streamed=streamed,
        scratch=[pltpu.VMEM(a.shape, a.dtype) for a in streamed] + [pltpu.SemaphoreType.DMA((8,))],
        micros=3.0,
    )


def attend_kernel(first, blocks, ids, q_ref, k_ref, v_ref, *refs):
    context_ref, e_ref, rl_ref = refs
    rows = rl_ref.shape[0] // blocks
    group_rows, width = k_ref.shape
    heads = width // HEAD_DIM
    ends = group_ends(ids)

    def one(t, carry):
        start = pl.multiple_of(ids[2 + first + t] * rows, rows)
        at = pl.multiple_of(t * rows, rows)

        def act(key0, w):
            q = q_ref[pl.ds(start, rows), :].astype(f32)
            seg_q = segment_of(start + lax.broadcasted_iota(i32, (rows, 1), 0), ends)
            seg_k = segment_of(key0 + lax.broadcasted_iota(i32, (1, w), 1), ends)
            k = k_ref[pl.ds(key0, w), :]
            v = v_ref[pl.ds(key0, w), :]
            context = jnp.zeros((rows, width), f32)
            wide = jnp.zeros((rows, width), f32)
            for h in range(heads):
                mask = head_mask(width, h)
                scores = mm_nt(jnp.where(mask, q, 0.0).astype(bf16), k)
                scores = jnp.where(seg_q == seg_k, scores, NEG)
                e = jnp.exp(scores - jnp.max(scores, axis=-1, keepdims=True))
                inverse = 1.0 / jnp.sum(e, axis=-1, keepdims=True)
                low = e.astype(bf16)
                e_ref[pl.ds(pl.multiple_of((t * heads + h) * rows, rows), rows), :w] = low
                context = jnp.where(mask, mm(low, v) * inverse, context)
                wide = jnp.where(mask, inverse, wide)
            rl_ref[pl.ds(at, rows), :] = wide
            context_ref[pl.ds(at, rows), :] = context.astype(bf16)

        by_window(rows, start, ends, group_rows, act)
        return carry

    lax.fori_loop(0, blocks, one, 0)


def attend(first, blocks, ids, q, k, v, share):
    group_rows, width = k.shape
    heads = width // HEAD_DIM
    return run(
        functools.partial(attend_kernel, first, blocks),
        (ids,),
        [q, k, v],
        [
            ((blocks * share, width), bf16),
            ((blocks * heads * share, group_rows), bf16),
            ((blocks * share, width), f32),
        ],
        vmem=20,
        micros=3.0 if first else 0.1,
    )


def attend_back_kernel(spots, first, last, ids, *refs):
    count = len(spots)
    grads, refs = refs[:count], refs[count:]
    contexts, es, rls, refs = refs[0:3], refs[3:6], refs[6:9], refs[9:]
    q_ref, k_ref, v_ref, refs = refs[0], refs[1], refs[2], refs[3:]
    if not first:
        before, refs = refs[:3], refs[3:]
    if last:
        w_ref, far_out, near_out, gq, gk, gv = refs
    else:
        gq, gk, gv = refs
    rows = grads[0].shape[0]
    group_rows, width = k_ref.shape
    heads = width // HEAD_DIM
    ends = group_ends(ids)
    if first:
        gk[...] = jnp.zeros_like(gk)
        gv[...] = jnp.zeros_like(gv)
    else:
        gq[...] = before[0][...]
        gk[...] = before[1][...]
        gv[...] = before[2][...]
    for g_ref, spot in zip(grads, spots):
        start = pl.multiple_of(ids[2 + spot] * rows, rows)
        part, t = (spot, 0) if spot < 2 else (2, spot - 2)
        g = g_ref[...].astype(f32) * rls[part][t * rows : (t + 1) * rows, :]
        dots = g * contexts[part][t * rows : (t + 1) * rows, :].astype(f32)
        q = q_ref[pl.ds(start, rows), :].astype(f32)

        def act(key0, w, g=g, dots=dots, q=q, part=part, t=t, start=start):
            keys = pl.ds(key0, w)
            k = k_ref[keys, :]
            v = v_ref[keys, :]
            out = jnp.zeros((rows, width), f32)
            add_k = jnp.zeros((w, width), f32)
            add_v = jnp.zeros((w, width), f32)
            for h in range(heads):
                mask = head_mask(width, h)
                g_head = jnp.where(mask, g, 0.0).astype(bf16)
                e = es[part][(t * heads + h) * rows : (t * heads + h + 1) * rows, :w]
                delta = jnp.sum(jnp.where(mask, dots, 0.0), axis=-1, keepdims=True)
                ds = (e.astype(f32) * (mm_nt(g_head, v) - delta)).astype(bf16)
                out = jnp.where(mask, mm(ds, k), out)
                add_k = add_k + mm_tn(ds, jnp.where(mask, q, 0.0).astype(bf16))
                add_v = add_v + mm_tn(e, g_head)
            gk[keys, :] += add_k
            gv[keys, :] += add_v
            gq[pl.ds(start, rows), :] = (out * HEAD_DIM ** (-0.5)).astype(bf16)

        by_window(rows, start, ends, group_rows, act)
    if last:
        for out, pair in ((far_out, (2, 3)), (near_out, (0, 1))):
            for t, spot in enumerate(pair):
                own = pl.ds(pl.multiple_of(ids[2 + spot] * rows, rows), rows)
                part = (
                    mm(gq[own, :], w_ref[:width, :])
                    + mm(gk[own, :].astype(bf16), w_ref[width : 2 * width, :])
                    + mm(gv[own, :].astype(bf16), w_ref[2 * width :, :])
                )
                out[t * rows : (t + 1) * rows, :] = part.astype(out.dtype)


def attend_back(spots, ids, grads, contexts, es, rls, qkv, before, w_t, share):
    group_rows, width = qkv[0].shape
    last = w_t is not None
    sums = [((group_rows, width), bf16), ((group_rows, width), f32), ((group_rows, width), f32)]
    inputs = [*grads, *contexts, *es, *rls, *qkv, *before]
    if last:
        model = w_t.shape[1]
        outputs = [((2 * share, model), bf16), ((2 * share, model), f32)]
        scratch = [pltpu.VMEM(*o) for o in sums]
        inputs.append(w_t)
    else:
        outputs, scratch = sums, []
    return run(
        functools.partial(attend_back_kernel, spots, not before, last),
        (ids,),
        inputs,
        outputs,
        scratch=scratch,
        vmem=20,
        micros=5.0 if last else 0.1,
    )


def early_kernel(ids, c0, x0, c1, c3, o0, o1, o3, *refs):
    mask_hbm, *vectors = refs[:10]
    out, vecs, weight, mask_ref, *tiles, sems = refs[10:]
    pairs = [(mask_hbm, mask_ref), *zip(vectors, tiles)]
    copies = [pltpu.make_async_copy(source, target, sems.at[j]) for j, (source, target) in enumerate(pairs)]
    for copy in copies:
        copy.start()
    share = out.shape[0] // 2
    attn = mm(c1[...], o1[...])
    for t, mine in enumerate((c0, x0)):
        rows = slice(t * share, (t + 1) * share)
        out[rows, :] = attn[rows] + mm(mine[...], o0[...]) + mm(c3[(1 - t) * share : (2 - t) * share, :], o3[...])
    for copy in copies:
        copy.wait()
    for j, tile in enumerate(tiles):
        vecs[j : j + 1, :] = one_row(tile[...].astype(f32))
    vecs[9:, :] = jnp.zeros((vecs.shape[0] - 9, vecs.shape[1]), f32)
    row = real_row(ids, mask_ref)
    here = lax.broadcasted_iota(i32, (share, share), 0) == lax.broadcasted_iota(i32, (share, share), 1)
    weight[...] = jnp.sum(jnp.where(here, jnp.broadcast_to(row, (share, share)), 0.0), axis=-1, keepdims=True)


def early_part(ids, arrays, mask, vectors, share):
    model = arrays[4].shape[1]
    streamed = [mask.reshape(-1, 128), *[v.reshape(-1, 128) for v in vectors]]
    return run(
        early_kernel,
        (ids,),
        arrays,
        [((2 * share, model), f32), ((16, model), f32), ((share, 1), f32)],
        streamed=streamed,
        scratch=[pltpu.VMEM(a.shape, a.dtype) for a in streamed] + [pltpu.SemaphoreType.DMA((len(streamed),))],
    )


def adapter_constants(down_bias, member_ref, spread_ref, bias_ref):
    flat = member_ref.shape[0]
    lane = lax.broadcasted_iota(i32, (flat, ADAPTERS), 0) - BOTTLENECK * lax.broadcasted_iota(
        i32, (flat, ADAPTERS), 1
    )
    member_ref[...] = ((lane >= 0) & (lane < BOTTLENECK)).astype(f32).astype(bf16)
    lane = lax.broadcasted_iota(i32, (ADAPTERS, flat), 1) - BOTTLENECK * lax.broadcasted_iota(
        i32, (ADAPTERS, flat), 0
    )
    spread = ((lane >= 0) & (lane < BOTTLENECK)).astype(f32)
    spread_ref[...] = spread.astype(bf16)
    cycle = lax.broadcasted_iota(i32, (BOTTLENECK, flat), 1) - lax.broadcasted_iota(i32, (BOTTLENECK, flat), 0)
    repeat = jnp.zeros(cycle.shape, f32)
    for a in range(ADAPTERS):
        repeat = repeat + (cycle == a * BOTTLENECK).astype(f32)
    bias_row = jnp.sum(mm(down_bias[...], repeat.astype(bf16)) * spread, axis=0, keepdims=True)
    bias_ref[...] = jnp.broadcast_to(bias_row, bias_ref.shape)


def forward_kernel(own, ids, early, c2, x_ref, o2, vecs, message, in0, in1, back0, back1, *rest):
    if own:
        inner_ref, down_bias, part_ref, slope, slope_two, first_ref, normed_ref, factor_ref, *constants = rest
    else:
        part_ref, inner_ref = rest
    share = early.shape[0] // 2
    t = 0 if own else 1
    attn = early[t * share : (t + 1) * share, :] + mm(c2[...], o2[...])
    vec = vecs[...].astype(f32)
    start = pl.multiple_of(ids[2 if own else 3] * share, share)
    normed, factor = norm_parts(attn + vec[0:1] + x_ref[pl.ds(start, share), :].astype(f32))
    first = normed * vec[1:2] + vec[2:3]
    low = first.astype(bf16)
    part = jnp.zeros(first.shape, f32)
    units = in0.shape[1]
    chunk = units
    for j, (w_in, bias, w_back) in enumerate(((in0, vec[8:9], back0), (in1, message[0:1, :], back1))):
        for at in range(0, units, chunk):
            here = slice(at, at + chunk)
            columns = slice(j * units + at, j * units + at + chunk)
            inner = mm(low, w_in[:, here]) + bias[:, here]
            if own:
                act, bend = gelu_both(inner)
                slope[:, columns] = bend.astype(bf16)
                slope_two[:, columns] = gelu_both(inner_ref[:, columns])[1].astype(bf16)
            else:
                act = 0.5 * inner * (1.0 + lax.erf(inner * ROOT_HALF))
                inner_ref[:, columns] = inner
            part = part + mm(act.astype(bf16), w_back[here, :])
    part_ref[...] = part.astype(part_ref.dtype)
    if own:
        first_ref[...] = first
        normed_ref[...] = normed
        factor_ref[...] = jnp.broadcast_to(factor, factor_ref.shape)
        adapter_constants(down_bias, *constants)


def forward_rows(own, ids, early, c2, x, o2, vecs, message, w_ins, w_backs, share, *more):
    model = x.shape[1]
    units = w_ins[0].shape[1]
    slope = ((share, 2 * units), bf16)
    flat = ADAPTERS * BOTTLENECK
    if own:
        outputs = [((share, model), f32), slope, slope] + [((share, model), f32)] * 2 + [((share, 128), f32)]
        outputs += [((flat, ADAPTERS), bf16), ((ADAPTERS, flat), bf16), ((8, flat), f32)]
    else:
        outputs = [((share, model), bf16), ((share, 2 * units), f32)]
    return run(
        functools.partial(forward_kernel, own),
        (ids,),
        [early, c2, x, o2, vecs, message, *w_ins, *w_backs, *more],
        outputs,
        vmem=16,
        micros=3.0,
    )


def backward_kernel(gp, slope, back0, back1, in0, in1, part_ref):
    grad = gp[...]
    units = in0.shape[1]
    part = jnp.zeros(grad.shape, f32)
    for j, (w_back, w_in) in enumerate(((back0, in0), (back1, in1))):
        bend = slope[:, j * units : (j + 1) * units].astype(f32)
        inner = (bend * mm_nt(grad, w_back[...])).astype(bf16)
        part = part + mm_nt(inner, w_in[...])
    part_ref[...] = part.astype(part_ref.dtype)


def backward_rows(grad, slope, w_backs, w_ins, dtype):
    share, model = grad.shape
    units = w_ins[0].shape[1]
    return run(
        backward_kernel,
        (),
        [grad, slope, *w_backs, *w_ins],
        [((share, model), dtype)],
    )


def first_norm_kernel(own, got, gpre2, normed, factor, vecs, o0, o1, o2, o3, gpre1, c0, c1, c2, c3):
    grad = own[...] + got[...].astype(f32) + gpre2[...]
    grad = norm_back(grad, normed[...], factor[:, 0:1], vecs[...].astype(f32)[1:2])
    gpre1[...] = grad
    low = grad.astype(bf16)
    for c, o in ((c2, o2), (c3, o3), (c1, o1), (c0, o0)):
        c[...] = mm_nt(low, o[...]).astype(bf16)


def first_norm_back(own, got, gpre2, normed, factor, vecs, outs):
    share, model = own.shape
    width = outs[0].shape[0]
    return run(
        first_norm_kernel,
        (),
        [own, got, gpre2, normed, factor, vecs, *outs],
        [((share, model), f32)] + [((share, width), bf16)] * 4,
    )


def adapter_kernel(
    slots, ids, own, got, first_ref, cot, weight, count, vecs, member_ref, spread_ref, bias_ref, up_bias, down, up,
    wq, wk, wv,
    out_hbm, keep, give, sums, turn_ref, reduced_ref, mix_ref, base_ref, normed_ref, factor_ref, layer_out, lefts, sem,
):
    flat, model = up.shape
    vec = vecs[...].astype(f32)
    member = member_ref[...]
    spread = spread_ref[...]
    inv_root = model ** (-0.5)
    scale = 0.5 * slots / jnp.maximum(count[0:1, 0:1], 1.0)

    normed_two, factor_two = norm_parts(own[...] + got[...].astype(f32) + vec[3:4] + first_ref[...])
    normed_ref[...] = normed_two
    factor_ref[...] = jnp.broadcast_to(factor_two, factor_ref.shape)
    second = normed_two * vec[4:5] + vec[5:6]
    second_low = second.astype(bf16)
    query_key = mm_nt(mm(second_low, wq[...]).astype(bf16), wk[...]) * inv_root
    query_key_low = query_key.astype(bf16)
    lift_key = mm_nt(query_key_low, up[...])
    reduced = mm_nt(second_low, down[...]) + bias_ref[0:1, :]
    reduced_ref[...] = reduced
    squeezed = 0.5 * reduced * (1.0 + lax.erf(reduced * ROOT_HALF))
    squeezed = squeezed.astype(bf16).astype(f32)
    logits = (
        mm((squeezed * lift_key).astype(bf16), member)
        + mm_nt(query_key_low, up_bias[...])
        + jnp.sum(query_key * second, axis=-1, keepdims=True)
    )
    shifted = logits - jnp.max(logits, axis=-1, keepdims=True)
    log_probs = shifted - jnp.log(jnp.sum(jnp.exp(shifted), axis=-1, keepdims=True))
    joining = jnp.exp(log_probs)
    entropy = -jnp.sum(joining * log_probs, axis=-1, keepdims=True)
    total = jnp.sum(joining, axis=-1, keepdims=True)
    joining_low = joining.astype(bf16)
    joining_wide = mm(joining_low, spread)
    joined_low = (joining_wide * squeezed).astype(bf16)
    mixed = total * second + mm(joined_low, up[...]) + mm(joining_low, up_bias[...])
    mixed_low = mixed.astype(bf16)
    normed_join, factor_join = norm_parts(second + mm(mixed_low, wv[...]))
    grad_out = cot[...].astype(f32)
    grad_pref = norm_back(grad_out, normed_join, factor_join, vec[6:7])
    grad_pref_low = grad_pref.astype(bf16)
    back_value = mm_nt(grad_pref_low, wv[...])
    back_value_low = back_value.astype(bf16)
    lift_value = mm_nt(back_value_low, up[...])
    grad_probs = (
        mm((squeezed * lift_value).astype(bf16), member)
        + mm_nt(back_value_low, up_bias[...])
        + jnp.sum(back_value * second, axis=-1, keepdims=True)
    )
    mean_grad = jnp.sum(joining * grad_probs, axis=-1, keepdims=True)
    grad_logits = joining * (grad_probs - mean_grad) - scale * weight[...] * joining * (log_probs + entropy)
    logits_low = grad_logits.astype(bf16)
    grad_wide = mm(logits_low, spread)
    logit_sum = jnp.sum(grad_logits, axis=-1, keepdims=True)
    turned = (
        logit_sum * second + mm((grad_wide * squeezed).astype(bf16), up[...]) + mm(logits_low, up_bias[...])
    ) * inv_root
    turned_low = turned.astype(bf16)
    turn_ref[...] = turned_low

    layer_out[...] = normed_join * vec[6:7] + vec[7:8]
    copy = pltpu.make_async_copy(layer_out, out_hbm, sem)
    copy.start()
    small = jnp.concatenate(
        [
            jnp.sum(grad_out * normed_join, axis=0, keepdims=True),
            jnp.sum(grad_out, axis=0, keepdims=True),
            jnp.zeros((sums.shape[0] - 2, model), f32),
        ],
        axis=0,
    )
    sums[...] = small
    write_small(give, small)
    mix_ref[...] = grad_wide * lift_key + joining_wide * lift_value
    base_ref[...] = grad_pref + logit_sum * query_key + total * back_value

    half = model // 2
    lefts[0] = second_low
    lefts[1] = mixed_low
    for j, right in enumerate((turned_low, grad_pref_low)):
        rows = slice(j * half, (j + 1) * half)
        other = lefts[j, :, pl.ds(pl.multiple_of((1 - ids[6]) * half, 128), half)]
        give[rows, :] = mm_tn(other, right).astype(bf16)
        mine = lefts[j, :, pl.ds(pl.multiple_of(ids[6] * half, 128), half)]
        keep[rows, :] = mm_tn(mine, right).astype(bf16)
    copy.wait()


def adapters(slots, ids, arrays):
    share, model = arrays[0].shape
    flat = ADAPTERS * BOTTLENECK
    wide, flat_wide = ((share, model), f32), ((share, flat), f32)
    return run(
        functools.partial(adapter_kernel, slots),
        (ids,),
        arrays,
        [
            ((share, model), f32, None),
            ((model, model), bf16),
            ((model + 16, model), bf16),
            ((8, model), f32),
            ((share, model), bf16),
            flat_wide,
            flat_wide,
            wide,
            wide,
            ((share, 128), f32),
        ],
        scratch=[
            pltpu.VMEM((share, model), f32),
            pltpu.VMEM((2, share, model), bf16),
            pltpu.SemaphoreType.DMA,
        ],
        vmem=20,
        micros=8.0,
    )


def adapter_rest_kernel(turn, reduced, mix, base, normed, factor, vecs, down, wq, wk, gpre2_ref, gpre2_low):
    grad_query_f = mm(turn[...], wk[...]).astype(bf16)
    grad_reduced = (gelu_both(reduced[...])[1] * mix[...]).astype(bf16)
    grad_second = base[...] + mm(grad_reduced, down[...]) + mm_nt(grad_query_f, wq[...])
    grad_pre2 = norm_back(grad_second, normed[...], factor[:, 0:1], vecs[4:5, :])
    gpre2_ref[...] = grad_pre2
    gpre2_low[...] = grad_pre2.astype(bf16)


def write_small(message, sums):
    high, low = halves_of(sums)
    rows = message.shape[0] - 16
    message[rows:, :] = jnp.concatenate([high, low], axis=0)


def read_small(message):
    rows = message.shape[0] - 16
    both = message[rows:, :].astype(f32)
    return both[:8] + both[8:]


def fold_kernel(base, start, split, last, ids, *refs):
    if start:
        keep, got, sums, *outs = refs
        rows = keep.shape[0] // 2
        pieces = [(keep, got, j * rows) for j in range(2)]
    else:
        *arrays, sums = refs[:5]
        outs = refs[5:]
        rows = arrays[0].shape[0]
        pieces = [(arrays[2 * j], arrays[2 * j + 1], 0) for j in range(2)]
        got = arrays[3]
    total = sums[...] + read_small(got)
    outs[-1][...] = total
    for j, (mine, other, at) in enumerate(pieces):
        def both(where):
            return (mine[where, :].astype(f32) + other[where, :].astype(f32)).astype(bf16)

        if split:
            half = rows // 2
            bit = ids[base + j]
            outs[2 * j][...] = both(pl.ds(pl.multiple_of(at + bit * half, 16), half))
            outs[2 * j + 1][:half, :] = both(pl.ds(pl.multiple_of(at + (1 - bit) * half, 16), half))
        elif last:
            outs[j][...] = both(pl.ds(at, rows))
        else:
            whole = both(pl.ds(at, rows))
            outs[2 * j][...] = whole
            outs[2 * j + 1][:rows, :] = whole
    if not last:
        write_small(outs[3], total)


def fold(ids, base, start, split, arrays, rows, sums, last=False):
    model = sums.shape[1]
    rows = rows // 2 if split else rows
    outputs = []
    for j in range(2):
        outputs += [((rows, model), bf16)] + ([] if last else [((rows + 16 * j, model), bf16)])
    outputs.append((sums.shape, f32))
    outs = run(functools.partial(fold_kernel, base, start, split, last), (ids,), [*arrays, sums], outputs)
    if last:
        return outs[:2], None, outs[2]
    return outs[0:4:2], outs[1:4:2], outs[4]


def join_kernel(base, last, ids, *refs):
    outs = refs[4:]
    for j in range(2):
        mine, got = refs[2 * j : 2 * j + 2]
        rows = mine.shape[0]
        bit = ids[base + j]
        out, at = (outs[0], 2 * rows * j) if last else (outs[j], 0)
        out[pl.ds(pl.multiple_of(at + bit * rows, 16), rows), :] = mine[...]
        out[pl.ds(pl.multiple_of(at + (1 - bit) * rows, 16), rows), :] = got[...]


def join(ids, base, last, mine, gots):
    rows, model = mine[0].shape
    outputs = [((4 * rows, model), bf16)] if last else [((2 * rows, model), bf16)] * 2
    arrays = [a for pair in zip(mine, gots) for a in pair]
    return run(functools.partial(join_kernel, base, last), (ids,), arrays, outputs)


def finish_kernel(first, ids, source, wq, wk, *refs):
    half = source.shape[0] // 2
    if first:
        part_own, part_got, out_q, out_v, key_part, out_x, stage, stage_x, sems = refs
    else:
        key_before, _, _, out_q, out_v, out_k, stage, stage_k, sems = refs
    core = ids[6] if first else 1 - ids[6]
    rows = pl.ds(pl.multiple_of(core * half, half), half)
    copies = []

    def send(j, source, target):
        copies.append(pltpu.make_async_copy(source, target, sems.at[j]))
        copies[-1].start()

    if first:
        stage_x[...] = part_own[...] + part_got[...].astype(f32)
        send(3, stage_x, out_x)
    mixed = source[:half, :]
    key = mm_tn(mixed, wq[rows, :])
    if first:
        key_part[...] = key
    else:
        stage_k[...] = key_before[...] + key
        send(2, stage_k, out_k)
    stage[1] = source[half:, :].astype(f32)
    send(1, stage.at[1], out_v.at[rows, :])
    stage[0] = mm(mixed, wk[...])
    send(0, stage.at[0], out_q.at[rows, :])
    for copy in copies:
        copy.wait()


def finish(ids, source, wq, wk, before, parts=()):
    model = source.shape[1]
    half = source.shape[0] // 2
    first = before is None
    vmem_spec = pl.BlockSpec(memory_space=pltpu.VMEM)
    any_spec = pl.BlockSpec(memory_space=pl.ANY)
    whole = jax.ShapeDtypeStruct((model, model), f32)
    inputs = [source, wq, wk, *(parts if first else [before[2]])]
    if first:
        out_specs = [any_spec, any_spec, vmem_spec, any_spec]
        shape = parts[0].shape
        out_shape = [whole, whole, pltpu.VMEM((model, model), f32), jax.ShapeDtypeStruct(shape, f32)]
    else:
        out_specs, shape, out_shape = [any_spec] * 3, (model, model), [whole] * 3
    return pl.pallas_call(
        functools.partial(finish_kernel, first),
        in_specs=[pl.BlockSpec(memory_space=pltpu.SMEM)]
        + [vmem_spec] * len(inputs)
        + ([] if first else [any_spec] * 2),
        out_specs=out_specs,
        out_shape=out_shape,
        input_output_aliases={} if first else {5: 0, 6: 1},
        scratch_shapes=[
            pltpu.VMEM((2, half, model), f32),
            pltpu.VMEM(shape, f32),
            pltpu.SemaphoreType.DMA((4,)),
        ],
        compiler_params=pltpu.CompilerParams(vmem_limit_bytes=16 * 1024 * 1024),
        cost_estimate=pl.CostEstimate(flops=int(2 * FLOPS), bytes_accessed=1, transcendentals=0),
    )(ids, *[pltpu.with_memory_space_constraint(a, pltpu.VMEM) for a in inputs], *([] if first else before[:2]))


def chip_kernel(near, got, gpre1, keep, give):
    share = keep.shape[0]
    give[...] = (near[share:, :] + got[share:, :].astype(f32)).astype(bf16)
    keep[...] = near[:share, :] + got[:share, :].astype(f32) + gpre1[...]


def body(
    layer_input,
    cotangent,
    seq_lens,
    seq_place,
    loss_mask,
    w_qkv,
    b_qv,
    w_out,
    b_out,
    ln1_gain,
    ln1_bias,
    w_in,
    b_in,
    w_back,
    b_back,
    ln2_gain,
    ln2_bias,
    ad_down,
    ad_down_bias,
    ad_up,
    ad_up_bias,
    join_query,
    join_key,
    join_value,
    join_gain,
    join_bias,
):
    group_rows, model = layer_input.shape
    share = cotangent.shape[0]
    rank = lax.axis_index("tp")
    dp_rank = lax.axis_index("dp")
    total_slots = group_rows * lax.axis_size("dp")

    core, near_x = ("tp", 1), ("tp", 2)
    others = []
    bit = 1
    while bit < lax.axis_size("dp"):
        others.append(("dp", bit))
        bit *= 2
    streams = [
        [others[0], *others[1:], near_x],
        [*others[1:2], others[0], near_x, *others[2:]],
    ]

    def bit_of(axis, which):
        return (lax.axis_index(axis) // which) % 2

    ids = [rank, dp_rank] + [rank ^ j for j in ORDER] + [bit_of(*core)]
    for at in range(len(others) + 1):
        ids += [bit_of(*stream[at]) for stream in streams]
    ids = jnp.stack(ids).astype(i32)
    ids = jnp.concatenate([ids, jnp.zeros(HEADER - ids.shape[0], i32), seq_lens, seq_place])
    vectors = [b_out, ln1_gain, ln1_bias, b_back, ln2_gain, ln2_bias, join_gain, join_bias, b_in]

    outs = [w_out, swap(w_out, "tp", 1), swap(w_out, "tp", 2)]
    outs.append(None)
    w_ins = [w_in, swap(w_in, "tp", 1)]
    w_backs = [w_back, swap(w_back, "tp", 1)]

    width = w_qkv.shape[2]
    w_t = jnp.transpose(w_qkv, (1, 2, 0)).reshape(3 * width, model)
    q, k, v, message = project(ids, layer_input, w_t, b_qv, loss_mask, b_in)
    message_got = swap(message, *core)
    far, e_far, rl_far = attend(2, 2, ids, q, k, v, share)
    far, message_got, outs[1], outs[2], w_ins[1], w_backs[1] = tie(
        far, message_got, *outs[1:3], w_ins[1], w_backs[1]
    )
    outs[3] = swap(outs[2], "tp", 1)
    c1, c3 = swap(far, "tp", 1), swap(far, "tp", 3)
    counted = message[1:2, :128] + message_got[1:2, :128]
    count_got = swap(counted, *near_x)
    q_near, _ = tie(q, far)
    near, e_near, rl_near = attend(0, 1, ids, q_near, k, v, share)
    c2_far = swap(near, *near_x)
    near, outs[3], c1 = tie(near, outs[3], c1)
    q_beside, _ = tie(q, near)
    beside, e_beside, rl_beside = attend(1, 1, ids, q_beside, k, v, share)
    c2_own = swap(beside, *near_x)
    early, vecs, weight_m = early_part(
        ids, [near, beside, c1, c3, outs[0], outs[1], outs[3]], loss_mask, vectors, share
    )

    give, inner = forward_rows(
        False, ids, early, c2_far, layer_input, outs[2], vecs, message_got, w_ins, w_backs, share
    )
    ffn_got = swap(give, *near_x)
    give, count_got = tie(give, count_got)
    counted = counted + count_got
    count_got = swap(counted, *others[0])
    own, slope_one, slope_two, first, normed_one, factor_one, *constants = forward_rows(
        True, ids, early, c2_own, layer_input, outs[2], vecs, message_got, w_ins, w_backs, share, inner,
        ad_down_bias,
    )
    own, count_got = tie(own, count_got)
    counted = counted + count_got
    pair = [bit for _, bit in others[1:3]]
    count_gots = [swap(counted, "dp", bit) for bit in [*pair, *([sum(pair)] if len(pair) == 2 else [])]]
    counted = sum(count_gots, counted)
    for axis, which in others[3:]:
        counted = counted + swap(counted, axis, which)

    flat = ADAPTERS * BOTTLENECK
    down_t = jnp.transpose(ad_down, (1, 2, 0)).reshape(flat, model)
    up = ad_up.reshape(flat, model)
    layer_out, keep, give, sums, turn, reduced, mix, base, normed_two, factor_two = adapters(
        total_slots,
        ids,
        [
            own, ffn_got, first, cotangent, weight_m, counted, vecs, *constants, ad_up_bias, down_t, up,
            join_query, join_key, join_value,
        ],
    )
    got = swap(give, *core)
    gpre2, gpre2_low = run(
        adapter_rest_kernel,
        (),
        [turn, reduced, mix, base, normed_two, factor_two, vecs, down_t, join_query, join_key],
        [((share, model), f32), ((share, model), bf16)],
    )
    gpre2_got = swap(gpre2_low, "tp", 2)

    state = {"at": 0, "history": [], "rows": keep.shape[0] // 2}

    def sum_step(keeps, gots, sums):
        at = state["at"]
        start = at == 0
        split = state["rows"] // 2 >= LEAST_ROWS
        arrays = [keeps, gots] if start else [a for pair in zip(keeps, gots) for a in pair]
        keeps, gives, sums = fold(ids, 7 + 2 * at, start, split, arrays, state["rows"], sums)
        if split:
            state["rows"] //= 2
            state["history"].append(at)
        state["at"] = at + 1
        return keeps, [swap(g, *stream[at]) for g, stream in zip(gives, streams)], sums

    (back_own,) = backward_rows(gpre2_low, slope_one, w_backs, w_ins, f32)
    back_own, got = tie(back_own, got)
    keeps, gots, sums = sum_step(keep, got, sums)
    keeps[0], gpre2_got = tie(keeps[0], gpre2_got)
    (back_give,) = backward_rows(gpre2_got, slope_two, w_backs, w_ins, bf16)
    back_give, *gots = tie(back_give, *gots)
    keeps, gots, sums = sum_step(keeps, gots, sums)
    keeps[0], back_give = tie(keeps[0], back_give)
    back_got = swap(back_give, "tp", 2)
    keeps, gots, sums = sum_step(keeps, gots, sums)
    keeps[0], back_got = tie(keeps[0], back_got)
    gpre1, c0, c1, c2, c3 = first_norm_back(back_own, back_got, gpre2, normed_one, factor_one, vecs, outs)
    c2, c3, c1 = swap(c2, "tp", 2), swap(c3, "tp", 3), swap(c1, "tp", 1)
    shared = ((near, beside, far), (e_near, e_beside, e_far), (rl_near, rl_beside, rl_far), (q, k, v))
    before = list(attend_back((0,), ids, (c0,), *shared, [], None, share))
    before[0], *gots = tie(before[0], *gots)
    keeps, gots, sums = sum_step(keeps, gots, sums)
    before[0], keeps[0] = tie(before[0], keeps[0])
    far_part, near_part = attend_back((2, 1, 3), ids, (c1, c2, c3), *shared, before, w_t, share)
    far_part, *gots = tie(far_part, *gots)
    far_got = swap(far_part, "tp", 1)
    while state["at"] < len(others) + 1:
        keeps, gots, sums = sum_step(keeps, gots, sums)
    arrays = [a for pair in zip(keeps, gots) for a in pair]
    keeps, _, sums = fold(ids, 0, False, False, arrays, state["rows"], sums, last=True)
    gain_grad, bias_grad = sums[0], sums[1]
    part_own, part_give = run(
        chip_kernel, (), [near_part, far_got, gpre1], [((share, model), f32), ((share, model), bf16)]
    )
    part_got = swap(part_give, "tp", 2)
    for at in reversed(state["history"]):
        gots = [swap(a, *stream[at]) for a, stream in zip(keeps, streams)]
        gots[0], part_own, gain_grad, bias_grad = tie(gots[0], part_own, gain_grad, bias_grad)
        keeps = join(ids, 7 + 2 * at, at == 0, keeps, gots)
    keeps[0], part_got = tie(keeps[0], part_got)
    got = swap(keeps[0], *core)
    *part, input_grad = finish(ids, keeps[0], join_query, join_key, None, (part_own, part_got))
    query_grad, value_grad, key_grad = finish(ids, got, join_query, join_key, part)
    return (layer_out, input_grad, query_grad, key_grad, value_grad, gain_grad, bias_grad)


def solution(mesh):
    placed = (
        P("dp", None),
        P(("dp", "tp"), None),
        P(),
        P(),
        P(("dp", "tp")),
        P(None, None, "tp"),
        P(None, "tp"),
        P("tp", None),
        P(),
        P(),
        P(),
        P(None, "tp"),
        P("tp"),
        P("tp", None),
        P(),
        P(),
        P(),
        P(),
        P(),
        P(),
        P(),
        P(),
        P(),
        P(),
        P(),
        P(),
    )
    return jax.shard_map(
        body,
        mesh=mesh,
        in_specs=placed,
        out_specs=(P(("dp", "tp"), None), P(("dp", "tp"), None), P(), P(), P(), P(), P()),
        check_vma=False,
    )
```

```python
import functools

import jax
import jax.numpy as jnp
from jax import lax
from jax.experimental import pallas as pl
from jax.experimental.pallas import tpu as pltpu
from jax.sharding import PartitionSpec as P

HEAD_DIM = 64
ADAPTERS = 16
BOTTLENECK = 48
SEQ_GRP = 4
LEAST_ROWS = 96
FLOPS = 1.15e9

EPS = 1e-06
NEG = -1e30
ROOT_HALF = 0.7071067811865476
INV_ROOT_TAU = 0.3989422804014327

f32 = jnp.float32
bf16 = jnp.bfloat16
i32 = jnp.int32

HEADER = 64

ORDER = (0, 2, 1, 3)


def gelu_both(values):
    phi = 0.5 * (1.0 + lax.erf(values * ROOT_HALF))
    return values * phi, phi + values * jnp.exp(-0.5 * values * values) * INV_ROOT_TAU


def row_mean(values):
    return jnp.sum(values, axis=-1, keepdims=True) * (1.0 / values.shape[-1])


def norm_parts(values):
    center = values - row_mean(values)
    factor = lax.rsqrt(row_mean(center * center) + EPS)
    return center * factor, factor


def norm_back(gradient, normed, factor, gain_vec):
    scaled = gradient * gain_vec
    return factor * (scaled - row_mean(scaled) - normed * row_mean(scaled * normed))


def mm(a, b):
    return lax.dot_general(a, b, (((1,), (0,)), ((), ())), preferred_element_type=f32)


def mm_nt(a, b):
    return lax.dot_general(a, b, (((1,), (1,)), ((), ())), preferred_element_type=f32)


def mm_tn(a, b):
    return lax.dot_general(a, b, (((0,), (0,)), ((), ())), preferred_element_type=f32)


def halves_of(a):
    high = a.astype(bf16)
    return high, (a - high.astype(f32)).astype(bf16)


def swap(value, axis, bit):
    size = lax.axis_size(axis)
    return lax.ppermute(value, axis, [(i, i ^ bit) for i in range(size)])


def tie(*values):
    return lax.optimization_barrier(values)


def run(kernel, scalars, inputs, outputs, streamed=(), scratch=(), vmem=12, micros=0.1):
    smem = pl.BlockSpec(memory_space=pltpu.SMEM)
    vmem_spec = pl.BlockSpec(memory_space=pltpu.VMEM)
    any_spec = pl.BlockSpec(memory_space=pl.ANY)
    outs = pl.pallas_call(
        kernel,
        in_specs=[smem] * len(scalars) + [vmem_spec] * len(inputs) + [any_spec] * len(streamed),
        out_specs=[vmem_spec if len(o) == 2 else any_spec for o in outputs],
        out_shape=[pltpu.VMEM(*o) if len(o) == 2 else jax.ShapeDtypeStruct(*o[:2]) for o in outputs],
        scratch_shapes=list(scratch),
        compiler_params=pltpu.CompilerParams(vmem_limit_bytes=vmem * 1024 * 1024),
        cost_estimate=pl.CostEstimate(flops=int(micros * FLOPS), bytes_accessed=1, transcendentals=0),
    )(
        *scalars,
        *[pltpu.with_memory_space_constraint(a, pltpu.VMEM) for a in inputs],
        *[pltpu.with_memory_space_constraint(a, pltpu.HBM) for a in streamed],
    )
    return list(outs)


def head_mask(width, head):
    lane = lax.broadcasted_iota(i32, (1, width), 1)
    return (lane >= head * HEAD_DIM) & (lane < (head + 1) * HEAD_DIM)


def group_ends(ints):
    count = (ints.shape[0] - HEADER) // 2

    def add(s, ends):
        spot = ints[HEADER + count + s] - ints[1] * SEQ_GRP
        length = jnp.where(spot >= 0, ints[HEADER + s], 0)
        return tuple(e + jnp.where(spot <= j, length, 0) for j, e in enumerate(ends))

    return lax.fori_loop(0, count, add, (jnp.int32(0),) * SEQ_GRP, unroll=8)


def segment_of(positions, ends):
    segment = jnp.zeros(positions.shape, i32)
    for e in ends:
        segment = segment + (positions >= e).astype(i32)
    return jnp.where(positions < ends[-1], segment, SEQ_GRP + positions)


def window(rows, start, ends, group_rows):
    low = jnp.int32(0)
    high = jnp.int32(0)
    last = start + rows - 1
    for e in ends:
        low = jnp.where(start >= e, jnp.maximum(low, e), low)
    for e in reversed(ends):
        high = jnp.where(last < e, e, high)
    padded = last >= ends[-1]
    low = jnp.where(start >= ends[-1], start, low)
    high = jnp.where(padded, start + rows, high)
    low = jnp.minimum(low // 128 * 128, group_rows - 128)
    return low, high - low


def by_window(rows, start, ends, group_rows, act):
    low, span = window(rows, start, ends, group_rows)
    widths = [w for w in (512,) if w < group_rows] + [group_rows]
    least = 0
    for w in widths:
        fits = (span > least) & (span <= w) if w < group_rows else span > least

        @pl.when(fits)
        def _(w=w):
            act(pl.multiple_of(jnp.minimum(low, group_rows - w), 128), w)

        least = w


def one_row(tile):
    return jnp.concatenate([tile[j : j + 1, :] for j in range(tile.shape[0])], axis=1)


def real_row(ids, mask):
    row = one_row(mask[...].astype(f32))
    lane = lax.broadcasted_iota(i32, row.shape, 1)
    return jnp.where(ids[0] * row.shape[1] + lane < group_ends(ids)[-1], row, 0.0)


def project_kernel(
    ids, x_hbm, w_hbm, bias_hbm, mask_hbm, b_in_hbm, q_ref, k_ref, v_ref, message, x_ref, w_ref, bias_ref, mask_ref,
    b_in_ref, sems,
):
    group_rows, width = q_ref.shape
    chunks = 4
    share = group_rows // chunks
    pairs = [(w_hbm, w_ref), (bias_hbm, bias_ref)]
    for c in range(chunks):
        rows = pl.ds(c * share, share)
        pairs.append((x_hbm.at[rows, :], x_ref.at[rows, :]))
    pairs += [(mask_hbm, mask_ref), (b_in_hbm, b_in_ref)]
    copies = [pltpu.make_async_copy(source, target, sems.at[j]) for j, (source, target) in enumerate(pairs)]
    for copy in copies:
        copy.start()
    copies[0].wait()
    copies[1].wait()
    bias = bias_ref[...].astype(f32)
    for c in range(chunks):
        rows = slice(c * share, (c + 1) * share)
        copies[2 + c].wait()
        x = x_ref[rows, :]
        k_ref[rows, :] = mm_nt(x, w_ref[width : 2 * width, :]).astype(bf16)
        v_ref[rows, :] = (mm_nt(x, w_ref[2 * width :, :]) + bias[1:2]).astype(bf16)
        q = (mm_nt(x, w_ref[:width, :]) + bias[0:1]).astype(bf16)
        q_ref[rows, :] = (q.astype(f32) * HEAD_DIM ** (-0.5)).astype(bf16)
    for copy in copies[2 + chunks :]:
        copy.wait()
    message[0:1, :] = one_row(b_in_ref[...].astype(f32))
    total = jnp.sum(real_row(ids, mask_ref), axis=-1, keepdims=True)
    message[1:, :] = jnp.broadcast_to(total, (message.shape[0] - 1, message.shape[1]))


def project(ids, x, w_t, b_qv, mask, b_in):
    group_rows, model = x.shape
    width = w_t.shape[0] // 3
    streamed = [x, w_t, b_qv, mask.reshape(-1, 128), b_in.reshape(-1, 128)]
    return run(
        project_kernel,
        (ids,),
        [],
        [((group_rows, width), bf16)] * 3 + [((8, model), f32)],
        streamed=streamed,
        scratch=[pltpu.VMEM(a.shape, a.dtype) for a in streamed] + [pltpu.SemaphoreType.DMA((8,))],
        micros=3.0,
    )


def attend_kernel(first, blocks, ids, q_ref, k_ref, v_ref, *refs):
    context_ref, e_ref, rl_ref = refs
    rows = rl_ref.shape[0] // blocks
    group_rows, width = k_ref.shape
    heads = width // HEAD_DIM
    ends = group_ends(ids)

    def one(t, carry):
        start = pl.multiple_of(ids[2 + first + t] * rows, rows)
        at = pl.multiple_of(t * rows, rows)

        def act(key0, w):
            q = q_ref[pl.ds(start, rows), :].astype(f32)
            seg_q = segment_of(start + lax.broadcasted_iota(i32, (rows, 1), 0), ends)
            seg_k = segment_of(key0 + lax.broadcasted_iota(i32, (1, w), 1), ends)
            k = k_ref[pl.ds(key0, w), :]
            v = v_ref[pl.ds(key0, w), :]
            context = jnp.zeros((rows, width), f32)
            wide = jnp.zeros((rows, width), f32)
            for h in range(heads):
                mask = head_mask(width, h)
                scores = mm_nt(jnp.where(mask, q, 0.0).astype(bf16), k)
                scores = jnp.where(seg_q == seg_k, scores, NEG)
                e = jnp.exp(scores - jnp.max(scores, axis=-1, keepdims=True))
                inverse = 1.0 / jnp.sum(e, axis=-1, keepdims=True)
                low = e.astype(bf16)
                e_ref[pl.ds(pl.multiple_of((t * heads + h) * rows, rows), rows), :w] = low
                context = jnp.where(mask, mm(low, v) * inverse, context)
                wide = jnp.where(mask, inverse, wide)
            rl_ref[pl.ds(at, rows), :] = wide
            context_ref[pl.ds(at, rows), :] = context.astype(bf16)

        by_window(rows, start, ends, group_rows, act)
        return carry

    lax.fori_loop(0, blocks, one, 0)


def attend(first, blocks, ids, q, k, v, share):
    group_rows, width = k.shape
    heads = width // HEAD_DIM
    return run(
        functools.partial(attend_kernel, first, blocks),
        (ids,),
        [q, k, v],
        [
            ((blocks * share, width), bf16),
            ((blocks * heads * share, group_rows), bf16),
            ((blocks * share, width), f32),
        ],
        vmem=20,
        micros=3.0 if first else 0.1,
    )


def attend_back_kernel(spots, first, last, ids, *refs):
    count = len(spots)
    grads, refs = refs[:count], refs[count:]
    contexts, es, rls, refs = refs[0:3], refs[3:6], refs[6:9], refs[9:]
    q_ref, k_ref, v_ref, refs = refs[0], refs[1], refs[2], refs[3:]
    if not first:
        before, refs = refs[:3], refs[3:]
    if last:
        w_ref, far_out, near_out, gq, gk, gv = refs
    else:
        gq, gk, gv = refs
    rows = grads[0].shape[0]
    group_rows, width = k_ref.shape
    heads = width // HEAD_DIM
    ends = group_ends(ids)
    if first:
        gk[...] = jnp.zeros_like(gk)
        gv[...] = jnp.zeros_like(gv)
    else:
        gq[...] = before[0][...]
        gk[...] = before[1][...]
        gv[...] = before[2][...]
    for g_ref, spot in zip(grads, spots):
        start = pl.multiple_of(ids[2 + spot] * rows, rows)
        part, t = (spot, 0) if spot < 2 else (2, spot - 2)
        g = g_ref[...].astype(f32) * rls[part][t * rows : (t + 1) * rows, :]
        dots = g * contexts[part][t * rows : (t + 1) * rows, :].astype(f32)
        q = q_ref[pl.ds(start, rows), :].astype(f32)

        def act(key0, w, g=g, dots=dots, q=q, part=part, t=t, start=start):
            keys = pl.ds(key0, w)
            k = k_ref[keys, :]
            v = v_ref[keys, :]
            out = jnp.zeros((rows, width), f32)
            add_k = jnp.zeros((w, width), f32)
            add_v = jnp.zeros((w, width), f32)
            for h in range(heads):
                mask = head_mask(width, h)
                g_head = jnp.where(mask, g, 0.0).astype(bf16)
                e = es[part][(t * heads + h) * rows : (t * heads + h + 1) * rows, :w]
                delta = jnp.sum(jnp.where(mask, dots, 0.0), axis=-1, keepdims=True)
                ds = (e.astype(f32) * (mm_nt(g_head, v) - delta)).astype(bf16)
                out = jnp.where(mask, mm(ds, k), out)
                add_k = add_k + mm_tn(ds, jnp.where(mask, q, 0.0).astype(bf16))
                add_v = add_v + mm_tn(e, g_head)
            gk[keys, :] += add_k
            gv[keys, :] += add_v
            gq[pl.ds(start, rows), :] = (out * HEAD_DIM ** (-0.5)).astype(bf16)

        by_window(rows, start, ends, group_rows, act)
    if last:
        for out, pair in ((far_out, (2, 3)), (near_out, (0, 1))):
            for t, spot in enumerate(pair):
                own = pl.ds(pl.multiple_of(ids[2 + spot] * rows, rows), rows)
                part = (
                    mm(gq[own, :], w_ref[:width, :])
                    + mm(gk[own, :].astype(bf16), w_ref[width : 2 * width, :])
                    + mm(gv[own, :].astype(bf16), w_ref[2 * width :, :])
                )
                out[t * rows : (t + 1) * rows, :] = part.astype(out.dtype)


def attend_back(spots, ids, grads, contexts, es, rls, qkv, before, w_t, share):
    group_rows, width = qkv[0].shape
    last = w_t is not None
    sums = [((group_rows, width), bf16), ((group_rows, width), f32), ((group_rows, width), f32)]
    inputs = [*grads, *contexts, *es, *rls, *qkv, *before]
    if last:
        model = w_t.shape[1]
        outputs = [((2 * share, model), bf16), ((2 * share, model), f32)]
        scratch = [pltpu.VMEM(*o) for o in sums]
        inputs.append(w_t)
    else:
        outputs, scratch = sums, []
    return run(
        functools.partial(attend_back_kernel, spots, not before, last),
        (ids,),
        inputs,
        outputs,
        scratch=scratch,
        vmem=20,
        micros=5.0 if last else 0.1,
    )


def early_kernel(ids, c0, x0, c1, c3, o0, o1, o3, *refs):
    mask_hbm, *vectors = refs[:10]
    out, vecs, weight, mask_ref, *tiles, sems = refs[10:]
    pairs = [(mask_hbm, mask_ref), *zip(vectors, tiles)]
    copies = [pltpu.make_async_copy(source, target, sems.at[j]) for j, (source, target) in enumerate(pairs)]
    for copy in copies:
        copy.start()
    share = out.shape[0] // 2
    attn = mm(c1[...], o1[...])
    for t, mine in enumerate((c0, x0)):
        rows = slice(t * share, (t + 1) * share)
        out[rows, :] = attn[rows] + mm(mine[...], o0[...]) + mm(c3[(1 - t) * share : (2 - t) * share, :], o3[...])
    for copy in copies:
        copy.wait()
    for j, tile in enumerate(tiles):
        vecs[j : j + 1, :] = one_row(tile[...].astype(f32))
    vecs[9:, :] = jnp.zeros((vecs.shape[0] - 9, vecs.shape[1]), f32)
    row = real_row(ids, mask_ref)
    here = lax.broadcasted_iota(i32, (share, share), 0) == lax.broadcasted_iota(i32, (share, share), 1)
    weight[...] = jnp.sum(jnp.where(here, jnp.broadcast_to(row, (share, share)), 0.0), axis=-1, keepdims=True)


def early_part(ids, arrays, mask, vectors, share):
    model = arrays[4].shape[1]
    streamed = [mask.reshape(-1, 128), *[v.reshape(-1, 128) for v in vectors]]
    return run(
        early_kernel,
        (ids,),
        arrays,
        [((2 * share, model), f32), ((16, model), f32), ((share, 1), f32)],
        streamed=streamed,
        scratch=[pltpu.VMEM(a.shape, a.dtype) for a in streamed] + [pltpu.SemaphoreType.DMA((len(streamed),))],
    )


def adapter_constants(down_bias, member_ref, spread_ref, bias_ref):
    flat = member_ref.shape[0]
    lane = lax.broadcasted_iota(i32, (flat, ADAPTERS), 0) - BOTTLENECK * lax.broadcasted_iota(
        i32, (flat, ADAPTERS), 1
    )
    member_ref[...] = ((lane >= 0) & (lane < BOTTLENECK)).astype(f32).astype(bf16)
    lane = lax.broadcasted_iota(i32, (ADAPTERS, flat), 1) - BOTTLENECK * lax.broadcasted_iota(
        i32, (ADAPTERS, flat), 0
    )
    spread = ((lane >= 0) & (lane < BOTTLENECK)).astype(f32)
    spread_ref[...] = spread.astype(bf16)
    cycle = lax.broadcasted_iota(i32, (BOTTLENECK, flat), 1) - lax.broadcasted_iota(i32, (BOTTLENECK, flat), 0)
    repeat = jnp.zeros(cycle.shape, f32)
    for a in range(ADAPTERS):
        repeat = repeat + (cycle == a * BOTTLENECK).astype(f32)
    bias_row = jnp.sum(mm(down_bias[...], repeat.astype(bf16)) * spread, axis=0, keepdims=True)
    bias_ref[...] = jnp.broadcast_to(bias_row, bias_ref.shape)


def forward_kernel(own, ids, early, c2, x_ref, o2, vecs, message, in0, in1, back0, back1, *rest):
    if own:
        inner_ref, down_bias, part_ref, slope, slope_two, first_ref, normed_ref, factor_ref, *constants = rest
    else:
        part_ref, inner_ref = rest
    share = early.shape[0] // 2
    t = 0 if own else 1
    attn = early[t * share : (t + 1) * share, :] + mm(c2[...], o2[...])
    vec = vecs[...].astype(f32)
    start = pl.multiple_of(ids[2 if own else 3] * share, share)
    normed, factor = norm_parts(attn + vec[0:1] + x_ref[pl.ds(start, share), :].astype(f32))
    first = normed * vec[1:2] + vec[2:3]
    low = first.astype(bf16)
    part = jnp.zeros(first.shape, f32)
    units = in0.shape[1]
    chunk = units
    for j, (w_in, bias, w_back) in enumerate(((in0, vec[8:9], back0), (in1, message[0:1, :], back1))):
        for at in range(0, units, chunk):
            here = slice(at, at + chunk)
            columns = slice(j * units + at, j * units + at + chunk)
            inner = mm(low, w_in[:, here]) + bias[:, here]
            if own:
                act, bend = gelu_both(inner)
                slope[:, columns] = bend.astype(bf16)
                slope_two[:, columns] = gelu_both(inner_ref[:, columns])[1].astype(bf16)
            else:
                act = 0.5 * inner * (1.0 + lax.erf(inner * ROOT_HALF))
                inner_ref[:, columns] = inner
            part = part + mm(act.astype(bf16), w_back[here, :])
    part_ref[...] = part.astype(part_ref.dtype)
    if own:
        first_ref[...] = first
        normed_ref[...] = normed
        factor_ref[...] = jnp.broadcast_to(factor, factor_ref.shape)
        adapter_constants(down_bias, *constants)


def forward_rows(own, ids, early, c2, x, o2, vecs, message, w_ins, w_backs, share, *more):
    model = x.shape[1]
    units = w_ins[0].shape[1]
    slope = ((share, 2 * units), bf16)
    flat = ADAPTERS * BOTTLENECK
    if own:
        outputs = [((share, model), f32), slope, slope] + [((share, model), f32)] * 2 + [((share, 128), f32)]
        outputs += [((flat, ADAPTERS), bf16), ((ADAPTERS, flat), bf16), ((8, flat), f32)]
    else:
        outputs = [((share, model), bf16), ((share, 2 * units), f32)]
    return run(
        functools.partial(forward_kernel, own),
        (ids,),
        [early, c2, x, o2, vecs, message, *w_ins, *w_backs, *more],
        outputs,
        vmem=16,
        micros=3.0,
    )


def backward_kernel(gp, slope, back0, back1, in0, in1, part_ref):
    grad = gp[...]
    units = in0.shape[1]
    part = jnp.zeros(grad.shape, f32)
    for j, (w_back, w_in) in enumerate(((back0, in0), (back1, in1))):
        bend = slope[:, j * units : (j + 1) * units].astype(f32)
        inner = (bend * mm_nt(grad, w_back[...])).astype(bf16)
        part = part + mm_nt(inner, w_in[...])
    part_ref[...] = part.astype(part_ref.dtype)


def backward_rows(grad, slope, w_backs, w_ins, dtype):
    share, model = grad.shape
    units = w_ins[0].shape[1]
    return run(
        backward_kernel,
        (),
        [grad, slope, *w_backs, *w_ins],
        [((share, model), dtype)],
    )


def first_norm_kernel(own, got, gpre2, normed, factor, vecs, o0, o1, o2, o3, gpre1, c0, c1, c2, c3):
    grad = own[...] + got[...].astype(f32) + gpre2[...]
    grad = norm_back(grad, normed[...], factor[:, 0:1], vecs[...].astype(f32)[1:2])
    gpre1[...] = grad
    low = grad.astype(bf16)
    for c, o in ((c2, o2), (c3, o3), (c1, o1), (c0, o0)):
        c[...] = mm_nt(low, o[...]).astype(bf16)


def first_norm_back(own, got, gpre2, normed, factor, vecs, outs):
    share, model = own.shape
    width = outs[0].shape[0]
    return run(
        first_norm_kernel,
        (),
        [own, got, gpre2, normed, factor, vecs, *outs],
        [((share, model), f32)] + [((share, width), bf16)] * 4,
    )


def adapter_kernel(
    slots, ids, own, got, first_ref, cot, weight, count, vecs, member_ref, spread_ref, bias_ref, up_bias, down, up,
    wq, wk, wv,
    out_hbm, keep, give, sums, turn_ref, reduced_ref, mix_ref, base_ref, normed_ref, factor_ref, layer_out, lefts, sem,
):
    flat, model = up.shape
    vec = vecs[...].astype(f32)
    member = member_ref[...]
    spread = spread_ref[...]
    inv_root = model ** (-0.5)
    scale = 0.5 * slots / jnp.maximum(count[0:1, 0:1], 1.0)

    normed_two, factor_two = norm_parts(own[...] + got[...].astype(f32) + vec[3:4] + first_ref[...])
    normed_ref[...] = normed_two
    factor_ref[...] = jnp.broadcast_to(factor_two, factor_ref.shape)
    second = normed_two * vec[4:5] + vec[5:6]
    second_low = second.astype(bf16)
    query_key = mm_nt(mm(second_low, wq[...]).astype(bf16), wk[...]) * inv_root
    query_key_low = query_key.astype(bf16)
    lift_key = mm_nt(query_key_low, up[...])
    reduced = mm_nt(second_low, down[...]) + bias_ref[0:1, :]
    reduced_ref[...] = reduced
    squeezed = 0.5 * reduced * (1.0 + lax.erf(reduced * ROOT_HALF))
    squeezed = squeezed.astype(bf16).astype(f32)
    logits = (
        mm((squeezed * lift_key).astype(bf16), member)
        + mm_nt(query_key_low, up_bias[...])
        + jnp.sum(query_key * second, axis=-1, keepdims=True)
    )
    shifted = logits - jnp.max(logits, axis=-1, keepdims=True)
    log_probs = shifted - jnp.log(jnp.sum(jnp.exp(shifted), axis=-1, keepdims=True))
    joining = jnp.exp(log_probs)
    entropy = -jnp.sum(joining * log_probs, axis=-1, keepdims=True)
    total = jnp.sum(joining, axis=-1, keepdims=True)
    joining_low = joining.astype(bf16)
    joining_wide = mm(joining_low, spread)
    joined_low = (joining_wide * squeezed).astype(bf16)
    mixed = total * second + mm(joined_low, up[...]) + mm(joining_low, up_bias[...])
    mixed_low = mixed.astype(bf16)
    normed_join, factor_join = norm_parts(second + mm(mixed_low, wv[...]))
    grad_out = cot[...].astype(f32)
    grad_pref = norm_back(grad_out, normed_join, factor_join, vec[6:7])
    grad_pref_low = grad_pref.astype(bf16)
    back_value = mm_nt(grad_pref_low, wv[...])
    back_value_low = back_value.astype(bf16)
    lift_value = mm_nt(back_value_low, up[...])
    grad_probs = (
        mm((squeezed * lift_value).astype(bf16), member)
        + mm_nt(back_value_low, up_bias[...])
        + jnp.sum(back_value * second, axis=-1, keepdims=True)
    )
    mean_grad = jnp.sum(joining * grad_probs, axis=-1, keepdims=True)
    grad_logits = joining * (grad_probs - mean_grad) - scale * weight[...] * joining * (log_probs + entropy)
    logits_low = grad_logits.astype(bf16)
    grad_wide = mm(logits_low, spread)
    logit_sum = jnp.sum(grad_logits, axis=-1, keepdims=True)
    turned = (
        logit_sum * second + mm((grad_wide * squeezed).astype(bf16), up[...]) + mm(logits_low, up_bias[...])
    ) * inv_root
    turned_low = turned.astype(bf16)
    turn_ref[...] = turned_low

    layer_out[...] = normed_join * vec[6:7] + vec[7:8]
    copy = pltpu.make_async_copy(layer_out, out_hbm, sem)
    copy.start()
    small = jnp.concatenate(
        [
            jnp.sum(grad_out * normed_join, axis=0, keepdims=True),
            jnp.sum(grad_out, axis=0, keepdims=True),
            jnp.zeros((sums.shape[0] - 2, model), f32),
        ],
        axis=0,
    )
    sums[...] = small
    write_small(give, small)
    mix_ref[...] = grad_wide * lift_key + joining_wide * lift_value
    base_ref[...] = grad_pref + logit_sum * query_key + total * back_value

    half = model // 2
    lefts[0] = second_low
    lefts[1] = mixed_low
    for j, right in enumerate((turned_low, grad_pref_low)):
        rows = slice(j * half, (j + 1) * half)
        other = lefts[j, :, pl.ds(pl.multiple_of((1 - ids[6]) * half, 128), half)]
        give[rows, :] = mm_tn(other, right).astype(bf16)
        mine = lefts[j, :, pl.ds(pl.multiple_of(ids[6] * half, 128), half)]
        keep[rows, :] = mm_tn(mine, right).astype(bf16)
    copy.wait()


def adapters(slots, ids, arrays):
    share, model = arrays[0].shape
    flat = ADAPTERS * BOTTLENECK
    wide, flat_wide = ((share, model), f32), ((share, flat), f32)
    return run(
        functools.partial(adapter_kernel, slots),
        (ids,),
        arrays,
        [
            ((share, model), f32, None),
            ((model, model), bf16),
            ((model + 16, model), bf16),
            ((8, model), f32),
            ((share, model), bf16),
            flat_wide,
            flat_wide,
            wide,
            wide,
            ((share, 128), f32),
        ],
        scratch=[
            pltpu.VMEM((share, model), f32),
            pltpu.VMEM((2, share, model), bf16),
            pltpu.SemaphoreType.DMA,
        ],
        vmem=20,
        micros=8.0,
    )


def adapter_rest_kernel(turn, reduced, mix, base, normed, factor, vecs, down, wq, wk, gpre2_ref, gpre2_low):
    grad_query_f = mm(turn[...], wk[...]).astype(bf16)
    grad_reduced = (gelu_both(reduced[...])[1] * mix[...]).astype(bf16)
    grad_second = base[...] + mm(grad_reduced, down[...]) + mm_nt(grad_query_f, wq[...])
    grad_pre2 = norm_back(grad_second, normed[...], factor[:, 0:1], vecs[4:5, :])
    gpre2_ref[...] = grad_pre2
    gpre2_low[...] = grad_pre2.astype(bf16)


def write_small(message, sums):
    high, low = halves_of(sums)
    rows = message.shape[0] - 16
    message[rows:, :] = jnp.concatenate([high, low], axis=0)


def read_small(message):
    rows = message.shape[0] - 16
    both = message[rows:, :].astype(f32)
    return both[:8] + both[8:]


def fold_kernel(base, start, split, last, ids, *refs):
    if start:
        keep, got, sums, *outs = refs
        rows = keep.shape[0] // 2
        pieces = [(keep, got, j * rows) for j in range(2)]
    else:
        *arrays, sums = refs[:5]
        outs = refs[5:]
        rows = arrays[0].shape[0]
        pieces = [(arrays[2 * j], arrays[2 * j + 1], 0) for j in range(2)]
        got = arrays[3]
    total = sums[...] + read_small(got)
    outs[-1][...] = total
    for j, (mine, other, at) in enumerate(pieces):
        def both(where):
            return (mine[where, :].astype(f32) + other[where, :].astype(f32)).astype(bf16)

        if split:
            half = rows // 2
            bit = ids[base + j]
            outs[2 * j][...] = both(pl.ds(pl.multiple_of(at + bit * half, 16), half))
            outs[2 * j + 1][:half, :] = both(pl.ds(pl.multiple_of(at + (1 - bit) * half, 16), half))
        elif last:
            outs[j][...] = both(pl.ds(at, rows))
        else:
            whole = both(pl.ds(at, rows))
            outs[2 * j][...] = whole
            outs[2 * j + 1][:rows, :] = whole
    if not last:
        write_small(outs[3], total)


def fold(ids, base, start, split, arrays, rows, sums, last=False):
    model = sums.shape[1]
    rows = rows // 2 if split else rows
    outputs = []
    for j in range(2):
        outputs += [((rows, model), bf16)] + ([] if last else [((rows + 16 * j, model), bf16)])
    outputs.append((sums.shape, f32))
    outs = run(functools.partial(fold_kernel, base, start, split, last), (ids,), [*arrays, sums], outputs)
    if last:
        return outs[:2], None, outs[2]
    return outs[0:4:2], outs[1:4:2], outs[4]


def join_kernel(base, last, ids, *refs):
    outs = refs[4:]
    for j in range(2):
        mine, got = refs[2 * j : 2 * j + 2]
        rows = mine.shape[0]
        bit = ids[base + j]
        out, at = (outs[0], 2 * rows * j) if last else (outs[j], 0)
        out[pl.ds(pl.multiple_of(at + bit * rows, 16), rows), :] = mine[...]
        out[pl.ds(pl.multiple_of(at + (1 - bit) * rows, 16), rows), :] = got[...]


def join(ids, base, last, mine, gots):
    rows, model = mine[0].shape
    outputs = [((4 * rows, model), bf16)] if last else [((2 * rows, model), bf16)] * 2
    arrays = [a for pair in zip(mine, gots) for a in pair]
    return run(functools.partial(join_kernel, base, last), (ids,), arrays, outputs)


def finish_kernel(first, ids, source, wq, wk, *refs):
    half = source.shape[0] // 2
    if first:
        part_own, part_got, out_q, out_v, key_part, out_x, stage, stage_x, sems = refs
    else:
        key_before, _, _, out_q, out_v, out_k, stage, stage_k, sems = refs
    core = ids[6] if first else 1 - ids[6]
    rows = pl.ds(pl.multiple_of(core * half, half), half)
    copies = []

    def send(j, source, target):
        copies.append(pltpu.make_async_copy(source, target, sems.at[j]))
        copies[-1].start()

    if first:
        stage_x[...] = part_own[...] + part_got[...].astype(f32)
        send(3, stage_x, out_x)
    mixed = source[:half, :]
    key = mm_tn(mixed, wq[rows, :])
    if first:
        key_part[...] = key
    else:
        stage_k[...] = key_before[...] + key
        send(2, stage_k, out_k)
    stage[1] = source[half:, :].astype(f32)
    send(1, stage.at[1], out_v.at[rows, :])
    stage[0] = mm(mixed, wk[...])
    send(0, stage.at[0], out_q.at[rows, :])
    for copy in copies:
        copy.wait()


def finish(ids, source, wq, wk, before, parts=()):
    model = source.shape[1]
    half = source.shape[0] // 2
    first = before is None
    vmem_spec = pl.BlockSpec(memory_space=pltpu.VMEM)
    any_spec = pl.BlockSpec(memory_space=pl.ANY)
    whole = jax.ShapeDtypeStruct((model, model), f32)
    inputs = [source, wq, wk, *(parts if first else [before[2]])]
    if first:
        out_specs = [any_spec, any_spec, vmem_spec, any_spec]
        shape = parts[0].shape
        out_shape = [whole, whole, pltpu.VMEM((model, model), f32), jax.ShapeDtypeStruct(shape, f32)]
    else:
        out_specs, shape, out_shape = [any_spec] * 3, (model, model), [whole] * 3
    return pl.pallas_call(
        functools.partial(finish_kernel, first),
        in_specs=[pl.BlockSpec(memory_space=pltpu.SMEM)]
        + [vmem_spec] * len(inputs)
        + ([] if first else [any_spec] * 2),
        out_specs=out_specs,
        out_shape=out_shape,
        input_output_aliases={} if first else {5: 0, 6: 1},
        scratch_shapes=[
            pltpu.VMEM((2, half, model), f32),
            pltpu.VMEM(shape, f32),
            pltpu.SemaphoreType.DMA((4,)),
        ],
        compiler_params=pltpu.CompilerParams(vmem_limit_bytes=16 * 1024 * 1024),
        cost_estimate=pl.CostEstimate(flops=int(2 * FLOPS), bytes_accessed=1, transcendentals=0),
    )(ids, *[pltpu.with_memory_space_constraint(a, pltpu.VMEM) for a in inputs], *([] if first else before[:2]))


def chip_kernel(near, got, gpre1, keep, give):
    share = keep.shape[0]
    give[...] = (near[share:, :] + got[share:, :].astype(f32)).astype(bf16)
    keep[...] = near[:share, :] + got[:share, :].astype(f32) + gpre1[...]


def body(
    layer_input,
    cotangent,
    seq_lens,
    seq_place,
    loss_mask,
    w_qkv,
    b_qv,
    w_out,
    b_out,
    ln1_gain,
    ln1_bias,
    w_in,
    b_in,
    w_back,
    b_back,
    ln2_gain,
    ln2_bias,
    ad_down,
    ad_down_bias,
    ad_up,
    ad_up_bias,
    join_query,
    join_key,
    join_value,
    join_gain,
    join_bias,
):
    group_rows, model = layer_input.shape
    share = cotangent.shape[0]
    rank = lax.axis_index("tp")
    dp_rank = lax.axis_index("dp")
    total_slots = group_rows * lax.axis_size("dp")

    core, near_x = ("tp", 1), ("tp", 2)
    others = []
    bit = 1
    while bit < lax.axis_size("dp"):
        others.append(("dp", bit))
        bit *= 2
    streams = [
        [others[0], *others[1:], near_x],
        [*others[1:2], others[0], near_x, *others[2:]],
    ]

    def bit_of(axis, which):
        return (lax.axis_index(axis) // which) % 2

    ids = [rank, dp_rank] + [rank ^ j for j in ORDER] + [bit_of(*core)]
    for at in range(len(others) + 1):
        ids += [bit_of(*stream[at]) for stream in streams]
    ids = jnp.stack(ids).astype(i32)
    ids = jnp.concatenate([ids, jnp.zeros(HEADER - ids.shape[0], i32), seq_lens, seq_place])
    vectors = [b_out, ln1_gain, ln1_bias, b_back, ln2_gain, ln2_bias, join_gain, join_bias, b_in]

    outs = [w_out, swap(w_out, "tp", 1), swap(w_out, "tp", 2)]
    outs.append(None)
    w_ins = [w_in, swap(w_in, "tp", 1)]
    w_backs = [w_back, swap(w_back, "tp", 1)]

    width = w_qkv.shape[2]
    w_t = jnp.transpose(w_qkv, (1, 2, 0)).reshape(3 * width, model)
    q, k, v, message = project(ids, layer_input, w_t, b_qv, loss_mask, b_in)
    message_got = swap(message, *core)
    far, e_far, rl_far = attend(2, 2, ids, q, k, v, share)
    far, message_got, outs[1], outs[2], w_ins[1], w_backs[1] = tie(
        far, message_got, *outs[1:3], w_ins[1], w_backs[1]
    )
    outs[3] = swap(outs[2], "tp", 1)
    c1, c3 = swap(far, "tp", 1), swap(far, "tp", 3)
    counted = message[1:2, :128] + message_got[1:2, :128]
    count_got = swap(counted, *others[0])
    q_near, _ = tie(q, far)
    near, e_near, rl_near = attend(0, 1, ids, q_near, k, v, share)
    c2_far = swap(near, *near_x)
    near, outs[3], c1 = tie(near, outs[3], c1)
    q_beside, _ = tie(q, near)
    beside, e_beside, rl_beside = attend(1, 1, ids, q_beside, k, v, share)
    c2_own = swap(beside, *near_x)
    early, vecs, weight_m = early_part(
        ids, [near, beside, c1, c3, outs[0], outs[1], outs[3]], loss_mask, vectors, share
    )

    give, inner = forward_rows(
        False, ids, early, c2_far, layer_input, outs[2], vecs, message_got, w_ins, w_backs, share
    )
    ffn_got = swap(give, *near_x)
    give, count_got = tie(give, count_got)
    counted = counted + count_got
    counted, _, _ = tie(counted, give, c2_own)
    pair = [bit for _, bit in others[1:3]]
    count_gots = [swap(counted, "dp", bit) for bit in [*pair, *([sum(pair)] if len(pair) == 2 else [])]]
    own, slope_one, slope_two, first, normed_one, factor_one, *constants = forward_rows(
        True, ids, early, c2_own, layer_input, outs[2], vecs, message_got, w_ins, w_backs, share, inner,
        ad_down_bias,
    )
    own, *count_gots = tie(own, *count_gots)
    counted = sum(count_gots, counted)
    for axis, which in [*others[3:], near_x]:
        counted = counted + swap(counted, axis, which)

    flat = ADAPTERS * BOTTLENECK
    down_t = jnp.transpose(ad_down, (1, 2, 0)).reshape(flat, model)
    up = ad_up.reshape(flat, model)
    layer_out, keep, give, sums, turn, reduced, mix, base, normed_two, factor_two = adapters(
        total_slots,
        ids,
        [
            own, ffn_got, first, cotangent, weight_m, counted, vecs, *constants, ad_up_bias, down_t, up,
            join_query, join_key, join_value,
        ],
    )
    got = swap(give, *core)
    gpre2, gpre2_low = run(
        adapter_rest_kernel,
        (),
        [turn, reduced, mix, base, normed_two, factor_two, vecs, down_t, join_query, join_key],
        [((share, model), f32), ((share, model), bf16)],
    )
    gpre2_got = swap(gpre2_low, "tp", 2)

    state = {"at": 0, "history": [], "rows": keep.shape[0] // 2}

    def sum_step(keeps, gots, sums):
        at = state["at"]
        start = at == 0
        split = state["rows"] // 2 >= LEAST_ROWS
        arrays = [keeps, gots] if start else [a for pair in zip(keeps, gots) for a in pair]
        keeps, gives, sums = fold(ids, 7 + 2 * at, start, split, arrays, state["rows"], sums)
        if split:
            state["rows"] //= 2
            state["history"].append(at)
        state["at"] = at + 1
        return keeps, [swap(g, *stream[at]) for g, stream in zip(gives, streams)], sums

    (back_own,) = backward_rows(gpre2_low, slope_one, w_backs, w_ins, f32)
    back_own, got = tie(back_own, got)
    keeps, gots, sums = sum_step(keep, got, sums)
    keeps[0], gpre2_got = tie(keeps[0], gpre2_got)
    (back_give,) = backward_rows(gpre2_got, slope_two, w_backs, w_ins, bf16)
    back_give, *gots = tie(back_give, *gots)
    keeps, gots, sums = sum_step(keeps, gots, sums)
    keeps[0], back_give = tie(keeps[0], back_give)
    back_got = swap(back_give, "tp", 2)
    keeps, gots, sums = sum_step(keeps, gots, sums)
    keeps[0], back_got = tie(keeps[0], back_got)
    gpre1, c0, c1, c2, c3 = first_norm_back(back_own, back_got, gpre2, normed_one, factor_one, vecs, outs)
    c2, c3, c1 = swap(c2, "tp", 2), swap(c3, "tp", 3), swap(c1, "tp", 1)
    shared = ((near, beside, far), (e_near, e_beside, e_far), (rl_near, rl_beside, rl_far), (q, k, v))
    before = list(attend_back((0,), ids, (c0,), *shared, [], None, share))
    before[0], *gots = tie(before[0], *gots)
    keeps, gots, sums = sum_step(keeps, gots, sums)
    before[0], keeps[0] = tie(before[0], keeps[0])
    far_part, near_part = attend_back((2, 1, 3), ids, (c1, c2, c3), *shared, before, w_t, share)
    far_part, *gots = tie(far_part, *gots)
    far_got = swap(far_part, "tp", 1)
    while state["at"] < len(others) + 1:
        keeps, gots, sums = sum_step(keeps, gots, sums)
    arrays = [a for pair in zip(keeps, gots) for a in pair]
    keeps, _, sums = fold(ids, 0, False, False, arrays, state["rows"], sums, last=True)
    gain_grad, bias_grad = sums[0], sums[1]
    part_own, part_give = run(
        chip_kernel, (), [near_part, far_got, gpre1], [((share, model), f32), ((share, model), bf16)]
    )
    part_got = swap(part_give, "tp", 2)
    for at in reversed(state["history"]):
        gots = [swap(a, *stream[at]) for a, stream in zip(keeps, streams)]
        gots[0], part_own, gain_grad, bias_grad = tie(gots[0], part_own, gain_grad, bias_grad)
        keeps = join(ids, 7 + 2 * at, at == 0, keeps, gots)
    keeps[0], part_got = tie(keeps[0], part_got)
    got = swap(keeps[0], *core)
    *part, input_grad = finish(ids, keeps[0], join_query, join_key, None, (part_own, part_got))
    query_grad, value_grad, key_grad = finish(ids, got, join_query, join_key, part)
    return (layer_out, input_grad, query_grad, key_grad, value_grad, gain_grad, bias_grad)


def solution(mesh):
    placed = (
        P("dp", None),
        P(("dp", "tp"), None),
        P(),
        P(),
        P(("dp", "tp")),
        P(None, None, "tp"),
        P(None, "tp"),
        P("tp", None),
        P(),
        P(),
        P(),
        P(None, "tp"),
        P("tp"),
        P("tp", None),
        P(),
        P(),
        P(),
        P(),
        P(),
        P(),
        P(),
        P(),
        P(),
        P(),
        P(),
        P(),
    )
    return jax.shard_map(
        body,
        mesh=mesh,
        in_specs=placed,
        out_specs=(P(("dp", "tp"), None), P(("dp", "tp"), None), P(), P(), P(), P(), P()),
        check_vma=False,
    )
```

```python
import functools

import jax
import jax.numpy as jnp
from jax import lax
from jax.experimental import pallas as pl
from jax.experimental.pallas import tpu as pltpu
from jax.sharding import PartitionSpec as P

HEAD_DIM = 64
ADAPTERS = 16
BOTTLENECK = 48
SEQ_GRP = 4
LEAST_ROWS = 96
FLOPS = 1.15e9

EPS = 1e-06
NEG = -1e30
ROOT_HALF = 0.7071067811865476
INV_ROOT_TAU = 0.3989422804014327

f32 = jnp.float32
bf16 = jnp.bfloat16
i32 = jnp.int32

HEADER = 64

ORDER = (0, 2, 1, 3)


def gelu_both(values):
    phi = 0.5 * (1.0 + lax.erf(values * ROOT_HALF))
    return values * phi, phi + values * jnp.exp(-0.5 * values * values) * INV_ROOT_TAU


def row_mean(values):
    return jnp.sum(values, axis=-1, keepdims=True) * (1.0 / values.shape[-1])


def norm_parts(values):
    center = values - row_mean(values)
    factor = lax.rsqrt(row_mean(center * center) + EPS)
    return center * factor, factor


def norm_back(gradient, normed, factor, gain_vec):
    scaled = gradient * gain_vec
    return factor * (scaled - row_mean(scaled) - normed * row_mean(scaled * normed))


def mm(a, b):
    return lax.dot_general(a, b, (((1,), (0,)), ((), ())), preferred_element_type=f32)


def mm_nt(a, b):
    return lax.dot_general(a, b, (((1,), (1,)), ((), ())), preferred_element_type=f32)


def mm_tn(a, b):
    return lax.dot_general(a, b, (((0,), (0,)), ((), ())), preferred_element_type=f32)


def halves_of(a):
    high = a.astype(bf16)
    return high, (a - high.astype(f32)).astype(bf16)


def swap(value, axis, bit):
    size = lax.axis_size(axis)
    return lax.ppermute(value, axis, [(i, i ^ bit) for i in range(size)])


def tie(*values):
    return lax.optimization_barrier(values)


def run(kernel, scalars, inputs, outputs, streamed=(), scratch=(), vmem=12, micros=0.1):
    smem = pl.BlockSpec(memory_space=pltpu.SMEM)
    vmem_spec = pl.BlockSpec(memory_space=pltpu.VMEM)
    any_spec = pl.BlockSpec(memory_space=pl.ANY)
    outs = pl.pallas_call(
        kernel,
        in_specs=[smem] * len(scalars) + [vmem_spec] * len(inputs) + [any_spec] * len(streamed),
        out_specs=[vmem_spec if len(o) == 2 else any_spec for o in outputs],
        out_shape=[pltpu.VMEM(*o) if len(o) == 2 else jax.ShapeDtypeStruct(*o[:2]) for o in outputs],
        scratch_shapes=list(scratch),
        compiler_params=pltpu.CompilerParams(vmem_limit_bytes=vmem * 1024 * 1024),
        cost_estimate=pl.CostEstimate(flops=int(micros * FLOPS), bytes_accessed=1, transcendentals=0),
    )(
        *scalars,
        *[pltpu.with_memory_space_constraint(a, pltpu.VMEM) for a in inputs],
        *[pltpu.with_memory_space_constraint(a, pltpu.HBM) for a in streamed],
    )
    return list(outs)


def head_mask(width, head):
    lane = lax.broadcasted_iota(i32, (1, width), 1)
    return (lane >= head * HEAD_DIM) & (lane < (head + 1) * HEAD_DIM)


def group_ends(ints):
    count = (ints.shape[0] - HEADER) // 2

    def add(s, ends):
        spot = ints[HEADER + count + s] - ints[1] * SEQ_GRP
        length = jnp.where(spot >= 0, ints[HEADER + s], 0)
        return tuple(e + jnp.where(spot <= j, length, 0) for j, e in enumerate(ends))

    return lax.fori_loop(0, count, add, (jnp.int32(0),) * SEQ_GRP, unroll=8)


def segment_of(positions, ends):
    segment = jnp.zeros(positions.shape, i32)
    for e in ends:
        segment = segment + (positions >= e).astype(i32)
    return jnp.where(positions < ends[-1], segment, SEQ_GRP + positions)


def window(rows, start, ends, group_rows):
    low = jnp.int32(0)
    high = jnp.int32(0)
    last = start + rows - 1
    for e in ends:
        low = jnp.where(start >= e, jnp.maximum(low, e), low)
    for e in reversed(ends):
        high = jnp.where(last < e, e, high)
    padded = last >= ends[-1]
    low = jnp.where(start >= ends[-1], start, low)
    high = jnp.where(padded, start + rows, high)
    low = jnp.minimum(low // 128 * 128, group_rows - 128)
    return low, high - low


def by_window(rows, start, ends, group_rows, act):
    low, span = window(rows, start, ends, group_rows)
    widths = [w for w in (512,) if w < group_rows] + [group_rows]
    least = 0
    for w in widths:
        fits = (span > least) & (span <= w) if w < group_rows else span > least

        @pl.when(fits)
        def _(w=w):
            act(pl.multiple_of(jnp.minimum(low, group_rows - w), 128), w)

        least = w


def one_row(tile):
    return jnp.concatenate([tile[j : j + 1, :] for j in range(tile.shape[0])], axis=1)


def real_row(ids, mask):
    row = one_row(mask[...].astype(f32))
    lane = lax.broadcasted_iota(i32, row.shape, 1)
    return jnp.where(ids[0] * row.shape[1] + lane < group_ends(ids)[-1], row, 0.0)


def project_kernel(
    ids, x_hbm, w_hbm, bias_hbm, mask_hbm, b_in_hbm, q_ref, k_ref, v_ref, message, x_ref, w_ref, bias_ref, mask_ref,
    b_in_ref, sems,
):
    group_rows, width = q_ref.shape
    chunks = 4
    share = group_rows // chunks
    pairs = [(w_hbm, w_ref), (bias_hbm, bias_ref)]
    for c in range(chunks):
        rows = pl.ds(c * share, share)
        pairs.append((x_hbm.at[rows, :], x_ref.at[rows, :]))
    pairs += [(mask_hbm, mask_ref), (b_in_hbm, b_in_ref)]
    copies = [pltpu.make_async_copy(source, target, sems.at[j]) for j, (source, target) in enumerate(pairs)]
    for copy in copies:
        copy.start()
    copies[0].wait()
    copies[1].wait()
    bias = bias_ref[...].astype(f32)
    for c in range(chunks):
        rows = slice(c * share, (c + 1) * share)
        copies[2 + c].wait()
        x = x_ref[rows, :]
        k_ref[rows, :] = mm_nt(x, w_ref[width : 2 * width, :]).astype(bf16)
        v_ref[rows, :] = (mm_nt(x, w_ref[2 * width :, :]) + bias[1:2]).astype(bf16)
        q = (mm_nt(x, w_ref[:width, :]) + bias[0:1]).astype(bf16)
        q_ref[rows, :] = (q.astype(f32) * HEAD_DIM ** (-0.5)).astype(bf16)
    for copy in copies[2 + chunks :]:
        copy.wait()
    message[0:1, :] = one_row(b_in_ref[...].astype(f32))
    total = jnp.sum(real_row(ids, mask_ref), axis=-1, keepdims=True)
    message[1:, :] = jnp.broadcast_to(total, (message.shape[0] - 1, message.shape[1]))


def project(ids, x, w_t, b_qv, mask, b_in):
    group_rows, model = x.shape
    width = w_t.shape[0] // 3
    streamed = [x, w_t, b_qv, mask.reshape(-1, 128), b_in.reshape(-1, 128)]
    return run(
        project_kernel,
        (ids,),
        [],
        [((group_rows, width), bf16)] * 3 + [((8, model), f32)],
        streamed=streamed,
        scratch=[pltpu.VMEM(a.shape, a.dtype) for a in streamed] + [pltpu.SemaphoreType.DMA((8,))],
        micros=3.0,
    )


def attend_kernel(first, blocks, ids, q_ref, k_ref, v_ref, *refs):
    context_ref, e_ref, rl_ref = refs
    rows = rl_ref.shape[0] // blocks
    group_rows, width = k_ref.shape
    heads = width // HEAD_DIM
    ends = group_ends(ids)

    def one(t, carry):
        start = pl.multiple_of(ids[2 + first + t] * rows, rows)
        at = pl.multiple_of(t * rows, rows)

        def act(key0, w):
            q = q_ref[pl.ds(start, rows), :].astype(f32)
            seg_q = segment_of(start + lax.broadcasted_iota(i32, (rows, 1), 0), ends)
            seg_k = segment_of(key0 + lax.broadcasted_iota(i32, (1, w), 1), ends)
            k = k_ref[pl.ds(key0, w), :]
            v = v_ref[pl.ds(key0, w), :]
            context = jnp.zeros((rows, width), f32)
            wide = jnp.zeros((rows, width), f32)
            for h in range(heads):
                mask = head_mask(width, h)
                scores = mm_nt(jnp.where(mask, q, 0.0).astype(bf16), k)
                scores = jnp.where(seg_q == seg_k, scores, NEG)
                e = jnp.exp(scores - jnp.max(scores, axis=-1, keepdims=True))
                inverse = 1.0 / jnp.sum(e, axis=-1, keepdims=True)
                low = e.astype(bf16)
                e_ref[pl.ds(pl.multiple_of((t * heads + h) * rows, rows), rows), :w] = low
                context = jnp.where(mask, mm(low, v) * inverse, context)
                wide = jnp.where(mask, inverse, wide)
            rl_ref[pl.ds(at, rows), :] = wide
            context_ref[pl.ds(at, rows), :] = context.astype(bf16)

        by_window(rows, start, ends, group_rows, act)
        return carry

    lax.fori_loop(0, blocks, one, 0)


def attend(first, blocks, ids, q, k, v, share):
    group_rows, width = k.shape
    heads = width // HEAD_DIM
    return run(
        functools.partial(attend_kernel, first, blocks),
        (ids,),
        [q, k, v],
        [
            ((blocks * share, width), bf16),
            ((blocks * heads * share, group_rows), bf16),
            ((blocks * share, width), f32),
        ],
        vmem=20,
        micros=3.0 if first else 0.1,
    )


def attend_back_kernel(spots, first, last, ids, *refs):
    count = len(spots)
    grads, refs = refs[:count], refs[count:]
    contexts, es, rls, refs = refs[0:3], refs[3:6], refs[6:9], refs[9:]
    q_ref, k_ref, v_ref, refs = refs[0], refs[1], refs[2], refs[3:]
    if not first:
        before, refs = refs[:3], refs[3:]
    if last:
        w_ref, far_out, near_out, gq, gk, gv = refs
    else:
        gq, gk, gv = refs
    rows = grads[0].shape[0]
    group_rows, width = k_ref.shape
    heads = width // HEAD_DIM
    ends = group_ends(ids)
    if first:
        gk[...] = jnp.zeros_like(gk)
        gv[...] = jnp.zeros_like(gv)
    else:
        gq[...] = before[0][...]
        gk[...] = before[1][...]
        gv[...] = before[2][...]
    for g_ref, spot in zip(grads, spots):
        start = pl.multiple_of(ids[2 + spot] * rows, rows)
        part, t = (spot, 0) if spot < 2 else (2, spot - 2)
        g = g_ref[...].astype(f32) * rls[part][t * rows : (t + 1) * rows, :]
        dots = g * contexts[part][t * rows : (t + 1) * rows, :].astype(f32)
        q = q_ref[pl.ds(start, rows), :].astype(f32)

        def act(key0, w, g=g, dots=dots, q=q, part=part, t=t, start=start):
            keys = pl.ds(key0, w)
            k = k_ref[keys, :]
            v = v_ref[keys, :]
            out = jnp.zeros((rows, width), f32)
            add_k = jnp.zeros((w, width), f32)
            add_v = jnp.zeros((w, width), f32)
            for h in range(heads):
                mask = head_mask(width, h)
                g_head = jnp.where(mask, g, 0.0).astype(bf16)
                e = es[part][(t * heads + h) * rows : (t * heads + h + 1) * rows, :w]
                delta = jnp.sum(jnp.where(mask, dots, 0.0), axis=-1, keepdims=True)
                ds = (e.astype(f32) * (mm_nt(g_head, v) - delta)).astype(bf16)
                out = jnp.where(mask, mm(ds, k), out)
                add_k = add_k + mm_tn(ds, jnp.where(mask, q, 0.0).astype(bf16))
                add_v = add_v + mm_tn(e, g_head)
            gk[keys, :] += add_k
            gv[keys, :] += add_v
            gq[pl.ds(start, rows), :] = (out * HEAD_DIM ** (-0.5)).astype(bf16)

        by_window(rows, start, ends, group_rows, act)
    if last:
        for out, pair in ((far_out, (2, 3)), (near_out, (0, 1))):
            for t, spot in enumerate(pair):
                own = pl.ds(pl.multiple_of(ids[2 + spot] * rows, rows), rows)
                part = (
                    mm(gq[own, :], w_ref[:width, :])
                    + mm(gk[own, :].astype(bf16), w_ref[width : 2 * width, :])
                    + mm(gv[own, :].astype(bf16), w_ref[2 * width :, :])
                )
                out[t * rows : (t + 1) * rows, :] = part.astype(out.dtype)


def attend_back(spots, ids, grads, contexts, es, rls, qkv, before, w_t, share):
    group_rows, width = qkv[0].shape
    last = w_t is not None
    sums = [((group_rows, width), bf16), ((group_rows, width), f32), ((group_rows, width), f32)]
    inputs = [*grads, *contexts, *es, *rls, *qkv, *before]
    if last:
        model = w_t.shape[1]
        outputs = [((2 * share, model), bf16), ((2 * share, model), f32)]
        scratch = [pltpu.VMEM(*o) for o in sums]
        inputs.append(w_t)
    else:
        outputs, scratch = sums, []
    return run(
        functools.partial(attend_back_kernel, spots, not before, last),
        (ids,),
        inputs,
        outputs,
        scratch=scratch,
        vmem=20,
        micros=5.0 if last else 0.1,
    )


def early_kernel(ids, c0, x0, c1, c3, o0, o1, o3, *refs):
    mask_hbm, *vectors = refs[:10]
    out, vecs, weight, mask_ref, *tiles, sems = refs[10:]
    pairs = [(mask_hbm, mask_ref), *zip(vectors, tiles)]
    copies = [pltpu.make_async_copy(source, target, sems.at[j]) for j, (source, target) in enumerate(pairs)]
    for copy in copies:
        copy.start()
    share = out.shape[0] // 2
    attn = mm(c1[...], o1[...])
    for t, mine in enumerate((c0, x0)):
        rows = slice(t * share, (t + 1) * share)
        out[rows, :] = attn[rows] + mm(mine[...], o0[...]) + mm(c3[(1 - t) * share : (2 - t) * share, :], o3[...])
    for copy in copies:
        copy.wait()
    for j, tile in enumerate(tiles):
        vecs[j : j + 1, :] = one_row(tile[...].astype(f32))
    vecs[9:, :] = jnp.zeros((vecs.shape[0] - 9, vecs.shape[1]), f32)
    row = real_row(ids, mask_ref)
    here = lax.broadcasted_iota(i32, (share, share), 0) == lax.broadcasted_iota(i32, (share, share), 1)
    weight[...] = jnp.sum(jnp.where(here, jnp.broadcast_to(row, (share, share)), 0.0), axis=-1, keepdims=True)


def early_part(ids, arrays, mask, vectors, share):
    model = arrays[4].shape[1]
    streamed = [mask.reshape(-1, 128), *[v.reshape(-1, 128) for v in vectors]]
    return run(
        early_kernel,
        (ids,),
        arrays,
        [((2 * share, model), f32), ((16, model), f32), ((share, 1), f32)],
        streamed=streamed,
        scratch=[pltpu.VMEM(a.shape, a.dtype) for a in streamed] + [pltpu.SemaphoreType.DMA((len(streamed),))],
    )


def adapter_constants(down_bias, member_ref, spread_ref, bias_ref):
    flat = member_ref.shape[0]
    lane = lax.broadcasted_iota(i32, (flat, ADAPTERS), 0) - BOTTLENECK * lax.broadcasted_iota(
        i32, (flat, ADAPTERS), 1
    )
    member_ref[...] = ((lane >= 0) & (lane < BOTTLENECK)).astype(f32).astype(bf16)
    lane = lax.broadcasted_iota(i32, (ADAPTERS, flat), 1) - BOTTLENECK * lax.broadcasted_iota(
        i32, (ADAPTERS, flat), 0
    )
    spread = ((lane >= 0) & (lane < BOTTLENECK)).astype(f32)
    spread_ref[...] = spread.astype(bf16)
    cycle = lax.broadcasted_iota(i32, (BOTTLENECK, flat), 1) - lax.broadcasted_iota(i32, (BOTTLENECK, flat), 0)
    repeat = jnp.zeros(cycle.shape, f32)
    for a in range(ADAPTERS):
        repeat = repeat + (cycle == a * BOTTLENECK).astype(f32)
    bias_row = jnp.sum(mm(down_bias[...], repeat.astype(bf16)) * spread, axis=0, keepdims=True)
    bias_ref[...] = jnp.broadcast_to(bias_row, bias_ref.shape)


def forward_kernel(own, ids, early, c2, x_ref, o2, vecs, message, in0, in1, back0, back1, *rest):
    if own:
        inner_ref, down_bias, part_ref, slope, slope_two, first_ref, normed_ref, factor_ref, *constants = rest
    else:
        part_ref, inner_ref = rest
    share = early.shape[0] // 2
    t = 0 if own else 1
    attn = early[t * share : (t + 1) * share, :] + mm(c2[...], o2[...])
    vec = vecs[...].astype(f32)
    start = pl.multiple_of(ids[2 if own else 3] * share, share)
    normed, factor = norm_parts(attn + vec[0:1] + x_ref[pl.ds(start, share), :].astype(f32))
    first = normed * vec[1:2] + vec[2:3]
    low = first.astype(bf16)
    part = jnp.zeros(first.shape, f32)
    units = in0.shape[1]
    chunk = units
    for j, (w_in, bias, w_back) in enumerate(((in0, vec[8:9], back0), (in1, message[0:1, :], back1))):
        for at in range(0, units, chunk):
            here = slice(at, at + chunk)
            columns = slice(j * units + at, j * units + at + chunk)
            inner = mm(low, w_in[:, here]) + bias[:, here]
            if own:
                act, bend = gelu_both(inner)
                slope[:, columns] = bend.astype(bf16)
                slope_two[:, columns] = gelu_both(inner_ref[:, columns])[1].astype(bf16)
            else:
                act = 0.5 * inner * (1.0 + lax.erf(inner * ROOT_HALF))
                inner_ref[:, columns] = inner
            part = part + mm(act.astype(bf16), w_back[here, :])
    part_ref[...] = part.astype(part_ref.dtype)
    if own:
        first_ref[...] = first
        normed_ref[...] = normed
        factor_ref[...] = jnp.broadcast_to(factor, factor_ref.shape)
        adapter_constants(down_bias, *constants)


def forward_rows(own, ids, early, c2, x, o2, vecs, message, w_ins, w_backs, share, *more):
    model = x.shape[1]
    units = w_ins[0].shape[1]
    slope = ((share, 2 * units), bf16)
    flat = ADAPTERS * BOTTLENECK
    if own:
        outputs = [((share, model), f32), slope, slope] + [((share, model), f32)] * 2 + [((share, 128), f32)]
        outputs += [((flat, ADAPTERS), bf16), ((ADAPTERS, flat), bf16), ((8, flat), f32)]
    else:
        outputs = [((share, model), bf16), ((share, 2 * units), f32)]
    return run(
        functools.partial(forward_kernel, own),
        (ids,),
        [early, c2, x, o2, vecs, message, *w_ins, *w_backs, *more],
        outputs,
        vmem=16,
        micros=3.0,
    )


def backward_kernel(gp, slope, back0, back1, in0, in1, part_ref):
    grad = gp[...]
    units = in0.shape[1]
    part = jnp.zeros(grad.shape, f32)
    for j, (w_back, w_in) in enumerate(((back0, in0), (back1, in1))):
        bend = slope[:, j * units : (j + 1) * units].astype(f32)
        inner = (bend * mm_nt(grad, w_back[...])).astype(bf16)
        part = part + mm_nt(inner, w_in[...])
    part_ref[...] = part.astype(part_ref.dtype)


def backward_rows(grad, slope, w_backs, w_ins, dtype):
    share, model = grad.shape
    units = w_ins[0].shape[1]
    return run(
        backward_kernel,
        (),
        [grad, slope, *w_backs, *w_ins],
        [((share, model), dtype)],
    )


def first_norm_kernel(own, got, gpre2, normed, factor, vecs, o0, o1, o2, o3, gpre1, c0, c1, c2, c3):
    grad = own[...] + got[...].astype(f32) + gpre2[...]
    grad = norm_back(grad, normed[...], factor[:, 0:1], vecs[...].astype(f32)[1:2])
    gpre1[...] = grad
    low = grad.astype(bf16)
    for c, o in ((c2, o2), (c3, o3), (c1, o1), (c0, o0)):
        c[...] = mm_nt(low, o[...]).astype(bf16)


def first_norm_back(own, got, gpre2, normed, factor, vecs, outs):
    share, model = own.shape
    width = outs[0].shape[0]
    return run(
        first_norm_kernel,
        (),
        [own, got, gpre2, normed, factor, vecs, *outs],
        [((share, model), f32)] + [((share, width), bf16)] * 4,
    )


def adapter_kernel(
    slots, ids, own, got, first_ref, cot, weight, count, vecs, member_ref, spread_ref, bias_ref, up_bias, down, up,
    wq, wk, wv,
    out_hbm, keep, give, sums, turn_ref, reduced_ref, mix_ref, base_ref, normed_ref, factor_ref, layer_out, lefts, sem,
):
    flat, model = up.shape
    vec = vecs[...].astype(f32)
    member = member_ref[...]
    spread = spread_ref[...]
    inv_root = model ** (-0.5)
    scale = 0.5 * slots / jnp.maximum(count[0:1, 0:1], 1.0)

    normed_two, factor_two = norm_parts(own[...] + got[...].astype(f32) + vec[3:4] + first_ref[...])
    normed_ref[...] = normed_two
    factor_ref[...] = jnp.broadcast_to(factor_two, factor_ref.shape)
    second = normed_two * vec[4:5] + vec[5:6]
    second_low = second.astype(bf16)
    query_key = mm_nt(mm(second_low, wq[...]).astype(bf16), wk[...]) * inv_root
    query_key_low = query_key.astype(bf16)
    lift_key = mm_nt(query_key_low, up[...])
    reduced = mm_nt(second_low, down[...]) + bias_ref[0:1, :]
    reduced_ref[...] = reduced
    squeezed = 0.5 * reduced * (1.0 + lax.erf(reduced * ROOT_HALF))
    squeezed = squeezed.astype(bf16).astype(f32)
    logits = (
        mm((squeezed * lift_key).astype(bf16), member)
        + mm_nt(query_key_low, up_bias[...])
        + jnp.sum(query_key * second, axis=-1, keepdims=True)
    )
    shifted = logits - jnp.max(logits, axis=-1, keepdims=True)
    log_probs = shifted - jnp.log(jnp.sum(jnp.exp(shifted), axis=-1, keepdims=True))
    joining = jnp.exp(log_probs)
    entropy = -jnp.sum(joining * log_probs, axis=-1, keepdims=True)
    total = jnp.sum(joining, axis=-1, keepdims=True)
    joining_low = joining.astype(bf16)
    joining_wide = mm(joining_low, spread)
    joined_low = (joining_wide * squeezed).astype(bf16)
    mixed = total * second + mm(joined_low, up[...]) + mm(joining_low, up_bias[...])
    mixed_low = mixed.astype(bf16)
    normed_join, factor_join = norm_parts(second + mm(mixed_low, wv[...]))
    grad_out = cot[...].astype(f32)
    grad_pref = norm_back(grad_out, normed_join, factor_join, vec[6:7])
    grad_pref_low = grad_pref.astype(bf16)
    back_value = mm_nt(grad_pref_low, wv[...])
    back_value_low = back_value.astype(bf16)
    lift_value = mm_nt(back_value_low, up[...])
    grad_probs = (
        mm((squeezed * lift_value).astype(bf16), member)
        + mm_nt(back_value_low, up_bias[...])
        + jnp.sum(back_value * second, axis=-1, keepdims=True)
    )
    mean_grad = jnp.sum(joining * grad_probs, axis=-1, keepdims=True)
    grad_logits = joining * (grad_probs - mean_grad) - scale * weight[...] * joining * (log_probs + entropy)
    logits_low = grad_logits.astype(bf16)
    grad_wide = mm(logits_low, spread)
    logit_sum = jnp.sum(grad_logits, axis=-1, keepdims=True)
    turned = (
        logit_sum * second + mm((grad_wide * squeezed).astype(bf16), up[...]) + mm(logits_low, up_bias[...])
    ) * inv_root
    turned_low = turned.astype(bf16)
    turn_ref[...] = turned_low

    layer_out[...] = normed_join * vec[6:7] + vec[7:8]
    copy = pltpu.make_async_copy(layer_out, out_hbm, sem)
    copy.start()
    small = jnp.concatenate(
        [
            jnp.sum(grad_out * normed_join, axis=0, keepdims=True),
            jnp.sum(grad_out, axis=0, keepdims=True),
            jnp.zeros((sums.shape[0] - 2, model), f32),
        ],
        axis=0,
    )
    sums[...] = small
    write_small(give, small)
    mix_ref[...] = grad_wide * lift_key + joining_wide * lift_value
    base_ref[...] = grad_pref + logit_sum * query_key + total * back_value

    half = model // 2
    lefts[0] = second_low
    lefts[1] = mixed_low
    for j, right in enumerate((turned_low, grad_pref_low)):
        rows = slice(j * half, (j + 1) * half)
        other = lefts[j, :, pl.ds(pl.multiple_of((1 - ids[6]) * half, 128), half)]
        give[rows, :] = mm_tn(other, right).astype(bf16)
        mine = lefts[j, :, pl.ds(pl.multiple_of(ids[6] * half, 128), half)]
        keep[rows, :] = mm_tn(mine, right).astype(bf16)
    copy.wait()


def adapters(slots, ids, arrays):
    share, model = arrays[0].shape
    flat = ADAPTERS * BOTTLENECK
    wide, flat_wide = ((share, model), f32), ((share, flat), f32)
    return run(
        functools.partial(adapter_kernel, slots),
        (ids,),
        arrays,
        [
            ((share, model), f32, None),
            ((model, model), bf16),
            ((model + 16, model), bf16),
            ((8, model), f32),
            ((share, model), bf16),
            flat_wide,
            flat_wide,
            wide,
            wide,
            ((share, 128), f32),
        ],
        scratch=[
            pltpu.VMEM((share, model), f32),
            pltpu.VMEM((2, share, model), bf16),
            pltpu.SemaphoreType.DMA,
        ],
        vmem=20,
        micros=8.0,
    )


def adapter_rest_kernel(turn, reduced, mix, base, normed, factor, vecs, down, wq, wk, gpre2_ref, gpre2_low):
    grad_query_f = mm(turn[...], wk[...]).astype(bf16)
    grad_reduced = (gelu_both(reduced[...])[1] * mix[...]).astype(bf16)
    grad_second = base[...] + mm(grad_reduced, down[...]) + mm_nt(grad_query_f, wq[...])
    grad_pre2 = norm_back(grad_second, normed[...], factor[:, 0:1], vecs[4:5, :])
    gpre2_ref[...] = grad_pre2
    gpre2_low[...] = grad_pre2.astype(bf16)


def write_small(message, sums):
    high, low = halves_of(sums)
    rows = message.shape[0] - 16
    message[rows:, :] = jnp.concatenate([high, low], axis=0)


def read_small(message):
    rows = message.shape[0] - 16
    both = message[rows:, :].astype(f32)
    return both[:8] + both[8:]


def fold_kernel(base, start, split, last, ids, *refs):
    if start:
        keep, got, sums, *outs = refs
        rows = keep.shape[0] // 2
        pieces = [(keep, got, j * rows) for j in range(2)]
    else:
        *arrays, sums = refs[:5]
        outs = refs[5:]
        rows = arrays[0].shape[0]
        pieces = [(arrays[2 * j], arrays[2 * j + 1], 0) for j in range(2)]
        got = arrays[3]
    total = sums[...] + read_small(got)
    outs[-1][...] = total
    for j, (mine, other, at) in enumerate(pieces):
        def both(where):
            return (mine[where, :].astype(f32) + other[where, :].astype(f32)).astype(bf16)

        if split:
            half = rows // 2
            bit = ids[base + j]
            outs[2 * j][...] = both(pl.ds(pl.multiple_of(at + bit * half, 16), half))
            outs[2 * j + 1][:half, :] = both(pl.ds(pl.multiple_of(at + (1 - bit) * half, 16), half))
        elif last:
            outs[j][...] = both(pl.ds(at, rows))
        else:
            whole = both(pl.ds(at, rows))
            outs[2 * j][...] = whole
            outs[2 * j + 1][:rows, :] = whole
    if not last:
        write_small(outs[3], total)


def fold(ids, base, start, split, arrays, rows, sums, last=False):
    model = sums.shape[1]
    rows = rows // 2 if split else rows
    outputs = []
    for j in range(2):
        outputs += [((rows, model), bf16)] + ([] if last else [((rows + 16 * j, model), bf16)])
    outputs.append((sums.shape, f32))
    outs = run(functools.partial(fold_kernel, base, start, split, last), (ids,), [*arrays, sums], outputs)
    if last:
        return outs[:2], None, outs[2]
    return outs[0:4:2], outs[1:4:2], outs[4]


def join_kernel(base, last, ids, *refs):
    outs = refs[4:]
    for j in range(2):
        mine, got = refs[2 * j : 2 * j + 2]
        rows = mine.shape[0]
        bit = ids[base + j]
        out, at = (outs[0], 2 * rows * j) if last else (outs[j], 0)
        out[pl.ds(pl.multiple_of(at + bit * rows, 16), rows), :] = mine[...]
        out[pl.ds(pl.multiple_of(at + (1 - bit) * rows, 16), rows), :] = got[...]


def join(ids, base, last, mine, gots):
    rows, model = mine[0].shape
    outputs = [((4 * rows, model), bf16)] if last else [((2 * rows, model), bf16)] * 2
    arrays = [a for pair in zip(mine, gots) for a in pair]
    return run(functools.partial(join_kernel, base, last), (ids,), arrays, outputs)


def finish_kernel(first, ids, source, wq, wk, *refs):
    half = source.shape[0] // 2
    if first:
        part_own, part_got, out_q, out_v, key_part, out_x, stage, stage_x, sems = refs
    else:
        key_before, _, _, out_q, out_v, out_k, stage, stage_k, sems = refs
    core = ids[6] if first else 1 - ids[6]
    rows = pl.ds(pl.multiple_of(core * half, half), half)
    copies = []

    def send(j, source, target):
        copies.append(pltpu.make_async_copy(source, target, sems.at[j]))
        copies[-1].start()

    if first:
        stage_x[...] = part_own[...] + part_got[...].astype(f32)
        send(3, stage_x, out_x)
    mixed = source[:half, :]
    key = mm_tn(mixed, wq[rows, :])
    if first:
        key_part[...] = key
    else:
        stage_k[...] = key_before[...] + key
        send(2, stage_k, out_k)
    stage[1] = source[half:, :].astype(f32)
    send(1, stage.at[1], out_v.at[rows, :])
    stage[0] = mm(mixed, wk[...])
    send(0, stage.at[0], out_q.at[rows, :])
    for copy in copies:
        copy.wait()


def finish(ids, source, wq, wk, before, parts=()):
    model = source.shape[1]
    half = source.shape[0] // 2
    first = before is None
    vmem_spec = pl.BlockSpec(memory_space=pltpu.VMEM)
    any_spec = pl.BlockSpec(memory_space=pl.ANY)
    whole = jax.ShapeDtypeStruct((model, model), f32)
    inputs = [source, wq, wk, *(parts if first else [before[2]])]
    if first:
        out_specs = [any_spec, any_spec, vmem_spec, any_spec]
        shape = parts[0].shape
        out_shape = [whole, whole, pltpu.VMEM((model, model), f32), jax.ShapeDtypeStruct(shape, f32)]
    else:
        out_specs, shape, out_shape = [any_spec] * 3, (model, model), [whole] * 3
    return pl.pallas_call(
        functools.partial(finish_kernel, first),
        in_specs=[pl.BlockSpec(memory_space=pltpu.SMEM)]
        + [vmem_spec] * len(inputs)
        + ([] if first else [any_spec] * 2),
        out_specs=out_specs,
        out_shape=out_shape,
        input_output_aliases={} if first else {5: 0, 6: 1},
        scratch_shapes=[
            pltpu.VMEM((2, half, model), f32),
            pltpu.VMEM(shape, f32),
            pltpu.SemaphoreType.DMA((4,)),
        ],
        compiler_params=pltpu.CompilerParams(vmem_limit_bytes=16 * 1024 * 1024),
        cost_estimate=pl.CostEstimate(flops=int(2 * FLOPS), bytes_accessed=1, transcendentals=0),
    )(ids, *[pltpu.with_memory_space_constraint(a, pltpu.VMEM) for a in inputs], *([] if first else before[:2]))


def chip_kernel(near, got, gpre1, keep, give):
    share = keep.shape[0]
    give[...] = (near[share:, :] + got[share:, :].astype(f32)).astype(bf16)
    keep[...] = near[:share, :] + got[:share, :].astype(f32) + gpre1[...]


def body(
    layer_input,
    cotangent,
    seq_lens,
    seq_place,
    loss_mask,
    w_qkv,
    b_qv,
    w_out,
    b_out,
    ln1_gain,
    ln1_bias,
    w_in,
    b_in,
    w_back,
    b_back,
    ln2_gain,
    ln2_bias,
    ad_down,
    ad_down_bias,
    ad_up,
    ad_up_bias,
    join_query,
    join_key,
    join_value,
    join_gain,
    join_bias,
):
    group_rows, model = layer_input.shape
    share = cotangent.shape[0]
    rank = lax.axis_index("tp")
    dp_rank = lax.axis_index("dp")
    total_slots = group_rows * lax.axis_size("dp")

    core, near_x = ("tp", 1), ("tp", 2)
    others = []
    bit = 1
    while bit < lax.axis_size("dp"):
        others.append(("dp", bit))
        bit *= 2
    streams = [
        [others[0], *others[1:], near_x],
        [*others[1:2], others[0], near_x, *others[2:]],
    ]

    def bit_of(axis, which):
        return (lax.axis_index(axis) // which) % 2

    ids = [rank, dp_rank] + [rank ^ j for j in ORDER] + [bit_of(*core)]
    for at in range(len(others) + 1):
        ids += [bit_of(*stream[at]) for stream in streams]
    ids = jnp.stack(ids).astype(i32)
    ids = jnp.concatenate([ids, jnp.zeros(HEADER - ids.shape[0], i32), seq_lens, seq_place])
    vectors = [b_out, ln1_gain, ln1_bias, b_back, ln2_gain, ln2_bias, join_gain, join_bias, b_in]

    outs = [w_out, swap(w_out, "tp", 1), swap(w_out, "tp", 2)]
    outs.append(None)
    w_ins = [w_in, swap(w_in, "tp", 1)]
    w_backs = [w_back, swap(w_back, "tp", 1)]

    width = w_qkv.shape[2]
    w_t = jnp.transpose(w_qkv, (1, 2, 0)).reshape(3 * width, model)
    q, k, v, message = project(ids, layer_input, w_t, b_qv, loss_mask, b_in)
    message_got = swap(message, *core)
    far, e_far, rl_far = attend(2, 2, ids, q, k, v, share)
    far, message_got, outs[1], outs[2], w_ins[1], w_backs[1] = tie(
        far, message_got, *outs[1:3], w_ins[1], w_backs[1]
    )
    outs[3] = swap(outs[2], "tp", 1)
    c1, c3 = swap(far, "tp", 1), swap(far, "tp", 3)
    counted = message[1:2, :128] + message_got[1:2, :128]
    count_got = swap(counted, *others[0])
    q_near, _ = tie(q, far)
    near, e_near, rl_near = attend(0, 1, ids, q_near, k, v, share)
    c2_far = swap(near, *near_x)
    near, outs[3], c1 = tie(near, outs[3], c1)
    q_beside, _ = tie(q, near)
    beside, e_beside, rl_beside = attend(1, 1, ids, q_beside, k, v, share)
    c2_own = swap(beside, *near_x)
    early, vecs, weight_m = early_part(
        ids, [near, beside, c1, c3, outs[0], outs[1], outs[3]], loss_mask, vectors, share
    )

    give, inner = forward_rows(
        False, ids, early, c2_far, layer_input, outs[2], vecs, message_got, w_ins, w_backs, share
    )
    ffn_got = swap(give, *near_x)
    give, count_got = tie(give, count_got)
    counted = counted + count_got
    counted, _, _ = tie(counted, give, c2_own)
    pair = [bit for _, bit in others[1:3]]
    count_gots = [swap(counted, "dp", bit) for bit in [*pair, *([sum(pair)] if len(pair) == 2 else [])]]
    own, slope_one, slope_two, first, normed_one, factor_one, *constants = forward_rows(
        True, ids, early, c2_own, layer_input, outs[2], vecs, message_got, w_ins, w_backs, share, inner,
        ad_down_bias,
    )
    own, *count_gots = tie(own, *count_gots)
    counted = sum(count_gots, counted)
    for axis, which in [*others[3:], near_x]:
        counted = counted + swap(counted, axis, which)

    flat = ADAPTERS * BOTTLENECK
    down_t = jnp.transpose(ad_down, (1, 2, 0)).reshape(flat, model)
    up = ad_up.reshape(flat, model)
    layer_out, keep, give, sums, turn, reduced, mix, base, normed_two, factor_two = adapters(
        total_slots,
        ids,
        [
            own, ffn_got, first, cotangent, weight_m, counted, vecs, *constants, ad_up_bias, down_t, up,
            join_query, join_key, join_value,
        ],
    )
    got = swap(give, *core)
    gpre2, gpre2_low = run(
        adapter_rest_kernel,
        (),
        [turn, reduced, mix, base, normed_two, factor_two, vecs, down_t, join_query, join_key],
        [((share, model), f32), ((share, model), bf16)],
    )
    gpre2_got = swap(gpre2_low, "tp", 2)

    state = {"at": 0, "history": [], "rows": keep.shape[0] // 2}

    def sum_step(keeps, gots, sums):
        at = state["at"]
        start = at == 0
        split = state["rows"] // 2 >= LEAST_ROWS
        arrays = [keeps, gots] if start else [a for pair in zip(keeps, gots) for a in pair]
        keeps, gives, sums = fold(ids, 7 + 2 * at, start, split, arrays, state["rows"], sums)
        if split:
            state["rows"] //= 2
            state["history"].append(at)
        state["at"] = at + 1
        return keeps, [swap(g, *stream[at]) for g, stream in zip(gives, streams)], sums

    keeps, gots, sums = sum_step(keep, got, sums)
    own_low, _ = tie(gpre2_low, keeps[0])
    (back_own,) = backward_rows(own_low, slope_one, w_backs, w_ins, f32)
    keeps[0], gpre2_got, back_own = tie(keeps[0], gpre2_got, back_own)
    (back_give,) = backward_rows(gpre2_got, slope_two, w_backs, w_ins, bf16)
    back_give, *gots = tie(back_give, *gots)
    keeps, gots, sums = sum_step(keeps, gots, sums)
    keeps[0], back_give = tie(keeps[0], back_give)
    back_got = swap(back_give, "tp", 2)
    keeps, gots, sums = sum_step(keeps, gots, sums)
    keeps[0], back_got = tie(keeps[0], back_got)
    gpre1, c0, c1, c2, c3 = first_norm_back(back_own, back_got, gpre2, normed_one, factor_one, vecs, outs)
    c2, c3, c1 = swap(c2, "tp", 2), swap(c3, "tp", 3), swap(c1, "tp", 1)
    shared = ((near, beside, far), (e_near, e_beside, e_far), (rl_near, rl_beside, rl_far), (q, k, v))
    before = list(attend_back((0,), ids, (c0,), *shared, [], None, share))
    before[0], *gots = tie(before[0], *gots)
    keeps, gots, sums = sum_step(keeps, gots, sums)
    before[0], keeps[0] = tie(before[0], keeps[0])
    far_part, near_part = attend_back((2, 1, 3), ids, (c1, c2, c3), *shared, before, w_t, share)
    far_part, *gots = tie(far_part, *gots)
    far_got = swap(far_part, "tp", 1)
    while state["at"] < len(others) + 1:
        keeps, gots, sums = sum_step(keeps, gots, sums)
    arrays = [a for pair in zip(keeps, gots) for a in pair]
    keeps, _, sums = fold(ids, 0, False, False, arrays, state["rows"], sums, last=True)
    gain_grad, bias_grad = sums[0], sums[1]
    part_own, part_give = run(
        chip_kernel, (), [near_part, far_got, gpre1], [((share, model), f32), ((share, model), bf16)]
    )
    part_got = swap(part_give, "tp", 2)
    for at in reversed(state["history"]):
        gots = [swap(a, *stream[at]) for a, stream in zip(keeps, streams)]
        gots[0], part_own, gain_grad, bias_grad = tie(gots[0], part_own, gain_grad, bias_grad)
        keeps = join(ids, 7 + 2 * at, at == 0, keeps, gots)
    keeps[0], part_got = tie(keeps[0], part_got)
    got = swap(keeps[0], *core)
    *part, input_grad = finish(ids, keeps[0], join_query, join_key, None, (part_own, part_got))
    query_grad, value_grad, key_grad = finish(ids, got, join_query, join_key, part)
    return (layer_out, input_grad, query_grad, key_grad, value_grad, gain_grad, bias_grad)


def solution(mesh):
    placed = (
        P("dp", None),
        P(("dp", "tp"), None),
        P(),
        P(),
        P(("dp", "tp")),
        P(None, None, "tp"),
        P(None, "tp"),
        P("tp", None),
        P(),
        P(),
        P(),
        P(None, "tp"),
        P("tp"),
        P("tp", None),
        P(),
        P(),
        P(),
        P(),
        P(),
        P(),
        P(),
        P(),
        P(),
        P(),
        P(),
        P(),
    )
    return jax.shard_map(
        body,
        mesh=mesh,
        in_specs=placed,
        out_specs=(P(("dp", "tp"), None), P(("dp", "tp"), None), P(), P(), P(), P(), P()),
        check_vma=False,
    )
```

```python
import functools

import jax
import jax.numpy as jnp
from jax import lax
from jax.experimental import pallas as pl
from jax.experimental.pallas import tpu as pltpu
from jax.sharding import PartitionSpec as P

HEAD_DIM = 64
ADAPTERS = 16
BOTTLENECK = 48
SEQ_GRP = 4
LEAST_ROWS = 96
FLOPS = 1.15e9

EPS = 1e-06
NEG = -1e30
ROOT_HALF = 0.7071067811865476
INV_ROOT_TAU = 0.3989422804014327

f32 = jnp.float32
bf16 = jnp.bfloat16
i32 = jnp.int32

HEADER = 64

ORDER = (0, 2, 1, 3)


def gelu_both(values):
    phi = 0.5 * (1.0 + lax.erf(values * ROOT_HALF))
    return values * phi, phi + values * jnp.exp(-0.5 * values * values) * INV_ROOT_TAU


def row_mean(values):
    return jnp.sum(values, axis=-1, keepdims=True) * (1.0 / values.shape[-1])


def norm_parts(values):
    center = values - row_mean(values)
    factor = lax.rsqrt(row_mean(center * center) + EPS)
    return center * factor, factor


def norm_back(gradient, normed, factor, gain_vec):
    scaled = gradient * gain_vec
    return factor * (scaled - row_mean(scaled) - normed * row_mean(scaled * normed))


def mm(a, b):
    return lax.dot_general(a, b, (((1,), (0,)), ((), ())), preferred_element_type=f32)


def mm_nt(a, b):
    return lax.dot_general(a, b, (((1,), (1,)), ((), ())), preferred_element_type=f32)


def mm_tn(a, b):
    return lax.dot_general(a, b, (((0,), (0,)), ((), ())), preferred_element_type=f32)


def halves_of(a):
    high = a.astype(bf16)
    return high, (a - high.astype(f32)).astype(bf16)


def swap(value, axis, bit):
    size = lax.axis_size(axis)
    return lax.ppermute(value, axis, [(i, i ^ bit) for i in range(size)])


def tie(*values):
    return lax.optimization_barrier(values)


def run(kernel, scalars, inputs, outputs, streamed=(), scratch=(), vmem=12, micros=0.1):
    smem = pl.BlockSpec(memory_space=pltpu.SMEM)
    vmem_spec = pl.BlockSpec(memory_space=pltpu.VMEM)
    any_spec = pl.BlockSpec(memory_space=pl.ANY)
    outs = pl.pallas_call(
        kernel,
        in_specs=[smem] * len(scalars) + [vmem_spec] * len(inputs) + [any_spec] * len(streamed),
        out_specs=[vmem_spec if len(o) == 2 else any_spec for o in outputs],
        out_shape=[pltpu.VMEM(*o) if len(o) == 2 else jax.ShapeDtypeStruct(*o[:2]) for o in outputs],
        scratch_shapes=list(scratch),
        compiler_params=pltpu.CompilerParams(vmem_limit_bytes=vmem * 1024 * 1024),
        cost_estimate=pl.CostEstimate(flops=int(micros * FLOPS), bytes_accessed=1, transcendentals=0),
    )(
        *scalars,
        *[pltpu.with_memory_space_constraint(a, pltpu.VMEM) for a in inputs],
        *[pltpu.with_memory_space_constraint(a, pltpu.HBM) for a in streamed],
    )
    return list(outs)


def head_mask(width, head):
    lane = lax.broadcasted_iota(i32, (1, width), 1)
    return (lane >= head * HEAD_DIM) & (lane < (head + 1) * HEAD_DIM)


def group_ends(ints):
    count = (ints.shape[0] - HEADER) // 2

    def add(s, ends):
        spot = ints[HEADER + count + s] - ints[1] * SEQ_GRP
        length = jnp.where(spot >= 0, ints[HEADER + s], 0)
        return tuple(e + jnp.where(spot <= j, length, 0) for j, e in enumerate(ends))

    return lax.fori_loop(0, count, add, (jnp.int32(0),) * SEQ_GRP, unroll=8)


def segment_of(positions, ends):
    segment = jnp.zeros(positions.shape, i32)
    for e in ends:
        segment = segment + (positions >= e).astype(i32)
    return jnp.where(positions < ends[-1], segment, SEQ_GRP + positions)


def window(rows, start, ends, group_rows):
    low = jnp.int32(0)
    high = jnp.int32(0)
    last = start + rows - 1
    for e in ends:
        low = jnp.where(start >= e, jnp.maximum(low, e), low)
    for e in reversed(ends):
        high = jnp.where(last < e, e, high)
    padded = last >= ends[-1]
    low = jnp.where(start >= ends[-1], start, low)
    high = jnp.where(padded, start + rows, high)
    low = jnp.minimum(low // 128 * 128, group_rows - 128)
    return low, high - low


def by_window(rows, start, ends, group_rows, act):
    low, span = window(rows, start, ends, group_rows)
    widths = [w for w in (512,) if w < group_rows] + [group_rows]
    least = 0
    for w in widths:
        fits = (span > least) & (span <= w) if w < group_rows else span > least

        @pl.when(fits)
        def _(w=w):
            act(pl.multiple_of(jnp.minimum(low, group_rows - w), 128), w)

        least = w


def one_row(tile):
    return jnp.concatenate([tile[j : j + 1, :] for j in range(tile.shape[0])], axis=1)


def real_row(ids, mask):
    row = one_row(mask[...].astype(f32))
    lane = lax.broadcasted_iota(i32, row.shape, 1)
    return jnp.where(ids[0] * row.shape[1] + lane < group_ends(ids)[-1], row, 0.0)


def project_kernel(
    ids, x_hbm, w_hbm, bias_hbm, mask_hbm, b_in_hbm, q_ref, k_ref, v_ref, message, x_ref, w_ref, bias_ref, mask_ref,
    b_in_ref, sems,
):
    group_rows, width = q_ref.shape
    chunks = 4
    share = group_rows // chunks
    pairs = [(w_hbm, w_ref), (bias_hbm, bias_ref)]
    for c in range(chunks):
        rows = pl.ds(c * share, share)
        pairs.append((x_hbm.at[rows, :], x_ref.at[rows, :]))
    pairs += [(mask_hbm, mask_ref), (b_in_hbm, b_in_ref)]
    copies = [pltpu.make_async_copy(source, target, sems.at[j]) for j, (source, target) in enumerate(pairs)]
    for copy in copies:
        copy.start()
    copies[0].wait()
    copies[1].wait()
    bias = bias_ref[...].astype(f32)
    for c in range(chunks):
        rows = slice(c * share, (c + 1) * share)
        copies[2 + c].wait()
        x = x_ref[rows, :]
        k_ref[rows, :] = mm_nt(x, w_ref[width : 2 * width, :]).astype(bf16)
        v_ref[rows, :] = (mm_nt(x, w_ref[2 * width :, :]) + bias[1:2]).astype(bf16)
        q = (mm_nt(x, w_ref[:width, :]) + bias[0:1]).astype(bf16)
        q_ref[rows, :] = (q.astype(f32) * HEAD_DIM ** (-0.5)).astype(bf16)
    for copy in copies[2 + chunks :]:
        copy.wait()
    message[0:1, :] = one_row(b_in_ref[...].astype(f32))
    total = jnp.sum(real_row(ids, mask_ref), axis=-1, keepdims=True)
    message[1:, :] = jnp.broadcast_to(total, (message.shape[0] - 1, message.shape[1]))


def project(ids, x, w_t, b_qv, mask, b_in):
    group_rows, model = x.shape
    width = w_t.shape[0] // 3
    streamed = [x, w_t, b_qv, mask.reshape(-1, 128), b_in.reshape(-1, 128)]
    return run(
        project_kernel,
        (ids,),
        [],
        [((group_rows, width), bf16)] * 3 + [((8, model), f32)],
        streamed=streamed,
        scratch=[pltpu.VMEM(a.shape, a.dtype) for a in streamed] + [pltpu.SemaphoreType.DMA((8,))],
        micros=3.0,
    )


def attend_kernel(first, blocks, ids, q_ref, k_ref, v_ref, *refs):
    context_ref, e_ref, rl_ref = refs
    rows = rl_ref.shape[0] // blocks
    group_rows, width = k_ref.shape
    heads = width // HEAD_DIM
    ends = group_ends(ids)

    def one(t, carry):
        start = pl.multiple_of(ids[2 + first + t] * rows, rows)
        at = pl.multiple_of(t * rows, rows)

        def act(key0, w):
            q = q_ref[pl.ds(start, rows), :].astype(f32)
            seg_q = segment_of(start + lax.broadcasted_iota(i32, (rows, 1), 0), ends)
            seg_k = segment_of(key0 + lax.broadcasted_iota(i32, (1, w), 1), ends)
            k = k_ref[pl.ds(key0, w), :]
            v = v_ref[pl.ds(key0, w), :]
            context = jnp.zeros((rows, width), f32)
            wide = jnp.zeros((rows, width), f32)
            for h in range(heads):
                mask = head_mask(width, h)
                scores = mm_nt(jnp.where(mask, q, 0.0).astype(bf16), k)
                scores = jnp.where(seg_q == seg_k, scores, NEG)
                e = jnp.exp(scores - jnp.max(scores, axis=-1, keepdims=True))
                inverse = 1.0 / jnp.sum(e, axis=-1, keepdims=True)
                low = e.astype(bf16)
                e_ref[pl.ds(pl.multiple_of((t * heads + h) * rows, rows), rows), :w] = low
                context = jnp.where(mask, mm(low, v) * inverse, context)
                wide = jnp.where(mask, inverse, wide)
            rl_ref[pl.ds(at, rows), :] = wide
            context_ref[pl.ds(at, rows), :] = context.astype(bf16)

        by_window(rows, start, ends, group_rows, act)
        return carry

    lax.fori_loop(0, blocks, one, 0)


def attend(first, blocks, ids, q, k, v, share):
    group_rows, width = k.shape
    heads = width // HEAD_DIM
    return run(
        functools.partial(attend_kernel, first, blocks),
        (ids,),
        [q, k, v],
        [
            ((blocks * share, width), bf16),
            ((blocks * heads * share, group_rows), bf16),
            ((blocks * share, width), f32),
        ],
        vmem=20,
        micros=3.0 if first else 0.1,
    )


def attend_back_kernel(spots, first, last, ids, *refs):
    count = len(spots)
    grads, refs = refs[:count], refs[count:]
    contexts, es, rls, refs = refs[0:3], refs[3:6], refs[6:9], refs[9:]
    q_ref, k_ref, v_ref, refs = refs[0], refs[1], refs[2], refs[3:]
    if not first:
        before, refs = refs[:3], refs[3:]
    if last:
        w_ref, far_out, near_out, gq, gk, gv = refs
    else:
        gq, gk, gv = refs
    rows = grads[0].shape[0]
    group_rows, width = k_ref.shape
    heads = width // HEAD_DIM
    ends = group_ends(ids)
    if first:
        gk[...] = jnp.zeros_like(gk)
        gv[...] = jnp.zeros_like(gv)
    else:
        gq[...] = before[0][...]
        gk[...] = before[1][...]
        gv[...] = before[2][...]
    for g_ref, spot in zip(grads, spots):
        start = pl.multiple_of(ids[2 + spot] * rows, rows)
        part, t = (spot, 0) if spot < 2 else (2, spot - 2)
        g = g_ref[...].astype(f32) * rls[part][t * rows : (t + 1) * rows, :]
        dots = g * contexts[part][t * rows : (t + 1) * rows, :].astype(f32)
        q = q_ref[pl.ds(start, rows), :].astype(f32)

        def act(key0, w, g=g, dots=dots, q=q, part=part, t=t, start=start):
            keys = pl.ds(key0, w)
            k = k_ref[keys, :]
            v = v_ref[keys, :]
            out = jnp.zeros((rows, width), f32)
            add_k = jnp.zeros((w, width), f32)
            add_v = jnp.zeros((w, width), f32)
            for h in range(heads):
                mask = head_mask(width, h)
                g_head = jnp.where(mask, g, 0.0).astype(bf16)
                e = es[part][(t * heads + h) * rows : (t * heads + h + 1) * rows, :w]
                delta = jnp.sum(jnp.where(mask, dots, 0.0), axis=-1, keepdims=True)
                ds = (e.astype(f32) * (mm_nt(g_head, v) - delta)).astype(bf16)
                out = jnp.where(mask, mm(ds, k), out)
                add_k = add_k + mm_tn(ds, jnp.where(mask, q, 0.0).astype(bf16))
                add_v = add_v + mm_tn(e, g_head)
            gk[keys, :] += add_k
            gv[keys, :] += add_v
            gq[pl.ds(start, rows), :] = (out * HEAD_DIM ** (-0.5)).astype(bf16)

        by_window(rows, start, ends, group_rows, act)
    if last:
        for out, pair in ((far_out, (2, 3)), (near_out, (0, 1))):
            for t, spot in enumerate(pair):
                own = pl.ds(pl.multiple_of(ids[2 + spot] * rows, rows), rows)
                part = (
                    mm(gq[own, :], w_ref[:width, :])
                    + mm(gk[own, :].astype(bf16), w_ref[width : 2 * width, :])
                    + mm(gv[own, :].astype(bf16), w_ref[2 * width :, :])
                )
                out[t * rows : (t + 1) * rows, :] = part.astype(out.dtype)


def attend_back(spots, ids, grads, contexts, es, rls, qkv, before, w_t, share):
    group_rows, width = qkv[0].shape
    last = w_t is not None
    sums = [((group_rows, width), bf16), ((group_rows, width), f32), ((group_rows, width), f32)]
    inputs = [*grads, *contexts, *es, *rls, *qkv, *before]
    if last:
        model = w_t.shape[1]
        outputs = [((2 * share, model), bf16), ((2 * share, model), f32)]
        scratch = [pltpu.VMEM(*o) for o in sums]
        inputs.append(w_t)
    else:
        outputs, scratch = sums, []
    return run(
        functools.partial(attend_back_kernel, spots, not before, last),
        (ids,),
        inputs,
        outputs,
        scratch=scratch,
        vmem=20,
        micros=5.0 if last else 0.1,
    )


def early_kernel(ids, c0, x0, c1, c3, o0, o1, o3, *refs):
    mask_hbm, *vectors = refs[:10]
    out, vecs, weight, mask_ref, *tiles, sems = refs[10:]
    pairs = [(mask_hbm, mask_ref), *zip(vectors, tiles)]
    copies = [pltpu.make_async_copy(source, target, sems.at[j]) for j, (source, target) in enumerate(pairs)]
    for copy in copies:
        copy.start()
    share = out.shape[0] // 2
    attn = mm(c1[...], o1[...])
    for t, mine in enumerate((c0, x0)):
        rows = slice(t * share, (t + 1) * share)
        out[rows, :] = attn[rows] + mm(mine[...], o0[...]) + mm(c3[(1 - t) * share : (2 - t) * share, :], o3[...])
    for copy in copies:
        copy.wait()
    for j, tile in enumerate(tiles):
        vecs[j : j + 1, :] = one_row(tile[...].astype(f32))
    vecs[9:, :] = jnp.zeros((vecs.shape[0] - 9, vecs.shape[1]), f32)
    row = real_row(ids, mask_ref)
    here = lax.broadcasted_iota(i32, (share, share), 0) == lax.broadcasted_iota(i32, (share, share), 1)
    weight[...] = jnp.sum(jnp.where(here, jnp.broadcast_to(row, (share, share)), 0.0), axis=-1, keepdims=True)


def early_part(ids, arrays, mask, vectors, share):
    model = arrays[4].shape[1]
    streamed = [mask.reshape(-1, 128), *[v.reshape(-1, 128) for v in vectors]]
    return run(
        early_kernel,
        (ids,),
        arrays,
        [((2 * share, model), f32), ((16, model), f32), ((share, 1), f32)],
        streamed=streamed,
        scratch=[pltpu.VMEM(a.shape, a.dtype) for a in streamed] + [pltpu.SemaphoreType.DMA((len(streamed),))],
    )


def adapter_constants(down_bias, member_ref, spread_ref, bias_ref):
    flat = member_ref.shape[0]
    lane = lax.broadcasted_iota(i32, (flat, ADAPTERS), 0) - BOTTLENECK * lax.broadcasted_iota(
        i32, (flat, ADAPTERS), 1
    )
    member_ref[...] = ((lane >= 0) & (lane < BOTTLENECK)).astype(f32).astype(bf16)
    lane = lax.broadcasted_iota(i32, (ADAPTERS, flat), 1) - BOTTLENECK * lax.broadcasted_iota(
        i32, (ADAPTERS, flat), 0
    )
    spread = ((lane >= 0) & (lane < BOTTLENECK)).astype(f32)
    spread_ref[...] = spread.astype(bf16)
    cycle = lax.broadcasted_iota(i32, (BOTTLENECK, flat), 1) - lax.broadcasted_iota(i32, (BOTTLENECK, flat), 0)
    repeat = jnp.zeros(cycle.shape, f32)
    for a in range(ADAPTERS):
        repeat = repeat + (cycle == a * BOTTLENECK).astype(f32)
    bias_row = jnp.sum(mm(down_bias[...], repeat.astype(bf16)) * spread, axis=0, keepdims=True)
    bias_ref[...] = jnp.broadcast_to(bias_row, bias_ref.shape)


def forward_kernel(own, ids, early, c2, x_ref, o2, vecs, message, in0, in1, back0, back1, *rest):
    if own:
        inner_ref, down_bias, part_ref, slope, slope_two, first_ref, normed_ref, factor_ref, *constants = rest
    else:
        part_ref, inner_ref = rest
    share = early.shape[0] // 2
    t = 0 if own else 1
    attn = early[t * share : (t + 1) * share, :] + mm(c2[...], o2[...])
    vec = vecs[...].astype(f32)
    start = pl.multiple_of(ids[2 if own else 3] * share, share)
    normed, factor = norm_parts(attn + vec[0:1] + x_ref[pl.ds(start, share), :].astype(f32))
    first = normed * vec[1:2] + vec[2:3]
    low = first.astype(bf16)
    part = jnp.zeros(first.shape, f32)
    units = in0.shape[1]
    chunk = units
    for j, (w_in, bias, w_back) in enumerate(((in0, vec[8:9], back0), (in1, message[0:1, :], back1))):
        for at in range(0, units, chunk):
            here = slice(at, at + chunk)
            columns = slice(j * units + at, j * units + at + chunk)
            inner = mm(low, w_in[:, here]) + bias[:, here]
            if own:
                act, bend = gelu_both(inner)
                slope[:, columns] = bend.astype(bf16)
                slope_two[:, columns] = gelu_both(inner_ref[:, columns])[1].astype(bf16)
            else:
                act = 0.5 * inner * (1.0 + lax.erf(inner * ROOT_HALF))
                inner_ref[:, columns] = inner
            part = part + mm(act.astype(bf16), w_back[here, :])
    part_ref[...] = part.astype(part_ref.dtype)
    if own:
        first_ref[...] = first
        normed_ref[...] = normed
        factor_ref[...] = jnp.broadcast_to(factor, factor_ref.shape)
        adapter_constants(down_bias, *constants)


def forward_rows(own, ids, early, c2, x, o2, vecs, message, w_ins, w_backs, share, *more):
    model = x.shape[1]
    units = w_ins[0].shape[1]
    slope = ((share, 2 * units), bf16)
    flat = ADAPTERS * BOTTLENECK
    if own:
        outputs = [((share, model), f32), slope, slope] + [((share, model), f32)] * 2 + [((share, 128), f32)]
        outputs += [((flat, ADAPTERS), bf16), ((ADAPTERS, flat), bf16), ((8, flat), f32)]
    else:
        outputs = [((share, model), bf16), ((share, 2 * units), f32)]
    return run(
        functools.partial(forward_kernel, own),
        (ids,),
        [early, c2, x, o2, vecs, message, *w_ins, *w_backs, *more],
        outputs,
        vmem=16,
        micros=3.0,
    )


def backward_kernel(gp, slope, back0, back1, in0, in1, part_ref):
    grad = gp[...]
    units = in0.shape[1]
    part = jnp.zeros(grad.shape, f32)
    for j, (w_back, w_in) in enumerate(((back0, in0), (back1, in1))):
        bend = slope[:, j * units : (j + 1) * units].astype(f32)
        inner = (bend * mm_nt(grad, w_back[...])).astype(bf16)
        part = part + mm_nt(inner, w_in[...])
    part_ref[...] = part.astype(part_ref.dtype)


def backward_rows(grad, slope, w_backs, w_ins, dtype):
    share, model = grad.shape
    units = w_ins[0].shape[1]
    return run(
        backward_kernel,
        (),
        [grad, slope, *w_backs, *w_ins],
        [((share, model), dtype)],
    )


def first_norm_kernel(own, got, gpre2, normed, factor, vecs, o0, o1, o2, o3, gpre1, c0, c1, c2, c3):
    grad = own[...] + got[...].astype(f32) + gpre2[...]
    grad = norm_back(grad, normed[...], factor[:, 0:1], vecs[...].astype(f32)[1:2])
    gpre1[...] = grad
    low = grad.astype(bf16)
    for c, o in ((c2, o2), (c3, o3), (c1, o1), (c0, o0)):
        c[...] = mm_nt(low, o[...]).astype(bf16)


def first_norm_back(own, got, gpre2, normed, factor, vecs, outs):
    share, model = own.shape
    width = outs[0].shape[0]
    return run(
        first_norm_kernel,
        (),
        [own, got, gpre2, normed, factor, vecs, *outs],
        [((share, model), f32)] + [((share, width), bf16)] * 4,
    )


def adapter_kernel(
    slots, ids, own, got, first_ref, cot, weight, count, vecs, member_ref, spread_ref, bias_ref, up_bias, down, up,
    wq, wk, wv,
    out_hbm, keep, give, sums, turn_ref, reduced_ref, mix_ref, base_ref, normed_ref, factor_ref, layer_out, lefts, sem,
):
    flat, model = up.shape
    vec = vecs[...].astype(f32)
    member = member_ref[...]
    spread = spread_ref[...]
    inv_root = model ** (-0.5)
    scale = 0.5 * slots / jnp.maximum(count[0:1, 0:1], 1.0)

    normed_two, factor_two = norm_parts(own[...] + got[...].astype(f32) + vec[3:4] + first_ref[...])
    normed_ref[...] = normed_two
    factor_ref[...] = jnp.broadcast_to(factor_two, factor_ref.shape)
    second = normed_two * vec[4:5] + vec[5:6]
    second_low = second.astype(bf16)
    query_key = mm_nt(mm(second_low, wq[...]).astype(bf16), wk[...]) * inv_root
    query_key_low = query_key.astype(bf16)
    lift_key = mm_nt(query_key_low, up[...])
    reduced = mm_nt(second_low, down[...]) + bias_ref[0:1, :]
    reduced_ref[...] = reduced
    squeezed = 0.5 * reduced * (1.0 + lax.erf(reduced * ROOT_HALF))
    squeezed = squeezed.astype(bf16).astype(f32)
    logits = (
        mm((squeezed * lift_key).astype(bf16), member)
        + mm_nt(query_key_low, up_bias[...])
        + jnp.sum(query_key * second, axis=-1, keepdims=True)
    )
    shifted = logits - jnp.max(logits, axis=-1, keepdims=True)
    log_probs = shifted - jnp.log(jnp.sum(jnp.exp(shifted), axis=-1, keepdims=True))
    joining = jnp.exp(log_probs)
    entropy = -jnp.sum(joining * log_probs, axis=-1, keepdims=True)
    total = jnp.sum(joining, axis=-1, keepdims=True)
    joining_low = joining.astype(bf16)
    joining_wide = mm(joining_low, spread)
    joined_low = (joining_wide * squeezed).astype(bf16)
    mixed = total * second + mm(joined_low, up[...]) + mm(joining_low, up_bias[...])
    mixed_low = mixed.astype(bf16)
    normed_join, factor_join = norm_parts(second + mm(mixed_low, wv[...]))
    grad_out = cot[...].astype(f32)
    grad_pref = norm_back(grad_out, normed_join, factor_join, vec[6:7])
    grad_pref_low = grad_pref.astype(bf16)
    back_value = mm_nt(grad_pref_low, wv[...])
    back_value_low = back_value.astype(bf16)
    lift_value = mm_nt(back_value_low, up[...])
    grad_probs = (
        mm((squeezed * lift_value).astype(bf16), member)
        + mm_nt(back_value_low, up_bias[...])
        + jnp.sum(back_value * second, axis=-1, keepdims=True)
    )
    mean_grad = jnp.sum(joining * grad_probs, axis=-1, keepdims=True)
    grad_logits = joining * (grad_probs - mean_grad) - scale * weight[...] * joining * (log_probs + entropy)
    logits_low = grad_logits.astype(bf16)
    grad_wide = mm(logits_low, spread)
    logit_sum = jnp.sum(grad_logits, axis=-1, keepdims=True)
    turned = (
        logit_sum * second + mm((grad_wide * squeezed).astype(bf16), up[...]) + mm(logits_low, up_bias[...])
    ) * inv_root
    turned_low = turned.astype(bf16)
    turn_ref[...] = turned_low

    layer_out[...] = normed_join * vec[6:7] + vec[7:8]
    copy = pltpu.make_async_copy(layer_out, out_hbm, sem)
    copy.start()
    small = jnp.concatenate(
        [
            jnp.sum(grad_out * normed_join, axis=0, keepdims=True),
            jnp.sum(grad_out, axis=0, keepdims=True),
            jnp.zeros((sums.shape[0] - 2, model), f32),
        ],
        axis=0,
    )
    sums[...] = small
    write_small(give, small)
    mix_ref[...] = grad_wide * lift_key + joining_wide * lift_value
    base_ref[...] = grad_pref + logit_sum * query_key + total * back_value

    half = model // 2
    lefts[0] = second_low
    lefts[1] = mixed_low
    for j, right in enumerate((turned_low, grad_pref_low)):
        rows = slice(j * half, (j + 1) * half)
        other = lefts[j, :, pl.ds(pl.multiple_of((1 - ids[6]) * half, 128), half)]
        give[rows, :] = mm_tn(other, right).astype(bf16)
        mine = lefts[j, :, pl.ds(pl.multiple_of(ids[6] * half, 128), half)]
        keep[rows, :] = mm_tn(mine, right).astype(bf16)
    copy.wait()


def adapters(slots, ids, arrays):
    share, model = arrays[0].shape
    flat = ADAPTERS * BOTTLENECK
    wide, flat_wide = ((share, model), f32), ((share, flat), f32)
    return run(
        functools.partial(adapter_kernel, slots),
        (ids,),
        arrays,
        [
            ((share, model), f32, None),
            ((model, model), bf16),
            ((model + 16, model), bf16),
            ((8, model), f32),
            ((share, model), bf16),
            flat_wide,
            flat_wide,
            wide,
            wide,
            ((share, 128), f32),
        ],
        scratch=[
            pltpu.VMEM((share, model), f32),
            pltpu.VMEM((2, share, model), bf16),
            pltpu.SemaphoreType.DMA,
        ],
        vmem=20,
        micros=8.0,
    )


def adapter_rest_kernel(turn, reduced, mix, base, normed, factor, vecs, down, wq, wk, gpre2_ref, gpre2_low):
    grad_query_f = mm(turn[...], wk[...]).astype(bf16)
    grad_reduced = (gelu_both(reduced[...])[1] * mix[...]).astype(bf16)
    grad_second = base[...] + mm(grad_reduced, down[...]) + mm_nt(grad_query_f, wq[...])
    grad_pre2 = norm_back(grad_second, normed[...], factor[:, 0:1], vecs[4:5, :])
    gpre2_ref[...] = grad_pre2
    gpre2_low[...] = grad_pre2.astype(bf16)


def write_small(message, sums):
    high, low = halves_of(sums)
    rows = message.shape[0] - 16
    message[rows:, :] = jnp.concatenate([high, low], axis=0)


def read_small(message):
    rows = message.shape[0] - 16
    both = message[rows:, :].astype(f32)
    return both[:8] + both[8:]


def fold_kernel(base, start, split, last, ids, *refs):
    if start:
        keep, got, sums, *outs = refs
        rows = keep.shape[0] // 2
        pieces = [(keep, got, j * rows) for j in range(2)]
    else:
        *arrays, sums = refs[:5]
        outs = refs[5:]
        rows = arrays[0].shape[0]
        pieces = [(arrays[2 * j], arrays[2 * j + 1], 0) for j in range(2)]
        got = arrays[3]
    total = sums[...] + read_small(got)
    outs[-1][...] = total
    for j, (mine, other, at) in enumerate(pieces):
        def both(where):
            return (mine[where, :].astype(f32) + other[where, :].astype(f32)).astype(bf16)

        if split:
            half = rows // 2
            bit = ids[base + j]
            outs[2 * j][...] = both(pl.ds(pl.multiple_of(at + bit * half, 16), half))
            outs[2 * j + 1][:half, :] = both(pl.ds(pl.multiple_of(at + (1 - bit) * half, 16), half))
        elif last:
            outs[j][...] = both(pl.ds(at, rows))
        else:
            whole = both(pl.ds(at, rows))
            outs[2 * j][...] = whole
            outs[2 * j + 1][:rows, :] = whole
    if not last:
        write_small(outs[3], total)


def fold(ids, base, start, split, arrays, rows, sums, last=False):
    model = sums.shape[1]
    rows = rows // 2 if split else rows
    outputs = []
    for j in range(2):
        outputs += [((rows, model), bf16)] + ([] if last else [((rows + 16 * j, model), bf16)])
    outputs.append((sums.shape, f32))
    outs = run(functools.partial(fold_kernel, base, start, split, last), (ids,), [*arrays, sums], outputs)
    if last:
        return outs[:2], None, outs[2]
    return outs[0:4:2], outs[1:4:2], outs[4]


def join_kernel(base, last, ids, *refs):
    outs = refs[4:]
    for j in range(2):
        mine, got = refs[2 * j : 2 * j + 2]
        rows = mine.shape[0]
        bit = ids[base + j]
        out, at = (outs[0], 2 * rows * j) if last else (outs[j], 0)
        out[pl.ds(pl.multiple_of(at + bit * rows, 16), rows), :] = mine[...]
        out[pl.ds(pl.multiple_of(at + (1 - bit) * rows, 16), rows), :] = got[...]


def join(ids, base, last, mine, gots):
    rows, model = mine[0].shape
    outputs = [((4 * rows, model), bf16)] if last else [((2 * rows, model), bf16)] * 2
    arrays = [a for pair in zip(mine, gots) for a in pair]
    return run(functools.partial(join_kernel, base, last), (ids,), arrays, outputs)


def finish_kernel(first, ids, source, wq, wk, *refs):
    half = source.shape[0] // 2
    if first:
        part_own, part_got, out_q, out_v, key_part, out_x, stage, stage_x, sems = refs
    else:
        key_before, _, _, out_q, out_v, out_k, stage, stage_k, sems = refs
    core = ids[6] if first else 1 - ids[6]
    rows = pl.ds(pl.multiple_of(core * half, half), half)
    copies = []

    def send(j, source, target):
        copies.append(pltpu.make_async_copy(source, target, sems.at[j]))
        copies[-1].start()

    if first:
        stage_x[...] = part_own[...] + part_got[...].astype(f32)
        send(3, stage_x, out_x)
    mixed = source[:half, :]
    key = mm_tn(mixed, wq[rows, :])
    if first:
        key_part[...] = key
    else:
        stage_k[...] = key_before[...] + key
        send(2, stage_k, out_k)
    stage[1] = source[half:, :].astype(f32)
    send(1, stage.at[1], out_v.at[rows, :])
    stage[0] = mm(mixed, wk[...])
    send(0, stage.at[0], out_q.at[rows, :])
    for copy in copies:
        copy.wait()


def finish(ids, source, wq, wk, before, parts=()):
    model = source.shape[1]
    half = source.shape[0] // 2
    first = before is None
    vmem_spec = pl.BlockSpec(memory_space=pltpu.VMEM)
    any_spec = pl.BlockSpec(memory_space=pl.ANY)
    whole = jax.ShapeDtypeStruct((model, model), f32)
    inputs = [source, wq, wk, *(parts if first else [before[2]])]
    if first:
        out_specs = [any_spec, any_spec, vmem_spec, any_spec]
        shape = parts[0].shape
        out_shape = [whole, whole, pltpu.VMEM((model, model), f32), jax.ShapeDtypeStruct(shape, f32)]
    else:
        out_specs, shape, out_shape = [any_spec] * 3, (model, model), [whole] * 3
    return pl.pallas_call(
        functools.partial(finish_kernel, first),
        in_specs=[pl.BlockSpec(memory_space=pltpu.SMEM)]
        + [vmem_spec] * len(inputs)
        + ([] if first else [any_spec] * 2),
        out_specs=out_specs,
        out_shape=out_shape,
        input_output_aliases={} if first else {5: 0, 6: 1},
        scratch_shapes=[
            pltpu.VMEM((2, half, model), f32),
            pltpu.VMEM(shape, f32),
            pltpu.SemaphoreType.DMA((4,)),
        ],
        compiler_params=pltpu.CompilerParams(vmem_limit_bytes=16 * 1024 * 1024),
        cost_estimate=pl.CostEstimate(flops=int(2 * FLOPS), bytes_accessed=1, transcendentals=0),
    )(ids, *[pltpu.with_memory_space_constraint(a, pltpu.VMEM) for a in inputs], *([] if first else before[:2]))


def chip_kernel(near, got, gpre1, keep, give):
    share = keep.shape[0]
    give[...] = (near[share:, :] + got[share:, :].astype(f32)).astype(bf16)
    keep[...] = near[:share, :] + got[:share, :].astype(f32) + gpre1[...]


def body(
    layer_input,
    cotangent,
    seq_lens,
    seq_place,
    loss_mask,
    w_qkv,
    b_qv,
    w_out,
    b_out,
    ln1_gain,
    ln1_bias,
    w_in,
    b_in,
    w_back,
    b_back,
    ln2_gain,
    ln2_bias,
    ad_down,
    ad_down_bias,
    ad_up,
    ad_up_bias,
    join_query,
    join_key,
    join_value,
    join_gain,
    join_bias,
):
    group_rows, model = layer_input.shape
    share = cotangent.shape[0]
    rank = lax.axis_index("tp")
    dp_rank = lax.axis_index("dp")
    total_slots = group_rows * lax.axis_size("dp")

    core, near_x = ("tp", 1), ("tp", 2)
    others = []
    bit = 1
    while bit < lax.axis_size("dp"):
        others.append(("dp", bit))
        bit *= 2
    streams = [
        [others[0], *others[1:], near_x],
        [*others[1:2], others[0], near_x, *others[2:]],
    ]

    def bit_of(axis, which):
        return (lax.axis_index(axis) // which) % 2

    ids = [rank, dp_rank] + [rank ^ j for j in ORDER] + [bit_of(*core)]
    for at in range(len(others) + 1):
        ids += [bit_of(*stream[at]) for stream in streams]
    ids = jnp.stack(ids).astype(i32)
    ids = jnp.concatenate([ids, jnp.zeros(HEADER - ids.shape[0], i32), seq_lens, seq_place])
    vectors = [b_out, ln1_gain, ln1_bias, b_back, ln2_gain, ln2_bias, join_gain, join_bias, b_in]

    outs = [w_out, swap(w_out, "tp", 1), swap(w_out, "tp", 2)]
    outs.append(None)
    w_ins = [w_in, swap(w_in, "tp", 1)]
    w_backs = [w_back, swap(w_back, "tp", 1)]

    width = w_qkv.shape[2]
    w_t = jnp.transpose(w_qkv, (1, 2, 0)).reshape(3 * width, model)
    q, k, v, message = project(ids, layer_input, w_t, b_qv, loss_mask, b_in)
    message_got = swap(message, *core)
    far, e_far, rl_far = attend(2, 2, ids, q, k, v, share)
    far, message_got, outs[1], outs[2], w_ins[1], w_backs[1] = tie(
        far, message_got, *outs[1:3], w_ins[1], w_backs[1]
    )
    outs[3] = swap(outs[2], "tp", 1)
    c1, c3 = swap(far, "tp", 1), swap(far, "tp", 3)
    counted = message[1:2, :128] + message_got[1:2, :128]
    count_got = swap(counted, *others[0])
    q_near, _ = tie(q, far)
    near, e_near, rl_near = attend(0, 1, ids, q_near, k, v, share)
    c2_far = swap(near, *near_x)
    near, outs[3], c1 = tie(near, outs[3], c1)
    q_beside, _ = tie(q, near)
    beside, e_beside, rl_beside = attend(1, 1, ids, q_beside, k, v, share)
    c2_own = swap(beside, *near_x)
    early, vecs, weight_m = early_part(
        ids, [near, beside, c1, c3, outs[0], outs[1], outs[3]], loss_mask, vectors, share
    )

    give, inner = forward_rows(
        False, ids, early, c2_far, layer_input, outs[2], vecs, message_got, w_ins, w_backs, share
    )
    ffn_got = swap(give, *near_x)
    give, count_got = tie(give, count_got)
    counted = counted + count_got
    counted, _, _ = tie(counted, give, c2_own)
    pair = [bit for _, bit in others[1:3]]
    count_gots = [swap(counted, "dp", bit) for bit in [*pair, *([sum(pair)] if len(pair) == 2 else [])]]
    own, slope_one, slope_two, first, normed_one, factor_one, *constants = forward_rows(
        True, ids, early, c2_own, layer_input, outs[2], vecs, message_got, w_ins, w_backs, share, inner,
        ad_down_bias,
    )
    own, *count_gots = tie(own, *count_gots)
    counted = sum(count_gots, counted)
    for axis, which in [*others[3:], near_x]:
        counted = counted + swap(counted, axis, which)

    flat = ADAPTERS * BOTTLENECK
    down_t = jnp.transpose(ad_down, (1, 2, 0)).reshape(flat, model)
    up = ad_up.reshape(flat, model)
    layer_out, keep, give, sums, turn, reduced, mix, base, normed_two, factor_two = adapters(
        total_slots,
        ids,
        [
            own, ffn_got, first, cotangent, weight_m, counted, vecs, *constants, ad_up_bias, down_t, up,
            join_query, join_key, join_value,
        ],
    )
    got = swap(give, *core)
    gpre2, gpre2_low = run(
        adapter_rest_kernel,
        (),
        [turn, reduced, mix, base, normed_two, factor_two, vecs, down_t, join_query, join_key],
        [((share, model), f32), ((share, model), bf16)],
    )
    gpre2_got = swap(gpre2_low, "tp", 2)

    state = {"at": 0, "history": [], "rows": keep.shape[0] // 2}

    def sum_step(keeps, gots, sums):
        at = state["at"]
        start = at == 0
        split = state["rows"] // 2 >= LEAST_ROWS
        arrays = [keeps, gots] if start else [a for pair in zip(keeps, gots) for a in pair]
        keeps, gives, sums = fold(ids, 7 + 2 * at, start, split, arrays, state["rows"], sums)
        if split:
            state["rows"] //= 2
            state["history"].append(at)
        state["at"] = at + 1
        return keeps, [swap(g, *stream[at]) for g, stream in zip(gives, streams)], sums

    keeps, gots, sums = sum_step(keep, got, sums)
    own_low, _ = tie(gpre2_low, keeps[0])
    (back_own,) = backward_rows(own_low, slope_one, w_backs, w_ins, f32)
    keeps[0], gpre2_got, back_own = tie(keeps[0], gpre2_got, back_own)
    (back_give,) = backward_rows(gpre2_got, slope_two, w_backs, w_ins, bf16)
    back_give, *gots = tie(back_give, *gots)
    keeps, gots, sums = sum_step(keeps, gots, sums)
    keeps[0], back_give = tie(keeps[0], back_give)
    back_got = swap(back_give, "tp", 2)
    keeps, gots, sums = sum_step(keeps, gots, sums)
    keeps[0], back_got = tie(keeps[0], back_got)
    gpre1, c0, c1, c2, c3 = first_norm_back(back_own, back_got, gpre2, normed_one, factor_one, vecs, outs)
    c2, c3, c1 = swap(c2, "tp", 2), swap(c3, "tp", 3), swap(c1, "tp", 1)
    shared = ((near, beside, far), (e_near, e_beside, e_far), (rl_near, rl_beside, rl_far), (q, k, v))
    keeps, gots, sums = sum_step(keeps, gots, sums)
    c0, _ = tie(c0, keeps[0])
    before = list(attend_back((0,), ids, (c0,), *shared, [], None, share))
    far_part, near_part = attend_back((2, 1, 3), ids, (c1, c2, c3), *shared, before, w_t, share)
    far_part, *gots = tie(far_part, *gots)
    far_got = swap(far_part, "tp", 1)
    while state["at"] < len(others) + 1:
        keeps, gots, sums = sum_step(keeps, gots, sums)
    arrays = [a for pair in zip(keeps, gots) for a in pair]
    keeps, _, sums = fold(ids, 0, False, False, arrays, state["rows"], sums, last=True)
    gain_grad, bias_grad = sums[0], sums[1]
    part_own, part_give = run(
        chip_kernel, (), [near_part, far_got, gpre1], [((share, model), f32), ((share, model), bf16)]
    )
    part_got = swap(part_give, "tp", 2)
    for at in reversed(state["history"]):
        gots = [swap(a, *stream[at]) for a, stream in zip(keeps, streams)]
        gots[0], part_own, gain_grad, bias_grad = tie(gots[0], part_own, gain_grad, bias_grad)
        keeps = join(ids, 7 + 2 * at, at == 0, keeps, gots)
    keeps[0], part_got = tie(keeps[0], part_got)
    got = swap(keeps[0], *core)
    *part, input_grad = finish(ids, keeps[0], join_query, join_key, None, (part_own, part_got))
    query_grad, value_grad, key_grad = finish(ids, got, join_query, join_key, part)
    return (layer_out, input_grad, query_grad, key_grad, value_grad, gain_grad, bias_grad)


def solution(mesh):
    placed = (
        P("dp", None),
        P(("dp", "tp"), None),
        P(),
        P(),
        P(("dp", "tp")),
        P(None, None, "tp"),
        P(None, "tp"),
        P("tp", None),
        P(),
        P(),
        P(),
        P(None, "tp"),
        P("tp"),
        P("tp", None),
        P(),
        P(),
        P(),
        P(),
        P(),
        P(),
        P(),
        P(),
        P(),
        P(),
        P(),
        P(),
    )
    return jax.shard_map(
        body,
        mesh=mesh,
        in_specs=placed,
        out_specs=(P(("dp", "tp"), None), P(("dp", "tp"), None), P(), P(), P(), P(), P()),
        check_vma=False,
    )
```
